32 devices in a mesh: batch: 8 (over y, x, core), head: 4 (over z).
Axes of the slice: x: 2, y: 2, z: 4, core: 2. Of those that a mesh axis runs over, the one named last changes fastest.
Arguments:
- tokens: bfloat16 [4608, 1024], P('batch'), may hold values from -6 to 6
- page_lengths: int32 [8], P('batch'), may hold values from 144 to 576
- corners: int32 [2, 4608], P(None, 'batch'), may hold values from 0 to 1023
- w_query: bfloat16 [1024, 1024], P(None, 'head'), may hold values from -0.1875 to 0.1875
- w_key: bfloat16 [1024, 1024], P(None, 'head'), may hold values from -0.1875 to 0.1875
- w_value: bfloat16 [1024, 1024], P(None, 'head'), may hold values from -0.1875 to 0.1875
- w_output: bfloat16 [1024, 1024], P('head'), may hold values from -0.75 to 0.75
- b_output: float32 [1024], replicated, may hold values from -1.5 to 1.5
- gain_attn: float32 [1024], replicated, may hold values from 0.1 to 1.9
- shift_attn: float32 [1024], replicated, may hold values from -2.5 to 2.5
- w_inner: bfloat16 [1024, 4096], P(None, 'head'), may hold values from -0.1875 to 0.1875
- b_inner: float32 [4096], P('head'), may hold values from -2.5 to 2.5
- w_outer: bfloat16 [4096, 1024], P('head'), may hold values from -0.125 to 0.125
- b_outer: float32 [1024], replicated, may hold values from -1.5 to 1.5
- gain_ffn: float32 [1024], replicated, may hold values from 0.1 to 1.9
- shift_ffn: float32 [1024], replicated, may hold values from -2.5 to 2.5
- rel_tables: bfloat16 [3, 128, 1024], replicated, may hold values from -6 to 6
- cotangent: bfloat16 [4608, 1024], P('batch'), may hold values from -6 to 6
Outputs:
- output: bfloat16 [4608, 1024], P('batch')
- grad_tokens: bfloat16 [4608, 1024], P('batch')
- grad_w_query: float32 [1024, 1024], P('batch', 'head')
- grad_w_key: float32 [1024, 1024], P('batch', 'head')
- grad_w_value: float32 [1024, 1024], P('batch', 'head')
- grad_w_output: float32 [1024, 1024], P('head', 'batch')
- grad_b_output: float32 [1024], replicated
- grad_gain_attn: float32 [1024], replicated
- grad_shift_attn: float32 [1024], replicated
- grad_w_inner: float32 [1024, 4096], P('batch', 'head')
- grad_b_inner: float32 [4096], P('head')
- grad_w_outer: float32 [4096, 1024], P('head', 'batch')
- grad_b_outer: float32 [1024], replicated
- grad_gain_ffn: float32 [1024], replicated
- grad_shift_ffn: float32 [1024], replicated
- grad_rel: float32 [3, 128, 1024], replicated
The draws below stay inside these ranges and needn't reach their ends.
All inputs are finite; a program needn't handle non-finite values.
Results may differ from the reference program's by a relative error of at most 0.02.
Values sent between devices are 32-bit elements; how exact they have to be, the bound alone decides.
A program may use at most 128 MiB of HBM per device.

```python
import jax
import jax.numpy as jnp
from jax import lax

D = 1024
HEADS = 16
HEAD = 64
FF = 4096
NB = 128
SLOTS = 576
BOX_STEP = 8
PAGES = 8
TOKENS = 4608


def with_ends(values, key, smallest, top_value):
    index_at = [jax.random.randint(jax.random.fold_in(key, axis), (), 0, length) for axis, length in enumerate(values.shape)]
    longest = values.shape.index(max(values.shape))
    beside = index_at[:longest] + [(index_at[longest] + 1) % values.shape[longest]] + index_at[longest + 1:]
    return values.at[tuple(index_at)].set(smallest).at[tuple(beside)].set(top_value)


def raised(values, rng, source, target, parts, factor):
    owner, partner = [(jnp.arange(values.shape[dim]) // (values.shape[dim] // parts)).reshape([-1 if axis == dim else 1 for axis in range(values.ndim)]) for dim in (source, target)]
    chosen = jax.random.permutation(rng, parts)[partner]
    strong = (owner == chosen) | (owner == (partner + parts // 2) % parts)
    return jnp.where(strong, factor * values, values)


def block_levels(key, dims, cuts, low, top_value):
    factor_of, own = 1.0, jax.random.fold_in(key, 6)
    for position, parts in cuts:
        draws = jnp.exp(jax.random.uniform(jax.random.fold_in(own, position), (parts,), jnp.float32, low / len(cuts), top_value / len(cuts)))
        factor_of = factor_of * jnp.repeat(draws, dims[position] // parts).reshape([-1 if axis == position else 1 for axis in range(len(dims))])
    return factor_of


def centred(own_key, dims, scale, reach, cuts=(), kind=jnp.bfloat16):
    factor_of = block_levels(own_key, dims, cuts, -0.22, 0.18) if cuts else 1.0
    result = jax.random.normal(own_key, dims, jnp.float32) * scale * factor_of
    return jnp.minimum(jnp.maximum(result, -reach), reach).astype(kind)


def heavy_noise(stream_key, extent, deviation, reach, split, heavy, kind=jnp.bfloat16):
    values = deviation * jax.random.normal(stream_key, extent, jnp.float32)
    if split:
        values = values * block_levels(stream_key, extent, split, -0.22, 0.18)
    return jnp.clip(raised(values, jax.random.fold_in(stream_key, 3), *heavy), -reach, reach).astype(kind)


def setup_inputs(seed: int = 0) -> dict:
    key_list = jax.random.split(jax.random.key(seed), 19)
    tokens = centred(key_list[0], (TOKENS, D), 1.0, 6.0, ((0, 8),))
    page_lengths = with_ends(jax.random.randint(key_list[1], (PAGES,), SLOTS // 4, SLOTS + 1), jax.random.fold_in(key_list[1], 1), SLOTS // 4, SLOTS).astype(jnp.int32)
    corners = with_ends(jax.random.randint(key_list[2], (2, TOKENS), 0, 1024), jax.random.fold_in(key_list[2], 1), 0, 1023).astype(jnp.int32)
    w_query = centred(key_list[3], (D, HEADS * HEAD), D ** -0.5, 0.1875, ((1, 4),))
    w_key = centred(key_list[4], (D, HEADS * HEAD), D ** -0.5, 0.1875, ((1, 4),))
    w_value = centred(key_list[5], (D, HEADS * HEAD), D ** -0.5, 0.1875, ((1, 4),))
    w_output = centred(key_list[6], (HEADS * HEAD, D), (D // 16) ** -0.5, 0.75, ((0, 4),))
    b_output = centred(key_list[7], (D,), 0.3, 1.5, (), jnp.float32)
    gain_attn = jnp.clip(1.0 + 0.18 * jax.random.normal(key_list[8], (D,), jnp.float32), 0.1, 1.9)
    shift_attn = centred(key_list[9], (D,), 0.5, 2.5, (), jnp.float32)
    w_inner = centred(key_list[10], (D, FF), D ** -0.5, 0.1875, ((1, 4),))
    b_inner = centred(key_list[11], (FF,), 0.5, 2.5, ((0, 4),), jnp.float32)
    w_outer = centred(key_list[12], (FF, D), (FF // 2) ** -0.5, 0.125, ((0, 4),))
    b_outer = centred(key_list[13], (D,), 0.3, 1.5, (), jnp.float32)
    gain_ffn = jnp.clip(1.0 + 0.18 * jax.random.normal(key_list[14], (D,), jnp.float32), 0.1, 1.9)
    shift_ffn = centred(key_list[15], (D,), 0.5, 2.5, (), jnp.float32)
    rel_tables = centred(key_list[16], (3, NB, D), 1.0, 6.0)
    cotangent = heavy_noise(key_list[17], (TOKENS, D), 1.0, 6.0, ((0, 8),), (0, 1, 8, 2.0))
    return dict(tokens=tokens, page_lengths=page_lengths, corners=corners, w_query=w_query, w_key=w_key, w_value=w_value, w_output=w_output, b_output=b_output, gain_attn=gain_attn, shift_attn=shift_attn, w_inner=w_inner, b_inner=b_inner, w_outer=w_outer, b_outer=b_outer, gain_ffn=gain_ffn, shift_ffn=shift_ffn, rel_tables=rel_tables, cotangent=cotangent)


@jax.custom_vjp
def low(v):
    return lax.optimization_barrier(v.astype(jnp.bfloat16)).astype(jnp.float32)

@jax.custom_vjp
def low_back(v):
    return v

def low_keep(v):
    return (low(v), None)

def low_pass(kept, grad):
    return (grad,)

def back_keep(v):
    return (v, None)

def back_low(kept, grad):
    return (low(grad),)
low.defvjp(low_keep, low_pass)
low_back.defvjp(back_keep, back_low)
NEG_FILL = -1000000000.0

def matmul(inputs, weight):
    return jnp.dot(inputs, weight, preferred_element_type=jnp.float32, precision=lax.Precision.HIGHEST)

def einsum_full_precision(pattern, operand_a, operand_b):
    return jnp.einsum(pattern, operand_a, operand_b, precision=lax.Precision.HIGHEST)

def bucket_table(coord_row, step_size):
    difference = coord_row[:, None] - coord_row[None, :]
    return jnp.clip(difference // step_size, -(NB // 2), NB // 2 - 1) + NB // 2

def layer_norm(values, gain_in, shift_in):
    average = lax.optimization_barrier(jnp.mean(values, axis=-1, keepdims=True))
    centered = values - average
    spread_squared = lax.optimization_barrier(jnp.mean(centered * centered, axis=-1, keepdims=True))
    return centered * lax.rsqrt(spread_squared + 1e-05) * gain_in + shift_in

def page_attention(query_page_rows, key_page, value_page, key_relative_table, query_rel, length, corner_x, corner_y):
    positions = jnp.arange(SLOTS, dtype=jnp.int32)
    tables = (bucket_table(positions, 1), bucket_table(corner_x, BOX_STEP), bucket_table(corner_y, BOX_STEP))
    summed = einsum_full_precision('ihd,jhd->hij', query_page_rows, key_page)
    for transposed_tensor in range(3):
        lookup = jnp.broadcast_to(tables[transposed_tensor][None], (HEADS, SLOTS, SLOTS))
        forward_offset = einsum_full_precision('exk,pxk->xep', query_page_rows, key_relative_table[transposed_tensor])
        summed = summed + jnp.take_along_axis(forward_offset, lookup, axis=2)
        beside = einsum_full_precision('jhd,bhd->hjb', key_page, query_rel[transposed_tensor])
        summed = summed + jnp.transpose(jnp.take_along_axis(beside, lookup, axis=2), (0, 2, 1))
    logits = low_back(summed * (7.0 * HEAD) ** (-0.5))
    masked = jnp.where(positions[None, None, :] < length, logits, NEG_FILL)
    attend = low(jax.nn.softmax(masked, axis=-1))
    return low_back(low(einsum_full_precision('hij,jhd->ihd', attend, value_page)))

def forward(tokens, w_query, w_key, w_value, w_output, b_output, gain_attn, shift_attn, w_inner, b_inner, w_outer, b_outer, gain_ffn, shift_ffn, rel_tables, page_lengths, corners):
    queries = low_back(low(matmul(tokens, w_query)))
    key_rows = low_back(low(matmul(tokens, w_key)))
    value_rows = low_back(low(matmul(tokens, w_value)))
    key_relative_table = low(einsum_full_precision('tbc,cd->tbd', rel_tables, w_key)).reshape(3, NB, HEADS, HEAD)
    query_rel = low(einsum_full_precision('tbc,cd->tbd', rel_tables, w_query)).reshape(3, NB, HEADS, HEAD)

    def by_page(matrix):
        return matrix.reshape(PAGES, SLOTS, HEADS, HEAD)

    def one_page(pieces):
        return page_attention(pieces[0], pieces[1], pieces[2], key_relative_table, query_rel, pieces[3], pieces[4], pieces[5])
    context = lax.map(jax.checkpoint(one_page), (by_page(queries), by_page(key_rows), by_page(value_rows), page_lengths, corners[0].reshape(PAGES, SLOTS), corners[1].reshape(PAGES, SLOTS)))
    context = context.reshape(TOKENS, HEADS * HEAD)
    attended = low_back(matmul(context, w_output))
    hidden_one = layer_norm(attended + b_output + tokens, gain_attn, shift_attn)
    inner_pre = low_back(matmul(low(hidden_one), w_inner) + b_inner)
    active = low(jax.nn.gelu(inner_pre, approximate=False))
    outer_sum = low_back(matmul(active, w_outer))
    return layer_norm(outer_sum + b_outer + hidden_one, gain_ffn, shift_ffn)

def reference(tokens, page_lengths, corners, w_query, w_key, w_value, w_output, b_output, gain_attn, shift_attn, w_inner, b_inner, w_outer, b_outer, gain_ffn, shift_ffn, rel_tables, cotangent):
    params = tuple((item.astype(jnp.float32) for item in (tokens, w_query, w_key, w_value, w_output, b_output, gain_attn, shift_attn, w_inner, b_inner, w_outer, b_outer, gain_ffn, shift_ffn, rel_tables)))
    output, pull = jax.vjp(lambda *inputs: forward(*inputs, page_lengths, corners), *params)
    grads = pull(cotangent.astype(jnp.float32))
    return (output.astype(jnp.bfloat16), grads[0].astype(jnp.bfloat16), grads[1], grads[2], grads[3], grads[4], grads[5], grads[6], grads[7], grads[8], grads[9], grads[10], grads[11], grads[12], grads[13], grads[14])
```

```python
import functools

import jax
import jax.numpy as jnp
from jax import lax
from jax.experimental import pallas as pl
from jax.experimental.pallas import tpu as pltpu
from jax.sharding import PartitionSpec as P

HEAD = 64
NB = 128
BOX_STEP = 8
NEG_FILL = -1000000000.0
LANES = 128
VMEM_LIMIT = 60 * 1024 * 1024


def dot_nn(a, b):
    return lax.dot_general(a, b, (((1,), (0,)), ((), ())), preferred_element_type=jnp.float32)


def dot_nt(a, b):
    return lax.dot_general(a, b, (((1,), (1,)), ((), ())), preferred_element_type=jnp.float32)


def dot_tn(a, b):
    return lax.dot_general(a, b, (((0,), (0,)), ((), ())), preferred_element_type=jnp.float32)


def lane_gather(table, index):
    return jnp.take_along_axis(table, index, axis=1, mode="promise_in_bounds")


def attention_forward_kernel(
    length_ref, tok_ref, wq_ref, wk_ref, wv_ref, rel_ref, col_ref, row_ref, wo_ref,
    q_ref, k_ref, v_ref, krel_ref, qrel_ref, attend_ref, ctx_ref, part_ref,
    idx_ref, log_ref, col_part_ref, tq_ref, tk_ref, kv_ref,
):
    slots = tok_ref.shape[0]
    wide = row_ref.shape[1]
    heads = wq_ref.shape[1] // HEAD
    chunks = wide // LANES
    scale = (7.0 * HEAD) ** (-0.5)
    tok = tok_ref[...]
    q_ref[...] = dot_nn(tok, wq_ref[...]).astype(jnp.bfloat16)
    k_ref[...] = dot_nn(tok, wk_ref[...]).astype(jnp.bfloat16)
    v_ref[...] = dot_nn(tok, wv_ref[...]).astype(jnp.bfloat16)
    rel = rel_ref[...]
    krel_ref[...] = dot_nn(rel, wk_ref[...]).astype(jnp.bfloat16)
    qrel_ref[...] = dot_nn(rel, wq_ref[...]).astype(jnp.bfloat16)
    kv_ref[...] = jnp.zeros_like(kv_ref)
    kv_ref[0, :slots, :] = k_ref[...]
    kv_ref[1, :slots, :] = v_ref[...]
    if wide > slots:
        col_part_ref[slots:, :] = jnp.zeros((wide - slots, wide), jnp.float32)

    block = 32
    length = length_ref[0]

    @pl.loop(0, slots // block)
    def _(step):
        at = pl.ds(pl.multiple_of(step * block, block), block)
        for kind in range(2):
            own = col_ref[at, kind : kind + 1]
            other = row_ref[kind : kind + 1, :]
            bucket = jnp.clip((own - other) >> 3, -(NB // 2), NB // 2 - 1) + NB // 2
            idx_ref[kind, at, :] = bucket

    for head in range(heads):
        cols = slice(head * HEAD, (head + 1) * HEAD)
        q_h = q_ref[:, cols]
        tq_ref[...] = dot_nt(q_h, krel_ref[:, cols])
        tk_ref[...] = dot_nt(k_ref[:, cols], qrel_ref[:, cols])
        log_ref[...] = dot_nt(q_h, kv_ref[0, :, cols])

        for big in range(chunks):
            rows_here = min(LANES, slots - big * LANES)

            @pl.loop(0, rows_here // block)
            def _(step, big=big):
                start = pl.multiple_of(big * LANES + step * block, block)
                at = pl.ds(start, block)
                tq = [tq_ref[at, t * NB : (t + 1) * NB] for t in range(3)]
                tk = [tk_ref[at, t * NB : (t + 1) * NB] for t in range(3)]
                for chunk in range(chunks):
                    lanes = slice(chunk * LANES, (chunk + 1) * LANES)
                    if big - chunk >= 2:
                        far = NB - 1
                        s1, s2 = tq[0][:, far : far + 1], tk[0][:, far : far + 1]
                    elif chunk - big >= 2:
                        s1, s2 = tq[0][:, 0:1], tk[0][:, 0:1]
                    else:
                        i_at = lax.broadcasted_iota(jnp.int32, (block, LANES), 0) + start
                        j_at = lax.broadcasted_iota(jnp.int32, (block, LANES), 1) + chunk * LANES
                        near = jnp.clip(i_at - j_at, -(NB // 2), NB // 2 - 1) + NB // 2
                        s1, s2 = lane_gather(tq[0], near), lane_gather(tk[0], near)
                    for kind in range(2):
                        index = idx_ref[kind, at, lanes]
                        s1 = s1 + lane_gather(tq[kind + 1], index)
                        s2 = s2 + lane_gather(tk[kind + 1], index)
                    log_ref[at, lanes] += s1
                    col_part_ref[at, lanes] = s2

        for big in range(chunks):
            rows_here = min(LANES, slots - big * LANES)
            at = slice(big * LANES, big * LANES + rows_here)
            for chunk in range(chunks):
                lanes = slice(chunk * LANES, (chunk + 1) * LANES)
                turned = col_part_ref[lanes, big * LANES : (big + 1) * LANES].T
                log_ref[at, lanes] += turned[:rows_here]

        @pl.loop(0, slots // block)
        def _(step, head=head):
            at = pl.ds(pl.multiple_of(step * block, block), block)
            j_at = lax.broadcasted_iota(jnp.int32, (block, wide), 1)
            masked = jnp.where(j_at < length, log_ref[at, :] * scale, NEG_FILL)
            peak = jnp.max(masked, axis=-1, keepdims=True)
            grown = jnp.exp(masked - peak)
            total = jnp.sum(grown, axis=-1, keepdims=True)
            attend_ref[head, at, :] = (grown / total).astype(jnp.bfloat16)

        ctx_ref[:, cols] = dot_nn(attend_ref[head], kv_ref[1, :, cols]).astype(jnp.bfloat16)
    part_ref[...] = dot_nn(ctx_ref[...], wo_ref[...])


def attention_forward(tokens, length, corner_col, corner_row, w_query, w_key, w_value, rel, w_output):
    slots, width = tokens.shape
    mine = w_query.shape[1]
    heads = mine // HEAD
    wide = corner_row.shape[1]
    low = jnp.bfloat16
    vmem = pl.BlockSpec(memory_space=pltpu.VMEM)
    return pl.pallas_call(
        attention_forward_kernel,
        out_shape=(
            jax.ShapeDtypeStruct((slots, mine), low),
            jax.ShapeDtypeStruct((slots, mine), low),
            jax.ShapeDtypeStruct((slots, mine), low),
            jax.ShapeDtypeStruct((3 * NB, mine), low),
            jax.ShapeDtypeStruct((3 * NB, mine), low),
            jax.ShapeDtypeStruct((heads, slots, wide), low),
            jax.ShapeDtypeStruct((slots, mine), low),
            jax.ShapeDtypeStruct((slots, width), jnp.float32),
        ),
        in_specs=[pl.BlockSpec(memory_space=pltpu.SMEM)] + [vmem] * 8,
        out_specs=(vmem,) * 8,
        scratch_shapes=[
            pltpu.VMEM((2, slots, wide), jnp.int32),
            pltpu.VMEM((slots, wide), jnp.float32),
            pltpu.VMEM((wide, wide), jnp.float32),
            pltpu.VMEM((slots, 3 * NB), jnp.float32),
            pltpu.VMEM((slots, 3 * NB), jnp.float32),
            pltpu.VMEM((2, wide, mine), low),
        ],
        compiler_params=pltpu.CompilerParams(vmem_limit_bytes=VMEM_LIMIT),
        name="attention_forward",
    )(length, tokens, w_query, w_key, w_value, rel, corner_col, corner_row, w_output)
def attention_backward_kernel(
    grad_ref, tok_ref, wq_ref, wk_ref, wv_ref, wo_ref, rel_ref, col_ref,
    q_ref, k_ref, v_ref, krel_ref, qrel_ref, attend_ref, ctx_ref,
    gwq_ref, gwk_ref, gwv_ref, gwo_ref, gin_ref, grel_ref,
    gc_ref, step_ref, kv_ref, mat_ref, fold_ref, hist_ref, gq_ref, gk_ref, gv_ref,
    gkrel_ref, gqrel_ref,
):
    slots = tok_ref.shape[0]
    wide = mat_ref.shape[1]
    heads = wq_ref.shape[1] // HEAD
    chunks = wide // LANES
    scale = (7.0 * HEAD) ** (-0.5)
    low = jnp.bfloat16
    block = 32
    gc_ref[...] = dot_nt(grad_ref[...], wo_ref[...]).astype(low)
    gwo_ref[...] = dot_tn(ctx_ref[...], grad_ref[...])
    kv_ref[...] = jnp.zeros_like(kv_ref)
    kv_ref[0, :slots, :] = k_ref[...]
    kv_ref[1, :slots, :] = v_ref[...]
    mat_ref[...] = jnp.zeros_like(mat_ref)
    step_ref[...] = jnp.zeros_like(step_ref)

    @pl.loop(0, slots // block)
    def _(step):
        at = pl.ds(pl.multiple_of(step * block, block), block)
        quotient = lax.broadcasted_iota(jnp.int32, (block, NB), 1) * BOX_STEP
        for kind in range(2):
            own = col_ref[at, kind : kind + 1]
            for rest in range(BOX_STEP):
                lanes = slice(rest * NB, (rest + 1) * NB)
                step_ref[kind, at, lanes] = (own <= quotient + rest).astype(jnp.float32).astype(low)

    for head in range(heads):
        cols = slice(head * HEAD, (head + 1) * HEAD)
        gc_h = gc_ref[:, cols]
        grad_attend = dot_nt(gc_h, kv_ref[1, :, cols])
        mean = jnp.sum(gc_h.astype(jnp.float32) * ctx_ref[:, cols].astype(jnp.float32), axis=-1, keepdims=True)
        mat_ref[0, :slots, :] = (attend_ref[head].astype(jnp.float32) * (grad_attend - mean)).astype(low)
        gv_ref[:, cols] = dot_tn(attend_ref[head], gc_h)[:slots].astype(low)
        for big in range(chunks):
            for chunk in range(chunks):
                here = slice(big * LANES, (big + 1) * LANES)
                there = slice(chunk * LANES, (chunk + 1) * LANES)
                mat_ref[1, there, here] = mat_ref[0, here, there].T

        for side in range(2):
            for kind in range(2):
                fold_ref[kind] = dot_nn(mat_ref[side, :slots, :], step_ref[kind])

            for big in range(chunks):
                rows_here = min(LANES, slots - big * LANES)

                @pl.loop(0, rows_here // block)
                def _(step, big=big, side=side):
                    local = step * block
                    at = pl.ds(pl.multiple_of(big * LANES + local, block), block)
                    lane = lax.broadcasted_iota(jnp.int32, (block, NB), 1)
                    row = lax.broadcasted_iota(jnp.int32, (block, NB), 0) + local
                    part = [
                        mat_ref[side, at, c * LANES : (c + 1) * LANES].astype(jnp.float32)
                        for c in range(chunks)
                    ]
                    zero = jnp.zeros((block, LANES), jnp.float32)
                    before = part[big - 1] if big >= 1 else zero
                    after = part[big + 1] if big + 1 < chunks else zero
                    mid = part[big]
                    delta = lane - row
                    window = jnp.where(
                        delta > NB // 2, before, jnp.where(delta < 1 - NB // 2, after, mid)
                    )
                    spread = lane_gather(window, (row + NB // 2 - lane) & (NB - 1))
                    under = jnp.where(delta <= NB // 2 + 1, before, 0.0) + jnp.where(
                        delta <= 1 - NB // 2, mid, 0.0
                    )
                    over = jnp.where(delta >= NB // 2, mid, 0.0) + jnp.where(
                        delta >= -(NB // 2), after, 0.0
                    )
                    for c in range(big - 1):
                        under = under + part[c]
                    for c in range(big + 2, chunks):
                        over = over + part[c]
                    under = jnp.sum(under, axis=-1, keepdims=True)
                    over = jnp.sum(over, axis=-1, keepdims=True)
                    spread = jnp.where(lane == 0, over, jnp.where(lane == NB - 1, under, spread))
                    hist_ref[side, at, 0:NB] = spread.astype(low)
                    for kind in range(2):
                        own = col_ref[at, kind : kind + 1]
                        rest = jnp.broadcast_to(own & (BOX_STEP - 1), (block, NB))
                        whole = jnp.broadcast_to(own >> 3, (block, NB))
                        groups = [
                            fold_ref[kind, at, r * NB : (r + 1) * NB] for r in range(BOX_STEP)
                        ]
                        every = groups[-1][:, NB - 1 : NB]
                        for bit in range(3):
                            odd = (rest & (1 << bit)) != 0
                            groups = [
                                jnp.where(odd, groups[g + 1], groups[g])
                                for g in range(0, len(groups), 2)
                            ]
                        index = whole + NB // 2 - lane
                        found = lane_gather(groups[0], index & (NB - 1))
                        found = jnp.where(index < 0, 0.0, found)
                        found = jnp.where((index >= NB) | (lane == 0), every, found)
                        following = pltpu.roll(found, NB - 1, 1)
                        found = found - jnp.where(lane == NB - 1, 0.0, following)
                        hist_ref[side, at, (kind + 1) * NB : (kind + 2) * NB] = found.astype(low)

        q_h, k_h = q_ref[:, cols], k_ref[:, cols]
        gq = dot_nn(mat_ref[0, :slots, :], kv_ref[0, :, cols]) + dot_nn(hist_ref[0], krel_ref[:, cols])
        gk = dot_nn(mat_ref[1, :slots, :slots], q_h) + dot_nn(hist_ref[1], qrel_ref[:, cols])
        gq_ref[:, cols] = (gq * scale).astype(low)
        gk_ref[:, cols] = (gk * scale).astype(low)
        gkrel_ref[:, cols] = (dot_tn(hist_ref[0], q_h) * scale).astype(low)
        gqrel_ref[:, cols] = (dot_tn(hist_ref[1], k_h) * scale).astype(low)

    tok, rel = tok_ref[...], rel_ref[...]
    gwq_ref[...] = dot_tn(tok, gq_ref[...]) + dot_tn(rel, gqrel_ref[...])
    gwk_ref[...] = dot_tn(tok, gk_ref[...]) + dot_tn(rel, gkrel_ref[...])
    gwv_ref[...] = dot_tn(tok, gv_ref[...])
    gin_ref[...] = (
        dot_nt(gq_ref[...], wq_ref[...])
        + dot_nt(gk_ref[...], wk_ref[...])
        + dot_nt(gv_ref[...], wv_ref[...])
    )
    grel_ref[...] = dot_nt(gkrel_ref[...], wk_ref[...]) + dot_nt(gqrel_ref[...], wq_ref[...])


def attention_backward(
    grad, tokens, w_query, w_key, w_value, w_output, rel, corner_col, q, k, v, krel, qrel, attend, ctx
):
    slots, width = tokens.shape
    mine = w_query.shape[1]
    wide = attend.shape[2]
    low, full = jnp.bfloat16, jnp.float32
    vmem = pl.BlockSpec(memory_space=pltpu.VMEM)
    return pl.pallas_call(
        attention_backward_kernel,
        out_shape=(
            jax.ShapeDtypeStruct((width, mine), full),
            jax.ShapeDtypeStruct((width, mine), full),
            jax.ShapeDtypeStruct((width, mine), full),
            jax.ShapeDtypeStruct((mine, width), full),
            jax.ShapeDtypeStruct((slots, width), full),
            jax.ShapeDtypeStruct((3 * NB, width), full),
        ),
        in_specs=[vmem] * 15,
        out_specs=(vmem,) * 6,
        scratch_shapes=[
            pltpu.VMEM((slots, mine), low),
            pltpu.VMEM((2, wide, BOX_STEP * NB), low),
            pltpu.VMEM((2, wide, mine), low),
            pltpu.VMEM((2, wide, wide), low),
            pltpu.VMEM((2, slots, BOX_STEP * NB), full),
            pltpu.VMEM((2, slots, 3 * NB), low),
            pltpu.VMEM((slots, mine), low),
            pltpu.VMEM((slots, mine), low),
            pltpu.VMEM((slots, mine), low),
            pltpu.VMEM((3 * NB, mine), low),
            pltpu.VMEM((3 * NB, mine), low),
        ],
        compiler_params=pltpu.CompilerParams(vmem_limit_bytes=VMEM_LIMIT),
        name="attention_backward",
    )(grad, tokens, w_query, w_key, w_value, w_output, rel, corner_col, q, k, v, krel, qrel, attend, ctx)


def layer_stats(values):
    average = jnp.mean(values, axis=-1, keepdims=True)
    centered = values - average
    spread_squared = jnp.mean(centered * centered, axis=-1, keepdims=True)
    scaling = lax.rsqrt(spread_squared + 1e-05)
    return (centered * scaling, scaling)


def norm_back(upstream, normed, scaling, gain_in):
    scaled = upstream * gain_in
    inward = scaling * (
        scaled
        - jnp.mean(scaled, axis=-1, keepdims=True)
        - normed * jnp.mean(scaled * normed, axis=-1, keepdims=True)
    )
    return (inward, jnp.sum(upstream * normed, axis=0), jnp.sum(upstream, axis=0))


def shards(
    tokens,
    page_lengths,
    corners,
    w_query,
    w_key,
    w_value,
    w_output,
    b_output,
    gain_attn,
    shift_attn,
    w_inner,
    b_inner,
    w_outer,
    b_outer,
    gain_ffn,
    shift_ffn,
    rel_tables,
    cotangent,
):
    slots_page = tokens.shape[0]
    wide = -(-slots_page // LANES) * LANES
    rel_rows = rel_tables.reshape(3 * NB, rel_tables.shape[2])
    corner_col = corners.T
    corner_row = jnp.pad(corners, ((0, 0), (0, wide - slots_page)))
    kept = attention_forward(
        tokens, page_lengths, corner_col, corner_row, w_query, w_key, w_value, rel_rows, w_output
    )
    partial_attn = kept[7]
    token_float = tokens.astype(jnp.float32)
    attention_total = lax.psum(partial_attn, "head")
    normed_one, scale_one = layer_stats(attention_total + b_output + token_float)
    hidden_one = normed_one * gain_attn + shift_attn
    hidden_low = hidden_one.astype(jnp.bfloat16)
    inner_pre = jnp.dot(hidden_low, w_inner, preferred_element_type=jnp.float32) + b_inner
    active = jax.nn.gelu(inner_pre, approximate=False).astype(jnp.bfloat16)
    partial_ffn = jnp.dot(active, w_outer, preferred_element_type=jnp.float32)
    ffn_total = lax.psum(partial_ffn, "head")
    normed_two, scale_two = layer_stats(ffn_total + b_outer + hidden_one)
    output = (normed_two * gain_ffn + shift_ffn).astype(jnp.bfloat16)
    grad_out = cotangent.astype(jnp.float32)
    grad_mid, grad_gain_ffn, grad_shift_ffn = norm_back(grad_out, normed_two, scale_two, gain_ffn)
    grad_b_outer = jnp.sum(grad_mid, axis=0)
    grad_mid_low = grad_mid.astype(jnp.bfloat16)
    grad_w_outer = jnp.einsum("tf,td->fd", active, grad_mid_low, preferred_element_type=jnp.float32)
    grad_active = jnp.einsum("td,fd->tf", grad_mid_low, w_outer, preferred_element_type=jnp.float32)
    _, gelu_pull = jax.vjp(lambda pre_value: jax.nn.gelu(pre_value, approximate=False), inner_pre)
    grad_inner = gelu_pull(grad_active)[0]
    grad_b_inner = jnp.sum(grad_inner, axis=0)
    grad_inner_low = grad_inner.astype(jnp.bfloat16)
    grad_w_inner = jnp.einsum(
        "td,tf->df", hidden_low, grad_inner_low, preferred_element_type=jnp.float32
    )
    partial_hidden = jnp.einsum(
        "tf,df->td", grad_inner_low, w_inner, preferred_element_type=jnp.float32
    )
    grad_hidden = lax.psum(partial_hidden, "head") + grad_mid
    grad_attn, grad_gain_attn, grad_shift_attn = norm_back(
        grad_hidden, normed_one, scale_one, gain_attn
    )
    grad_b_output = jnp.sum(grad_attn, axis=0)
    grad_attn_low = grad_attn.astype(jnp.bfloat16)
    grad_w_query, grad_w_key, grad_w_value, grad_w_output, partial_input, partial_rel = (
        attention_backward(
            grad_attn_low, tokens, w_query, w_key, w_value, w_output, rel_rows, corner_col, *kept[:7]
        )
    )
    grad_tokens = (lax.psum(partial_input, "head") + grad_attn).astype(jnp.bfloat16)
    grad_rel = lax.psum(partial_rel, ("batch", "head")).reshape(rel_tables.shape)
    summed_weights = (
        lax.psum_scatter(grad_w_query, "batch", scatter_dimension=0, tiled=True),
        lax.psum_scatter(grad_w_key, "batch", scatter_dimension=0, tiled=True),
        lax.psum_scatter(grad_w_value, "batch", scatter_dimension=0, tiled=True),
        lax.psum_scatter(grad_w_output, "batch", scatter_dimension=1, tiled=True),
        lax.psum_scatter(grad_w_inner, "batch", scatter_dimension=0, tiled=True),
        lax.psum_scatter(grad_w_outer, "batch", scatter_dimension=1, tiled=True),
    )
    summed_small = lax.psum(
        (
            grad_b_output,
            grad_gain_attn,
            grad_shift_attn,
            grad_b_inner,
            grad_b_outer,
            grad_gain_ffn,
            grad_shift_ffn,
        ),
        "batch",
    )
    return (
        output,
        grad_tokens,
        summed_weights[0],
        summed_weights[1],
        summed_weights[2],
        summed_weights[3],
        summed_small[0],
        summed_small[1],
        summed_small[2],
        summed_weights[4],
        summed_small[3],
        summed_weights[5],
        summed_small[4],
        summed_small[5],
        summed_small[6],
        grad_rel,
    )


def solution(mesh):
    in_specs = (
        P("batch", None),
        P("batch"),
        P(None, "batch"),
        P(None, "head"),
        P(None, "head"),
        P(None, "head"),
        P("head", None),
        P(),
        P(),
        P(),
        P(None, "head"),
        P("head"),
        P("head", None),
        P(),
        P(),
        P(),
        P(),
        P("batch", None),
    )
    out_specs = (
        P("batch", None),
        P("batch", None),
        P("batch", "head"),
        P("batch", "head"),
        P("batch", "head"),
        P("head", "batch"),
        P(),
        P(),
        P(),
        P("batch", "head"),
        P("head"),
        P("head", "batch"),
        P(),
        P(),
        P(),
        P(),
    )
    return jax.shard_map(shards, mesh=mesh, in_specs=in_specs, out_specs=out_specs, check_vma=False)
```

```python
import functools

import jax
import jax.numpy as jnp
from jax import lax
from jax.experimental import pallas as pl
from jax.experimental.pallas import tpu as pltpu
from jax.sharding import PartitionSpec as P

HEAD = 64
NB = 128
BOX_STEP = 8
NEG_FILL = -1000000000.0
LANES = 128
VMEM_LIMIT = 60 * 1024 * 1024


def dot_nn(a, b):
    return lax.dot_general(a, b, (((1,), (0,)), ((), ())), preferred_element_type=jnp.float32)


def dot_nt(a, b):
    return lax.dot_general(a, b, (((1,), (1,)), ((), ())), preferred_element_type=jnp.float32)


def dot_tn(a, b):
    return lax.dot_general(a, b, (((0,), (0,)), ((), ())), preferred_element_type=jnp.float32)


def lane_gather(table, index):
    return jnp.take_along_axis(table, index, axis=1, mode="promise_in_bounds")


def attention_forward_kernel(
    length_ref, tok_ref, wq_ref, wk_ref, wv_ref, rel_ref, col_ref, row_ref,
    q_ref, k_ref, v_ref, krel_ref, qrel_ref, attend_ref, ctx_ref,
    idx_ref, log_ref, col_part_ref, tq_ref, tk_ref, kv_ref,
):
    slots = tok_ref.shape[0]
    wide = row_ref.shape[1]
    heads = wq_ref.shape[1] // HEAD
    chunks = wide // LANES
    scale = (7.0 * HEAD) ** (-0.5)
    tok = tok_ref[...]
    q_ref[...] = dot_nn(tok, wq_ref[...]).astype(jnp.bfloat16)
    k_ref[...] = dot_nn(tok, wk_ref[...]).astype(jnp.bfloat16)
    v_ref[...] = dot_nn(tok, wv_ref[...]).astype(jnp.bfloat16)
    rel = rel_ref[...]
    krel_ref[...] = dot_nn(rel, wk_ref[...]).astype(jnp.bfloat16)
    qrel_ref[...] = dot_nn(rel, wq_ref[...]).astype(jnp.bfloat16)
    kv_ref[...] = jnp.zeros_like(kv_ref)
    kv_ref[0, :slots, :] = k_ref[...]
    kv_ref[1, :slots, :] = v_ref[...]
    if wide > slots:
        col_part_ref[slots:, :] = jnp.zeros((wide - slots, wide), jnp.float32)

    block = 32
    length = length_ref[0]

    @pl.loop(0, slots // block)
    def _(step):
        at = pl.ds(pl.multiple_of(step * block, block), block)
        for kind in range(2):
            own = col_ref[at, kind : kind + 1]
            other = row_ref[kind : kind + 1, :]
            bucket = jnp.clip((own - other) >> 3, -(NB // 2), NB // 2 - 1) + NB // 2
            idx_ref[kind, at, :] = bucket

    for head in range(heads):
        cols = slice(head * HEAD, (head + 1) * HEAD)
        q_h = q_ref[:, cols]
        tq_ref[...] = dot_nt(q_h, krel_ref[:, cols])
        tk_ref[...] = dot_nt(k_ref[:, cols], qrel_ref[:, cols])
        log_ref[...] = dot_nt(q_h, kv_ref[0, :, cols])

        for big in range(chunks):
            rows_here = min(LANES, slots - big * LANES)

            @pl.loop(0, rows_here // block)
            def _(step, big=big):
                start = pl.multiple_of(big * LANES + step * block, block)
                at = pl.ds(start, block)
                tq = [tq_ref[at, t * NB : (t + 1) * NB] for t in range(3)]
                tk = [tk_ref[at, t * NB : (t + 1) * NB] for t in range(3)]
                for chunk in range(chunks):
                    lanes = slice(chunk * LANES, (chunk + 1) * LANES)
                    if big - chunk >= 2:
                        far = NB - 1
                        s1, s2 = tq[0][:, far : far + 1], tk[0][:, far : far + 1]
                    elif chunk - big >= 2:
                        s1, s2 = tq[0][:, 0:1], tk[0][:, 0:1]
                    else:
                        i_at = lax.broadcasted_iota(jnp.int32, (block, LANES), 0) + start
                        j_at = lax.broadcasted_iota(jnp.int32, (block, LANES), 1) + chunk * LANES
                        near = jnp.clip(i_at - j_at, -(NB // 2), NB // 2 - 1) + NB // 2
                        s1, s2 = lane_gather(tq[0], near), lane_gather(tk[0], near)
                    for kind in range(2):
                        index = idx_ref[kind, at, lanes]
                        s1 = s1 + lane_gather(tq[kind + 1], index)
                        s2 = s2 + lane_gather(tk[kind + 1], index)
                    log_ref[at, lanes] += s1
                    col_part_ref[at, lanes] = s2

        for big in range(chunks):
            rows_here = min(LANES, slots - big * LANES)
            at = slice(big * LANES, big * LANES + rows_here)
            for chunk in range(chunks):
                lanes = slice(chunk * LANES, (chunk + 1) * LANES)
                turned = col_part_ref[lanes, big * LANES : (big + 1) * LANES].T
                log_ref[at, lanes] += turned[:rows_here]

        @pl.loop(0, slots // block)
        def _(step, head=head):
            at = pl.ds(pl.multiple_of(step * block, block), block)
            j_at = lax.broadcasted_iota(jnp.int32, (block, wide), 1)
            masked = jnp.where(j_at < length, log_ref[at, :] * scale, NEG_FILL)
            peak = jnp.max(masked, axis=-1, keepdims=True)
            grown = jnp.exp(masked - peak)
            total = jnp.sum(grown, axis=-1, keepdims=True)
            attend_ref[head, at, :] = (grown / total).astype(jnp.bfloat16)

        ctx_ref[:, cols] = dot_nn(attend_ref[head], kv_ref[1, :, cols]).astype(jnp.bfloat16)


def attention_forward(tokens, length, corner_col, corner_row, w_query, w_key, w_value, rel):
    slots, width = tokens.shape
    mine = w_query.shape[1]
    heads = mine // HEAD
    wide = corner_row.shape[1]
    low = jnp.bfloat16
    vmem = pl.BlockSpec(memory_space=pltpu.VMEM)
    return pl.pallas_call(
        attention_forward_kernel,
        out_shape=(
            jax.ShapeDtypeStruct((slots, mine), low),
            jax.ShapeDtypeStruct((slots, mine), low),
            jax.ShapeDtypeStruct((slots, mine), low),
            jax.ShapeDtypeStruct((3 * NB, mine), low),
            jax.ShapeDtypeStruct((3 * NB, mine), low),
            jax.ShapeDtypeStruct((heads, slots, wide), low),
            jax.ShapeDtypeStruct((slots, mine), low),
        ),
        in_specs=[pl.BlockSpec(memory_space=pltpu.SMEM)] + [vmem] * 7,
        out_specs=(vmem,) * 7,
        scratch_shapes=[
            pltpu.VMEM((2, slots, wide), jnp.int32),
            pltpu.VMEM((slots, wide), jnp.float32),
            pltpu.VMEM((wide, wide), jnp.float32),
            pltpu.VMEM((slots, 3 * NB), jnp.float32),
            pltpu.VMEM((slots, 3 * NB), jnp.float32),
            pltpu.VMEM((2, wide, mine), low),
        ],
        compiler_params=pltpu.CompilerParams(vmem_limit_bytes=VMEM_LIMIT),
        name="attention_forward",
    )(length, tokens, w_query, w_key, w_value, rel, corner_col, corner_row)


def attention_backward_kernel(
    grad_ref, tok_ref, wq_ref, wk_ref, wv_ref, wo_ref, rel_ref, col_ref,
    q_ref, k_ref, v_ref, krel_ref, qrel_ref, attend_ref, ctx_ref,
    gwq_ref, gwk_ref, gwv_ref, gwo_ref, gin_ref, grel_ref,
    gc_ref, step_ref, kv_ref, mat_ref, fold_ref, hist_ref, gq_ref, gk_ref, gv_ref,
    gkrel_ref, gqrel_ref,
):
    slots = tok_ref.shape[0]
    wide = mat_ref.shape[1]
    heads = wq_ref.shape[1] // HEAD
    chunks = wide // LANES
    scale = (7.0 * HEAD) ** (-0.5)
    low = jnp.bfloat16
    block = 32
    gc_ref[...] = dot_nt(grad_ref[...], wo_ref[...]).astype(low)
    gwo_ref[...] = dot_tn(grad_ref[...], ctx_ref[...])
    kv_ref[...] = jnp.zeros_like(kv_ref)
    kv_ref[0, :slots, :] = k_ref[...]
    kv_ref[1, :slots, :] = v_ref[...]
    mat_ref[...] = jnp.zeros_like(mat_ref)
    step_ref[...] = jnp.zeros_like(step_ref)

    @pl.loop(0, slots // block)
    def _(step):
        at = pl.ds(pl.multiple_of(step * block, block), block)
        quotient = lax.broadcasted_iota(jnp.int32, (block, NB), 1) * BOX_STEP
        for kind in range(2):
            own = col_ref[at, kind : kind + 1]
            for rest in range(BOX_STEP):
                lanes = slice(rest * NB, (rest + 1) * NB)
                step_ref[kind, at, lanes] = (own <= quotient + rest).astype(jnp.float32).astype(low)

    for head in range(heads):
        cols = slice(head * HEAD, (head + 1) * HEAD)
        gc_h = gc_ref[:, cols]
        grad_attend = dot_nt(gc_h, kv_ref[1, :, cols])
        mean = jnp.sum(gc_h.astype(jnp.float32) * ctx_ref[:, cols].astype(jnp.float32), axis=-1, keepdims=True)
        mat_ref[0, :slots, :] = (attend_ref[head].astype(jnp.float32) * (grad_attend - mean)).astype(low)
        gv_ref[:, cols] = dot_tn(attend_ref[head], gc_h)[:slots].astype(low)
        for big in range(chunks):
            for chunk in range(chunks):
                here = slice(big * LANES, (big + 1) * LANES)
                there = slice(chunk * LANES, (chunk + 1) * LANES)
                mat_ref[1, there, here] = mat_ref[0, here, there].T

        for side in range(2):
            for kind in range(2):
                fold_ref[kind] = dot_nn(mat_ref[side, :slots, :], step_ref[kind])

            for big in range(chunks):
                rows_here = min(LANES, slots - big * LANES)

                @pl.loop(0, rows_here // block)
                def _(step, big=big, side=side):
                    local = step * block
                    at = pl.ds(pl.multiple_of(big * LANES + local, block), block)
                    lane = lax.broadcasted_iota(jnp.int32, (block, NB), 1)
                    row = lax.broadcasted_iota(jnp.int32, (block, NB), 0) + local
                    part = [
                        mat_ref[side, at, c * LANES : (c + 1) * LANES].astype(jnp.float32)
                        for c in range(chunks)
                    ]
                    zero = jnp.zeros((block, LANES), jnp.float32)
                    before = part[big - 1] if big >= 1 else zero
                    after = part[big + 1] if big + 1 < chunks else zero
                    mid = part[big]
                    delta = lane - row
                    window = jnp.where(
                        delta > NB // 2, before, jnp.where(delta < 1 - NB // 2, after, mid)
                    )
                    spread = lane_gather(window, (row + NB // 2 - lane) & (NB - 1))
                    under = jnp.where(delta <= NB // 2 + 1, before, 0.0) + jnp.where(
                        delta <= 1 - NB // 2, mid, 0.0
                    )
                    over = jnp.where(delta >= NB // 2, mid, 0.0) + jnp.where(
                        delta >= -(NB // 2), after, 0.0
                    )
                    for c in range(big - 1):
                        under = under + part[c]
                    for c in range(big + 2, chunks):
                        over = over + part[c]
                    under = jnp.sum(under, axis=-1, keepdims=True)
                    over = jnp.sum(over, axis=-1, keepdims=True)
                    spread = jnp.where(lane == 0, over, jnp.where(lane == NB - 1, under, spread))
                    hist_ref[side, at, 0:NB] = spread.astype(low)
                    for kind in range(2):
                        own = col_ref[at, kind : kind + 1]
                        rest = jnp.broadcast_to(own & (BOX_STEP - 1), (block, NB))
                        whole = jnp.broadcast_to(own >> 3, (block, NB))
                        groups = [
                            fold_ref[kind, at, r * NB : (r + 1) * NB] for r in range(BOX_STEP)
                        ]
                        every = groups[-1][:, NB - 1 : NB]
                        for bit in range(3):
                            odd = (rest & (1 << bit)) != 0
                            groups = [
                                jnp.where(odd, groups[g + 1], groups[g])
                                for g in range(0, len(groups), 2)
                            ]
                        index = whole + NB // 2 - lane
                        found = lane_gather(groups[0], index & (NB - 1))
                        found = jnp.where(index < 0, 0.0, found)
                        found = jnp.where((index >= NB) | (lane == 0), every, found)
                        following = pltpu.roll(found, NB - 1, 1)
                        found = found - jnp.where(lane == NB - 1, 0.0, following)
                        hist_ref[side, at, (kind + 1) * NB : (kind + 2) * NB] = found.astype(low)

        q_h, k_h = q_ref[:, cols], k_ref[:, cols]
        gq = dot_nn(mat_ref[0, :slots, :], kv_ref[0, :, cols]) + dot_nn(hist_ref[0], krel_ref[:, cols])
        gk = dot_nn(mat_ref[1, :slots, :slots], q_h) + dot_nn(hist_ref[1], qrel_ref[:, cols])
        gq_ref[:, cols] = (gq * scale).astype(low)
        gk_ref[:, cols] = (gk * scale).astype(low)
        gkrel_ref[:, cols] = (dot_tn(hist_ref[0], q_h) * scale).astype(low)
        gqrel_ref[:, cols] = (dot_tn(hist_ref[1], k_h) * scale).astype(low)

    tok, rel = tok_ref[...], rel_ref[...]
    gwq_ref[...] = dot_tn(tok, gq_ref[...]) + dot_tn(rel, gqrel_ref[...])
    gwk_ref[...] = dot_tn(tok, gk_ref[...]) + dot_tn(rel, gkrel_ref[...])
    gwv_ref[...] = dot_tn(tok, gv_ref[...])
    gin_ref[...] = (
        dot_nt(gq_ref[...], wq_ref[...])
        + dot_nt(gk_ref[...], wk_ref[...])
        + dot_nt(gv_ref[...], wv_ref[...])
    )
    grel_ref[...] = dot_nt(gkrel_ref[...], wk_ref[...]) + dot_nt(gqrel_ref[...], wq_ref[...])


def attention_backward(
    grad, tokens, w_query, w_key, w_value, w_output, rel, corner_col, q, k, v, krel, qrel, attend, ctx
):
    slots, width = tokens.shape
    mine = w_query.shape[1]
    wide = attend.shape[2]
    low, full = jnp.bfloat16, jnp.float32
    vmem = pl.BlockSpec(memory_space=pltpu.VMEM)
    return pl.pallas_call(
        attention_backward_kernel,
        out_shape=(
            jax.ShapeDtypeStruct((width, mine), full),
            jax.ShapeDtypeStruct((width, mine), full),
            jax.ShapeDtypeStruct((width, mine), full),
            jax.ShapeDtypeStruct((width, mine), full),
            jax.ShapeDtypeStruct((slots, width), full),
            jax.ShapeDtypeStruct((3 * NB, width), full),
        ),
        in_specs=[vmem] * 15,
        out_specs=(vmem,) * 6,
        scratch_shapes=[
            pltpu.VMEM((slots, mine), low),
            pltpu.VMEM((2, wide, BOX_STEP * NB), low),
            pltpu.VMEM((2, wide, mine), low),
            pltpu.VMEM((2, wide, wide), low),
            pltpu.VMEM((2, slots, BOX_STEP * NB), full),
            pltpu.VMEM((2, slots, 3 * NB), low),
            pltpu.VMEM((slots, mine), low),
            pltpu.VMEM((slots, mine), low),
            pltpu.VMEM((slots, mine), low),
            pltpu.VMEM((3 * NB, mine), low),
            pltpu.VMEM((3 * NB, mine), low),
        ],
        compiler_params=pltpu.CompilerParams(vmem_limit_bytes=VMEM_LIMIT),
        name="attention_backward",
    )(grad, tokens, w_query, w_key, w_value, w_output, rel, corner_col, q, k, v, krel, qrel, attend, ctx)


MESH = pl.DeviceIdType.MESH


class Line:
    def __init__(self, axis, own, inner, outer, sems):
        self.axis, self.own, self.inner, self.outer = axis, own, inner, outer
        self.in_send, self.in_recv, self.out_send, self.out_recv = sems
        self.n = lax.axis_size(axis)
        me = lax.axis_index(axis)
        left = me < self.n // 2
        self.depth = jnp.where(left, me, self.n - 1 - me)
        self.inward = jnp.where(left, me + 1, me - 1)
        self.outward = jnp.where(self.depth == 0, self.inward, jnp.where(left, me - 1, me + 1))
        self.last = self.n // 2 - 1

    def greet(self, barrier):
        pl.semaphore_signal(barrier, inc=1, device_id={self.axis: self.inward}, device_id_type=MESH)

        @pl.when(self.depth > 0)
        def _():
            pl.semaphore_signal(
                barrier, inc=1, device_id={self.axis: self.outward}, device_id_type=MESH
            )

    def greeted(self):
        return jnp.where(self.depth > 0, 2, 1)

    def copy(self, source, target, send, recv, to):
        return pltpu.make_async_remote_copy(
            src_ref=source,
            dst_ref=target,
            send_sem=send,
            recv_sem=recv,
            device_id={self.axis: to},
            device_id_type=MESH,
        )

    def send_in(self, u, source):
        @pl.when(self.depth < self.last)
        def _():
            self.copy(
                source, self.inner.at[u], self.in_send.at[u], self.in_recv.at[u], self.inward
            ).start()

        @pl.when(self.depth == self.last)
        def _():
            self.copy(
                source, self.outer.at[u], self.in_send.at[u], self.out_recv.at[u], self.inward
            ).start()

    def step(self, slot, count):
        here = slot - self.depth

        @pl.when((here >= 0) & (here < count))
        def _():
            u = here

            @pl.when(self.depth == 0)
            def _():
                self.send_in(u, self.own.at[u])

            @pl.when(self.depth > 0)
            def _():
                self.copy(
                    self.own.at[u], self.inner.at[u], self.in_send.at[u], self.in_recv.at[u], self.inward
                ).wait_recv()
                self.inner[u] += self.own[u]
                self.send_in(u, self.inner.at[u])

        back = slot - (self.n - 1 - self.depth)

        @pl.when((back >= 0) & (back < count))
        def _():
            u = back
            self.copy(
                self.own.at[u], self.outer.at[u], self.out_send.at[u], self.out_recv.at[u], self.outward
            ).wait_recv()

            @pl.when(self.depth == self.last)
            def _():
                self.outer[u] += self.inner[u] if self.last > 0 else self.own[u]

            @pl.when(self.depth > 0)
            def _():
                self.copy(
                    self.outer.at[u],
                    self.outer.at[u],
                    self.out_send.at[u],
                    self.out_recv.at[u],
                    self.outward,
                ).start()

    def drain(self, count):
        @pl.loop(0, count)
        def _(u):
            self.copy(
                self.own.at[u], self.inner.at[u], self.in_send.at[u], self.in_recv.at[u], self.inward
            ).wait_send()

            @pl.when(self.depth > 0)
            def _():
                self.copy(
                    self.outer.at[u],
                    self.outer.at[u],
                    self.out_send.at[u],
                    self.out_recv.at[u],
                    self.outward,
                ).wait_send()


def centre(values):
    average = jnp.mean(values, axis=-1, keepdims=True)
    centered = values - average
    spread = jnp.mean(centered * centered, axis=-1, keepdims=True)
    scaling = lax.rsqrt(spread + 1e-05)
    return centered * scaling, scaling


def norm_inward(scaled, normed, scaling):
    return scaling * (
        scaled
        - jnp.mean(scaled, axis=-1, keepdims=True)
        - normed * jnp.mean(scaled * normed, axis=-1, keepdims=True)
    )


def fold_rows(values):
    rows, width = values.shape
    return jnp.sum(values.reshape(rows // 8, 8, width), axis=0)


CHUNK = 64


def middle_kernel(
    ctx_ref, wo_ref, tok_ref, cot_ref, wi_ref, wu_ref,
    bo_ref, ga_ref, sa_ref, bi_ref, bu_ref, gf_ref, sf_ref,
    out_ref, grad_ref, grad_low_ref, hidden_ref, active_ref, mid_low_ref, inner_low_ref, small_ref,
    own, inner, outer, normed_ref, scale_ref, pre_ref, mid_ref, sums_ref,
    in_send, in_recv, out_send, out_recv,
):
    slots = tok_ref.shape[0]
    chunks = slots // CHUNK
    low, full = jnp.bfloat16, jnp.float32
    line = Line("head", own, inner, outer, (in_send, in_recv, out_send, out_recv))
    barrier = pltpu.get_barrier_semaphore()
    line.greet(barrier)
    sums_ref[...] = jnp.zeros_like(sums_ref)
    pl.semaphore_wait(barrier, line.greeted())
    root = 0.5**0.5
    bell = (0.5 / jnp.pi) ** 0.5

    def rows(c):
        return pl.ds(pl.multiple_of(c * CHUNK, CHUNK), CHUNK)

    def project(c):
        own[c] = dot_nn(ctx_ref[rows(c), :], wo_ref[...])

    def after_attention(c, u):
        at = rows(c)
        normed, scaling = centre(outer[u] + bo_ref[...] + tok_ref[at, :].astype(full))
        normed_ref[at, :] = normed
        scale_ref[at, :] = scaling
        hidden_low = (normed * ga_ref[...] + sa_ref[...]).astype(low)
        hidden_ref[at, :] = hidden_low
        pre = dot_nn(hidden_low, wi_ref[...]) + bi_ref[...]
        pre_ref[at, :] = pre
        active = (pre * (1.0 + lax.erf(pre * root)) * 0.5).astype(low)
        active_ref[at, :] = active
        own[u + chunks] = dot_nn(active, wu_ref[...])

    def after_ffn(c, u):
        at = rows(c)
        hidden = normed_ref[at, :] * ga_ref[...] + sa_ref[...]
        normed, scaling = centre(outer[u] + bu_ref[...] + hidden)
        out_ref[at, :] = (normed * gf_ref[...] + sf_ref[...]).astype(low)
        upstream = cot_ref[at, :].astype(full)
        grad_mid = norm_inward(upstream * gf_ref[...], normed, scaling)
        sums_ref[4] += fold_rows(grad_mid)
        sums_ref[5] += fold_rows(upstream * normed)
        sums_ref[6] += fold_rows(upstream)
        mid_ref[at, :] = grad_mid
        mid_low = grad_mid.astype(low)
        mid_low_ref[at, :] = mid_low
        grad_active = dot_nt(mid_low, wu_ref[...])
        pre = pre_ref[at, :]
        slope = (1.0 + lax.erf(pre * root)) * 0.5 + pre * jnp.exp(-0.5 * pre * pre) * bell
        inner_low = (grad_active * slope).astype(low)
        sums_ref[3] += fold_rows(inner_low.astype(full))
        inner_low_ref[at, :] = inner_low
        own[u + chunks] = dot_nt(inner_low, wi_ref[...])

    def after_hidden(c, u):
        at = rows(c)
        upstream = outer[u] + mid_ref[at, :]
        normed = normed_ref[at, :]
        grad_attn = norm_inward(upstream * ga_ref[...], normed, scale_ref[at, :])
        sums_ref[0] += fold_rows(grad_attn)
        sums_ref[1] += fold_rows(upstream * normed)
        sums_ref[2] += fold_rows(upstream)
        grad_ref[at, :] = grad_attn
        grad_low_ref[at, :] = grad_attn.astype(low)

    @pl.loop(0, 3 * chunks + line.n - 1)
    def _(slot):
        @pl.when(slot < chunks)
        def _():
            project(slot)

        line.step(slot, 3 * chunks)
        done = slot - (line.n - 1)

        @pl.when((done >= 0) & (done < chunks))
        def _():
            after_attention(done, done)

        @pl.when((done >= chunks) & (done < 2 * chunks))
        def _():
            after_ffn(done - chunks, done)

        @pl.when(done >= 2 * chunks)
        def _():
            after_hidden(done - 2 * chunks, done)

    for at in range(7):
        small_ref[at : at + 1, :] = jnp.sum(sums_ref[at], axis=0, keepdims=True)
    small_ref[7:8, :] = jnp.zeros_like(small_ref[7:8, :])
    line.drain(3 * chunks)


def middle(ctx, w_output, tokens, cotangent, w_inner, w_outer, vectors):
    slots, width = tokens.shape
    units = w_inner.shape[1]
    assert units == width
    low, full = jnp.bfloat16, jnp.float32
    vmem = pl.BlockSpec(memory_space=pltpu.VMEM)
    steps = 3 * (slots // CHUNK)
    return pl.pallas_call(
        middle_kernel,
        out_shape=(
            jax.ShapeDtypeStruct((slots, width), low),
            jax.ShapeDtypeStruct((slots, width), full),
            jax.ShapeDtypeStruct((slots, width), low),
            jax.ShapeDtypeStruct((slots, width), low),
            jax.ShapeDtypeStruct((slots, units), low),
            jax.ShapeDtypeStruct((slots, width), low),
            jax.ShapeDtypeStruct((slots, units), low),
            jax.ShapeDtypeStruct((8, width), full),
        ),
        in_specs=[vmem] * 13,
        out_specs=(vmem,) * 8,
        scratch_shapes=[
            pltpu.VMEM((steps, CHUNK, width), full),
            pltpu.VMEM((steps, CHUNK, width), full),
            pltpu.VMEM((steps, CHUNK, width), full),
            pltpu.VMEM((slots, width), full),
            pltpu.VMEM((slots, 1), full),
            pltpu.VMEM((slots, units), full),
            pltpu.VMEM((slots, width), full),
            pltpu.VMEM((7, 8, width), full),
        ]
        + [pltpu.SemaphoreType.DMA((steps,))] * 4,
        compiler_params=pltpu.CompilerParams(
            vmem_limit_bytes=VMEM_LIMIT, collective_id=1, has_side_effects=True
        ),
        name="middle",
    )(ctx, w_output, tokens, cotangent, w_inner, w_outer, *[v.reshape(1, -1) for v in vectors])


class Halving:
    def __init__(self, order, source, got, out, send, recv):
        self.order, self.source, self.got, self.out = order, source, got, out
        self.send, self.recv = send, recv
        self.b = lax.axis_index("batch")

    def part(self, stage, flip):
        bit = self.order[stage]
        rest = sorted(self.order[stage:], reverse=True)
        mine = (self.b >> bit) & 1
        pick = 1 - mine if flip else mine
        return tuple(pick if k == bit else slice(None) for k in rest)

    def copy(self, stage):
        source = self.source if stage == 0 else self.got[stage - 1]
        return pltpu.make_async_remote_copy(
            src_ref=source.at[self.part(stage, True)],
            dst_ref=self.got[stage],
            send_sem=self.send.at[stage],
            recv_sem=self.recv.at[stage],
            device_id={"batch": self.b ^ (1 << self.order[stage])},
            device_id_type=MESH,
        )

    def start(self):
        self.copy(0).start()

    def turn(self, stage):
        self.copy(stage).wait_recv()
        kept = self.source if stage == 0 else self.got[stage - 1]
        value = kept[self.part(stage, False)] + self.got[stage][...]
        if stage + 1 < len(self.order):
            self.got[stage][...] = value
            self.copy(stage + 1).start()
        else:
            self.out[...] = value

    def drain(self):
        for stage in range(len(self.order)):
            self.copy(stage).wait_send()


def final_kernel(
    gin_ref, grad_ref, gwq_ref, gwk_ref, gwv_ref, gwo_ref,
    hidden_ref, active_ref, mid_low_ref, inner_low_ref, grel_ref, small_ref,
    gtok_ref, owq_ref, owk_ref, owv_ref, owo_ref, owi_ref, owu_ref, orel_ref, osmall_ref,
    inner, outer, gwi_ref, gwu_ref, rel_own, rel_in, rel_out, rel_all, small_sum, small_got,
    *rest,
    bits, pieces,
):
    got = [rest[at * bits : (at + 1) * bits] for at in range(len(pieces) + 1)]
    (in_send, in_recv, out_send, out_recv, rin_send, rin_recv, rout_send, rout_recv,
     piece_send, piece_recv, back_send, back_recv, small_send, small_recv) = rest[(len(pieces) + 1) * bits :]
    chunks = gin_ref.shape[0]
    low, full = jnp.bfloat16, jnp.float32
    line = Line("head", gin_ref, inner, outer, (in_send, in_recv, out_send, out_recv))
    rel_line = Line("head", rel_own, rel_in, rel_out, (rin_send, rin_recv, rout_send, rout_recv))
    b = lax.axis_index("batch")
    barrier = pltpu.get_barrier_semaphore()
    line.greet(barrier)
    for k in range(bits):
        pl.semaphore_signal(barrier, inc=1, device_id={"batch": b ^ (1 << k)}, device_id_type=MESH)
    pl.semaphore_wait(barrier, line.greeted() + bits)

    orders = (list(range(bits)), [0] + list(range(bits - 1, 0, -1)))
    sources = (gwq_ref, gwk_ref, gwv_ref, gwo_ref, gwi_ref, gwu_ref)
    outs = (owq_ref, owk_ref, owv_ref, owo_ref, owi_ref, owu_ref)
    whole = (slice(None),) * (bits + 1)
    jobs = []
    for at, (which, start, size) in enumerate(pieces):
        lanes = slice(start, start + size)
        jobs.append(
            Halving(
                orders[at % 2],
                sources[which].at[whole + (lanes,)],
                got[at],
                outs[which].at[:, lanes],
                piece_send.at[at],
                piece_recv.at[at],
            )
        )
    rel_job = Halving(
        orders[0], grel_ref, got[-1], rel_own.at[0], piece_send.at[len(pieces)], piece_recv.at[len(pieces)]
    )

    def make(at):
        which, start, size = pieces[at]
        lanes = slice(start, start + size)
        if which == 4:
            value = dot_tn(hidden_ref[...], inner_low_ref[:, lanes])
        elif which == 5:
            value = dot_tn(mid_low_ref[...], active_ref[:, lanes])
        else:
            return
        target = sources[which]
        target[whole + (lanes,)] = value.reshape(target.shape[:-1] + (size,))

    def small_copy(k):
        return pltpu.make_async_remote_copy(
            src_ref=small_sum.at[k],
            dst_ref=small_got.at[k],
            send_sem=small_send.at[k],
            recv_sem=small_recv.at[k],
            device_id={"batch": b ^ (1 << k)},
            device_id_type=MESH,
        )

    def small_turn(k):
        small_copy(k).wait_recv()
        value = small_sum[k] + small_got[k]
        if k + 1 < bits:
            small_sum[k + 1] = value
            small_copy(k + 1).start()
        else:
            osmall_ref[...] = value

    def back_copy(k):
        region = tuple(
            slice(None) if other > k else (b >> other) & 1 for other in range(bits - 1, -1, -1)
        )
        return pltpu.make_async_remote_copy(
            src_ref=rel_all.at[region],
            dst_ref=rel_all.at[region],
            send_sem=back_send.at[k],
            recv_sem=back_recv.at[k],
            device_id={"batch": b ^ (1 << k)},
            device_id_type=MESH,
        )

    def back_turn(k):
        back_copy(k).wait_recv()
        if k > 0:
            back_copy(k - 1).start()

    def rel_step(slot):
        rel_line.step(slot, 1)
        if slot == rel_line.n - 1:
            region = tuple((b >> other) & 1 for other in range(bits - 1, -1, -1))
            rel_all[region] = rel_out[0]
            back_copy(bits - 1).start()

    def tokens_step(done):
        gtok_ref[done] = (outer[done] + grad_ref[done]).astype(low)

    small_sum[0] = small_ref[...]
    small_copy(0).start()
    rel_job.start()
    for at in range(len(pieces)):
        if pieces[at][0] < 4:
            jobs[at].start()

    early = [at for at in range(len(pieces)) if pieces[at][0] < 4]
    late = [at for at in range(len(pieces)) if pieces[at][0] >= 4]
    tasks = {}

    def add(slot, task):
        tasks.setdefault(slot, []).append(task)

    total = chunks + line.n - 1
    for at in late:
        add(0, lambda at=at: (make(at), jobs[at].start()))
    add(1, lambda: rel_job.turn(0))
    add(1, lambda: small_turn(0))
    for at in early:
        add(1, lambda at=at: jobs[at].turn(0))
    for at in late:
        add(2, lambda at=at: jobs[at].turn(0))
    for k in range(1, bits):
        add(1 + k, lambda k=k: rel_job.turn(k))
        add(1 + k, lambda k=k: small_turn(k))
    for step in range(line.n):
        add(1 + bits + step, lambda step=step: rel_step(step))
    for k in range(bits - 1, -1, -1):
        add(1 + bits + line.n + bits - k, lambda k=k: back_turn(k))
    for stage in range(1, bits):
        for place, at in enumerate(early):
            add(1 + 2 * stage + place // 2, lambda at=at, stage=stage: jobs[at].turn(stage))
        for place, at in enumerate(late):
            add(2 + 3 * stage + 2 * (place // 2) , lambda at=at, stage=stage: jobs[at].turn(stage))

    for slot in range(max(total, max(tasks) + 1)):
        if slot < total:
            line.step(jnp.int32(slot), chunks)
            if slot >= line.n - 1:
                tokens_step(slot - (line.n - 1))
        for task in tasks.get(slot, ()):
            task()
    orel_ref[...] = rel_all[...]
    line.drain(chunks)
    rel_line.drain(1)
    for job in jobs:
        job.drain()
    rel_job.drain()
    for k in range(bits):
        small_copy(k).wait_send()
        back_copy(k).wait_send()


def final(gin, grad, gwq, gwk, gwv, gwo, hidden, active, mid_low, inner_low, grel, small, batch):
    slots, width = gin.shape
    mine, units = gwq.shape[1], active.shape[1]
    bits = batch.bit_length() - 1
    assert 1 << bits == batch
    low, full = jnp.bfloat16, jnp.float32
    vmem = pl.BlockSpec(memory_space=pltpu.VMEM)
    chunks = slots // CHUNK
    split = (2,) * bits
    part = width // batch
    rel_part = grel.shape[0] // batch
    piece = 512
    pieces = [(which, 0, mine) for which in range(4)]
    for start in range(0, units, piece):
        pieces += [(4, start, piece), (5, start, piece)]
    shape = jax.ShapeDtypeStruct
    got = []
    for _, _, size in pieces:
        got += [pltpu.VMEM((2,) * (bits - 1 - s) + (part, size), full) for s in range(bits)]
    got += [pltpu.VMEM((2,) * (bits - 1 - s) + (rel_part, width), full) for s in range(bits)]
    dma = pltpu.SemaphoreType.DMA
    by_block = lambda a: a.reshape(split + (a.shape[0] // batch, a.shape[1]))
    by_chunk = lambda a: a.reshape(chunks, CHUNK, width)
    outs = pl.pallas_call(
        functools.partial(final_kernel, bits=bits, pieces=pieces),
        out_shape=(
            shape((chunks, CHUNK, width), low),
            shape((part, mine), full),
            shape((part, mine), full),
            shape((part, mine), full),
            shape((part, mine), full),
            shape((part, units), full),
            shape((part, units), full),
            shape(split + (rel_part, width), full),
            shape((8, width), full),
        ),
        in_specs=[vmem] * 12,
        out_specs=(vmem,) * 9,
        scratch_shapes=[
            pltpu.VMEM((chunks, CHUNK, width), full),
            pltpu.VMEM((chunks, CHUNK, width), full),
            pltpu.VMEM(split + (part, units), full),
            pltpu.VMEM(split + (part, units), full),
            pltpu.VMEM((1, rel_part, width), full),
            pltpu.VMEM((1, rel_part, width), full),
            pltpu.VMEM((1, rel_part, width), full),
            pltpu.VMEM(split + (rel_part, width), full),
            pltpu.VMEM((bits, 8, width), full),
            pltpu.VMEM((bits, 8, width), full),
        ]
        + got
        + [dma((chunks,))] * 4
        + [dma((1,))] * 4
        + [dma((len(pieces) + 1, bits))] * 2
        + [dma((bits,))] * 4,
        compiler_params=pltpu.CompilerParams(
            vmem_limit_bytes=VMEM_LIMIT, collective_id=2, has_side_effects=True
        ),
        name="final",
    )(
        by_chunk(gin), by_chunk(grad), by_block(gwq), by_block(gwk), by_block(gwv), by_block(gwo),
        hidden, active, mid_low, inner_low, by_block(grel), small,
    )
    return (outs[0].reshape(slots, width),) + tuple(outs[1:7]) + (outs[7].reshape(grel.shape), outs[8])


def shards(
    tokens,
    page_lengths,
    corners,
    w_query,
    w_key,
    w_value,
    w_output,
    b_output,
    gain_attn,
    shift_attn,
    w_inner,
    b_inner,
    w_outer,
    b_outer,
    gain_ffn,
    shift_ffn,
    rel_tables,
    cotangent,
):
    slots_page = tokens.shape[0]
    wide = -(-slots_page // LANES) * LANES
    rel_rows = rel_tables.reshape(3 * NB, rel_tables.shape[2])
    corner_col = corners.T
    corner_row = jnp.pad(corners, ((0, 0), (0, wide - slots_page)))
    kept = attention_forward(
        tokens, page_lengths, corner_col, corner_row, w_query, w_key, w_value, rel_rows
    )
    vectors = (b_output, gain_attn, shift_attn, b_inner, b_outer, gain_ffn, shift_ffn)
    output, grad_attn, grad_low, hidden, active, mid_low, inner_low, small = middle(
        kept[6], w_output, tokens, cotangent, w_inner, w_outer, vectors
    )
    grads = attention_backward(
        grad_low, tokens, w_query, w_key, w_value, w_output, rel_rows, corner_col, *kept
    )
    done = final(
        grads[4], grad_attn, *grads[:4], hidden, active, mid_low, inner_low, grads[5], small,
        lax.axis_size("batch"),
    )
    small = done[8]
    return (
        output,
        done[0],
        done[1],
        done[2],
        done[3],
        done[4].T,
        small[0],
        small[1],
        small[2],
        done[5],
        small[3],
        done[6].T,
        small[4],
        small[5],
        small[6],
        done[7].reshape(rel_tables.shape),
    )


def solution(mesh):
    in_specs = (
        P("batch", None),
        P("batch"),
        P(None, "batch"),
        P(None, "head"),
        P(None, "head"),
        P(None, "head"),
        P("head", None),
        P(),
        P(),
        P(),
        P(None, "head"),
        P("head"),
        P("head", None),
        P(),
        P(),
        P(),
        P(),
        P("batch", None),
    )
    out_specs = (
        P("batch", None),
        P("batch", None),
        P("batch", "head"),
        P("batch", "head"),
        P("batch", "head"),
        P("head", "batch"),
        P(),
        P(),
        P(),
        P("batch", "head"),
        P("head"),
        P("head", "batch"),
        P(),
        P(),
        P(),
        P(),
    )
    return jax.shard_map(shards, mesh=mesh, in_specs=in_specs, out_specs=out_specs, check_vma=False)
```

```python
import functools

import jax
import jax.numpy as jnp
from jax import lax
from jax.experimental import pallas as pl
from jax.experimental.pallas import tpu as pltpu
from jax.sharding import PartitionSpec as P

HEAD = 64
NB = 128
BOX_STEP = 8
NEG_FILL = -1000000000.0
LANES = 128
VMEM_LIMIT = 60 * 1024 * 1024


def dot_nn(a, b):
    return lax.dot_general(a, b, (((1,), (0,)), ((), ())), preferred_element_type=jnp.float32)


def dot_nt(a, b):
    return lax.dot_general(a, b, (((1,), (1,)), ((), ())), preferred_element_type=jnp.float32)


def dot_tn(a, b):
    return lax.dot_general(a, b, (((0,), (0,)), ((), ())), preferred_element_type=jnp.float32)


def lane_gather(table, index):
    return jnp.take_along_axis(table, index, axis=1, mode="promise_in_bounds")


def bucket(step):
    return jnp.clip(step, -(NB // 2), NB // 2 - 1) + NB // 2


def attention_setup(tok_ref, wq_ref, wk_ref, wv_ref, rel_ref, col_ref, row_ref,
                    q_ref, k_ref, v_ref, krel_ref, qrel_ref, tq_ref, tk_ref, idx_ref):
    slots = tok_ref.shape[0]
    heads, wide = q_ref.shape[0], q_ref.shape[1]
    low = jnp.bfloat16
    for weight, target in ((wq_ref, q_ref), (wk_ref, k_ref), (wv_ref, v_ref)):
        value = dot_nn(tok_ref[...], weight[...]).astype(low)
        for head in range(heads):
            target[head, :slots, :] = value[:, head * HEAD : (head + 1) * HEAD]
            if wide > slots:
                target[head, slots:, :] = jnp.zeros((wide - slots, HEAD), low)
    for weight, target in ((wk_ref, krel_ref), (wq_ref, qrel_ref)):
        value = dot_nn(rel_ref[...], weight[...]).astype(low)
        for head in range(heads):
            target[head] = value[:, head * HEAD : (head + 1) * HEAD]
    for head in range(heads):
        tq_ref[head] = dot_nt(q_ref[head], krel_ref[head])
        tk_ref[head] = dot_nt(k_ref[head], qrel_ref[head])

    block = 64

    @pl.loop(0, slots // block)
    def _(step):
        at = pl.ds(pl.multiple_of(step * block, block), block)
        for kind in range(2):
            own = jnp.broadcast_to(col_ref[at, kind : kind + 1], (block, LANES))
            for chunk in range(wide // LANES):
                other = row_ref[kind : kind + 1, chunk * LANES : (chunk + 1) * LANES]
                idx_ref[kind, chunk, at, :] = bucket((own - other) >> 3)

    if wide > slots:
        idx_ref[:, :, slots:, :] = jnp.zeros_like(idx_ref[:, :, slots:, :])


def attention_block(big, length, q_ref, k_ref, v_ref, tq_ref, tk_ref, idx_ref, log_ref, attend_ref, ctx_ref):
    heads, wide = q_ref.shape[0], q_ref.shape[1]
    chunks = wide // LANES
    slots = attend_ref.shape[1]
    scale = (7.0 * HEAD) ** (-0.5)
    rows = min(LANES, slots - big * LANES)
    here = slice(big * LANES, (big + 1) * LANES)
    some = slice(big * LANES, big * LANES + rows)
    slant = lax.broadcasted_iota(jnp.int32, (LANES, LANES), 0) - lax.broadcasted_iota(
        jnp.int32, (LANES, LANES), 1
    )

    @pl.loop(0, heads)
    def _(head):
        log_ref[:rows, :] = dot_nt(q_ref[head, some, :], k_ref[head])
        for chunk in range(chunks):
            there = slice(chunk * LANES, (chunk + 1) * LANES)
            away = (big - chunk) * LANES
            toward = log_ref[:rows, there]
            if abs(big - chunk) >= 2:
                lane = NB - 1 if away > 0 else 0
                toward = toward + tq_ref[head, some, lane : lane + 1]
                lane = NB - 1 - lane
                beside = jnp.broadcast_to(tk_ref[head, there, lane : lane + 1], (LANES, LANES))
            else:
                toward = toward + lane_gather(tq_ref[head, some, :NB], bucket(slant + away)[:rows])
                beside = lane_gather(tk_ref[head, there, :NB], bucket(slant - away))
            for kind in range(2):
                lanes = slice((kind + 1) * NB, (kind + 2) * NB)
                toward = toward + lane_gather(tq_ref[head, some, lanes], idx_ref[kind, chunk, some, :])
                beside = beside + lane_gather(tk_ref[head, there, lanes], idx_ref[kind, big, there, :])
            log_ref[:rows, there] = toward + beside.T[:rows]
        block = 32
        for start in range(0, rows, block):
            at = slice(start, start + block)
            j_at = lax.broadcasted_iota(jnp.int32, (block, wide), 1)
            masked = jnp.where(j_at < length, log_ref[at, :], NEG_FILL)
            peak = jnp.max(masked, axis=-1, keepdims=True)
            grown = jnp.exp((masked - peak) * scale)
            total = jnp.sum(grown, axis=-1, keepdims=True)
            attend_ref[head, big * LANES + start : big * LANES + start + block, :] = (
                grown * (1.0 / total)
            ).astype(jnp.bfloat16)
        ctx_ref[head, some, :] = dot_nn(attend_ref[head, some, :], v_ref[head]).astype(jnp.bfloat16)


MESH = pl.DeviceIdType.MESH


class Line:
    def __init__(self, axis, own, inner, outer, sems):
        self.axis, self.own, self.inner, self.outer = axis, own, inner, outer
        self.in_send, self.in_recv, self.out_send, self.out_recv = sems
        self.ring = own.shape[0]
        self.n = lax.axis_size(axis)
        me = lax.axis_index(axis)
        left = me < self.n // 2
        self.depth = jnp.where(left, me, self.n - 1 - me)
        self.inward = jnp.where(left, me + 1, me - 1)
        self.outward = jnp.where(self.depth == 0, self.inward, jnp.where(left, me - 1, me + 1))
        self.last = self.n // 2 - 1

    def greet(self, barrier):
        pl.semaphore_signal(barrier, inc=1, device_id={self.axis: self.inward}, device_id_type=MESH)

        @pl.when(self.depth > 0)
        def _():
            pl.semaphore_signal(
                barrier, inc=1, device_id={self.axis: self.outward}, device_id_type=MESH
            )

    def greeted(self):
        return jnp.where(self.depth > 0, 2, 1)

    def copy(self, source, target, send, recv, to):
        return pltpu.make_async_remote_copy(
            src_ref=source,
            dst_ref=target,
            send_sem=send,
            recv_sem=recv,
            device_id={self.axis: to},
            device_id_type=MESH,
        )

    def out_copy(self, u):
        return self.copy(
            self.outer.at[u], self.outer.at[u], self.out_send.at[u], self.out_recv.at[u], self.outward
        )

    def in_copy(self, c, source):
        return self.copy(
            source, self.inner.at[c], self.in_send.at[c], self.in_recv.at[c], self.inward
        )

    def send_in(self, u, c, source):
        @pl.when(self.depth < self.last)
        def _():
            self.in_copy(c, source).start()

        @pl.when(self.depth == self.last)
        def _():
            self.copy(
                source, self.outer.at[u], self.in_send.at[c], self.out_recv.at[u], self.inward
            ).start()

    def step(self, slot, count):
        here = slot - self.depth

        @pl.when((here >= 0) & (here < count))
        def _():
            u = here
            c = lax.rem(u, self.ring)

            @pl.when(self.depth == 0)
            def _():
                self.send_in(u, c, self.own.at[c])

            @pl.when(self.depth > 0)
            def _():
                self.in_copy(c, self.own.at[c]).wait_recv()
                self.inner[c] += self.own[c]
                self.send_in(u, c, self.inner.at[c])

        back = slot - (self.n - 1 - self.depth)

        @pl.when((back >= 0) & (back < count))
        def _():
            u = back
            c = lax.rem(u, self.ring)
            self.in_copy(c, self.own.at[c]).wait_send()
            self.out_copy(u).wait_recv()

            @pl.when(self.depth == self.last)
            def _():
                self.outer[u] += self.inner[c] if self.last > 0 else self.own[c]

            @pl.when(self.depth > 0)
            def _():
                self.out_copy(u).start()

    def drain(self, count):
        @pl.when(self.depth > 0)
        def _():
            @pl.loop(0, count)
            def _(u):
                self.out_copy(u).wait_send()


def centre(values):
    average = jnp.mean(values, axis=-1, keepdims=True)
    centered = values - average
    spread = jnp.mean(centered * centered, axis=-1, keepdims=True)
    scaling = lax.rsqrt(spread + 1e-05)
    return centered * scaling, scaling


def norm_inward(scaled, normed, scaling):
    return scaling * (
        scaled
        - jnp.mean(scaled, axis=-1, keepdims=True)
        - normed * jnp.mean(scaled * normed, axis=-1, keepdims=True)
    )


def fold_rows(values):
    rows, width = values.shape
    return jnp.sum(values.reshape(rows // 8, 8, width), axis=0)


CHUNK = 64


def layer_kernel(
    length_ref, tok_ref, wq_ref, wk_ref, wv_ref, rel_ref, col_ref, row_ref,
    wo_ref, cot_ref, wi_ref, wu_ref, bo_ref, ga_ref, sa_ref, bi_ref, bu_ref, gf_ref, sf_ref,
    q_ref, k_ref, v_ref, krel_ref, qrel_ref, attend_ref, ctx_ref,
    out_ref, grad_ref, grad_low_ref, hidden_ref, active_ref, mid_low_ref, inner_low_ref, small_ref,
    tq_ref, tk_ref, idx_ref, log_ref,
    own, inner, outer, normed_ref, scale_ref, pre_ref, sums_ref,
    in_send, in_recv, out_send, out_recv,
):
    slots = tok_ref.shape[0]
    chunks = slots // CHUNK
    heads, wide = q_ref.shape[0], q_ref.shape[1]
    low, full = jnp.bfloat16, jnp.float32
    line = Line("head", own, inner, outer, (in_send, in_recv, out_send, out_recv))
    barrier = pltpu.get_barrier_semaphore()
    line.greet(barrier)
    sums_ref[...] = jnp.zeros_like(sums_ref)
    attention_setup(tok_ref, wq_ref, wk_ref, wv_ref, rel_ref, col_ref, row_ref,
                    q_ref, k_ref, v_ref, krel_ref, qrel_ref, tq_ref, tk_ref, idx_ref)
    pl.semaphore_wait(barrier, line.greeted())
    root = 0.5**0.5
    bell = (0.5 / jnp.pi) ** 0.5

    def rows(c):
        return pl.ds(pl.multiple_of(c * CHUNK, CHUNK), CHUNK)

    def project(c):
        context = jnp.concatenate([ctx_ref[head, rows(c), :] for head in range(heads)], axis=1)
        own[c] = dot_nn(context, wo_ref[...])

    def after_attention(c, u):
        at = rows(c)
        normed, scaling = centre(outer[u] + bo_ref[...] + tok_ref[at, :].astype(full))
        normed_ref[at, :] = normed
        scale_ref[at, :] = scaling
        hidden_low = (normed * ga_ref[...] + sa_ref[...]).astype(low)
        hidden_ref[at, :] = hidden_low
        pre = dot_nn(hidden_low, wi_ref[...]) + bi_ref[...]
        pre_ref[at, :] = pre
        active = (pre * (1.0 + lax.erf(pre * root)) * 0.5).astype(low)
        active_ref[at, :] = active
        own[c] = dot_nn(active, wu_ref[...])

    def after_ffn(c, u):
        at = rows(c)
        hidden = normed_ref[at, :] * ga_ref[...] + sa_ref[...]
        normed, scaling = centre(outer[u] + bu_ref[...] + hidden)
        out_ref[at, :] = (normed * gf_ref[...] + sf_ref[...]).astype(low)
        upstream = cot_ref[at, :].astype(full)
        grad_mid = norm_inward(upstream * gf_ref[...], normed, scaling)
        sums_ref[4] += fold_rows(grad_mid)
        sums_ref[5] += fold_rows(upstream * normed)
        sums_ref[6] += fold_rows(upstream)
        grad_ref[c] = grad_mid
        mid_low = grad_mid.astype(low)
        mid_low_ref[at, :] = mid_low
        grad_active = dot_nt(mid_low, wu_ref[...])
        pre = pre_ref[at, :]
        slope = (1.0 + lax.erf(pre * root)) * 0.5 + pre * jnp.exp(-0.5 * pre * pre) * bell
        inner_low = (grad_active * slope).astype(low)
        sums_ref[3] += fold_rows(inner_low.astype(full))
        inner_low_ref[at, :] = inner_low
        own[c] = dot_nt(inner_low, wi_ref[...])

    def after_hidden(c, u):
        at = rows(c)
        upstream = outer[u] + grad_ref[c]
        normed = normed_ref[at, :]
        grad_attn = norm_inward(upstream * ga_ref[...], normed, scale_ref[at, :])
        sums_ref[0] += fold_rows(grad_attn)
        sums_ref[1] += fold_rows(upstream * normed)
        sums_ref[2] += fold_rows(upstream)
        grad_ref[c] = grad_attn
        grad_low_ref[at, :] = grad_attn.astype(low)

    per = LANES // CHUNK

    @pl.loop(0, 3 * chunks + line.n - 1)
    def _(slot):
        for big in range(wide // LANES):

            @pl.when(slot == big * per)
            def _(big=big):
                attention_block(big, length_ref[0], q_ref, k_ref, v_ref, tq_ref, tk_ref, idx_ref, log_ref,
                                attend_ref, ctx_ref)

        @pl.when(slot < chunks)
        def _():
            project(slot)

        line.step(slot, 3 * chunks)
        done = slot - (line.n - 1)

        @pl.when((done >= 0) & (done < chunks))
        def _():
            after_attention(done, done)

        @pl.when((done >= chunks) & (done < 2 * chunks))
        def _():
            after_ffn(done - chunks, done)

        @pl.when(done >= 2 * chunks)
        def _():
            after_hidden(done - 2 * chunks, done)

    for at in range(7):
        small_ref[at : at + 1, :] = jnp.sum(sums_ref[at], axis=0, keepdims=True)
    small_ref[7:8, :] = jnp.zeros_like(small_ref[7:8, :])
    line.drain(3 * chunks)


def layer(tokens, length, corner_col, corner_row, w_query, w_key, w_value, rel, w_output, cotangent, w_inner, w_outer, vectors):
    slots, width = tokens.shape
    units = w_inner.shape[1]
    mine = w_query.shape[1]
    heads = mine // HEAD
    wide = corner_row.shape[1]
    assert units == width
    low, full = jnp.bfloat16, jnp.float32
    vmem = pl.BlockSpec(memory_space=pltpu.VMEM)
    chunks = slots // CHUNK
    steps = 3 * chunks
    shape = jax.ShapeDtypeStruct
    dma = pltpu.SemaphoreType.DMA
    return pl.pallas_call(
        layer_kernel,
        out_shape=(
            shape((heads, wide, HEAD), low),
            shape((heads, wide, HEAD), low),
            shape((heads, wide, HEAD), low),
            shape((heads, 3 * NB, HEAD), low),
            shape((heads, 3 * NB, HEAD), low),
            shape((heads, slots, wide), low),
            shape((heads, slots, HEAD), low),
            shape((slots, width), low),
            shape((chunks, CHUNK, width), full),
            shape((slots, width), low),
            shape((slots, width), low),
            shape((slots, units), low),
            shape((slots, width), low),
            shape((slots, units), low),
            shape((8, width), full),
        ),
        in_specs=[pl.BlockSpec(memory_space=pltpu.SMEM)] + [vmem] * 18,
        out_specs=(vmem,) * 15,
        scratch_shapes=[
            pltpu.VMEM((heads, wide, 3 * NB), full),
            pltpu.VMEM((heads, wide, 3 * NB), full),
            pltpu.VMEM((2, wide // LANES, wide, LANES), jnp.int32),
            pltpu.VMEM((LANES, wide), full),
            pltpu.VMEM((chunks, CHUNK, width), full),
            pltpu.VMEM((chunks, CHUNK, width), full),
            pltpu.VMEM((steps, CHUNK, width), full),
            pltpu.VMEM((slots, width), full),
            pltpu.VMEM((slots, 1), full),
            pltpu.VMEM((slots, units), full),
            pltpu.VMEM((7, 8, width), full),
            dma((chunks,)),
            dma((chunks,)),
            dma((steps,)),
            dma((steps,)),
        ],
        compiler_params=pltpu.CompilerParams(
            vmem_limit_bytes=VMEM_LIMIT, collective_id=1, has_side_effects=True
        ),
        name="layer",
    )(length, tokens, w_query, w_key, w_value, rel, corner_col, corner_row,
      w_output, cotangent, w_inner, w_outer, *[v.reshape(1, -1) for v in vectors])


def attention_backward_kernel(
    grad_ref, tok_ref, wq_ref, wk_ref, wv_ref, wo_ref, rel_ref, col_ref,
    q_ref, k_ref, v_ref, krel_ref, qrel_ref, attend_ref, ctx_ref,
    gwq_ref, gwk_ref, gwv_ref, gwo_ref, gin_ref, grel_ref,
    gc_ref, step_ref, mat_ref, fold_ref, hist_ref, gq_ref, gk_ref, gv_ref,
    gkrel_ref, gqrel_ref,
):
    slots = tok_ref.shape[0]
    wide = mat_ref.shape[1]
    heads = wq_ref.shape[1] // HEAD
    chunks = wide // LANES
    scale = (7.0 * HEAD) ** (-0.5)
    low = jnp.bfloat16
    block = 32
    gc_ref[...] = dot_nt(grad_ref[...], wo_ref[...]).astype(low)
    gwo_ref[...] = dot_tn(
        grad_ref[...], jnp.concatenate([ctx_ref[head] for head in range(heads)], axis=1)
    )
    mat_ref[...] = jnp.zeros_like(mat_ref)
    step_ref[...] = jnp.zeros_like(step_ref)

    @pl.loop(0, slots // block)
    def _(step):
        at = pl.ds(pl.multiple_of(step * block, block), block)
        quotient = lax.broadcasted_iota(jnp.int32, (block, NB), 1) * BOX_STEP
        for kind in range(2):
            own = col_ref[at, kind : kind + 1]
            for rest in range(BOX_STEP):
                lanes = slice(rest * NB, (rest + 1) * NB)
                step_ref[kind, at, lanes] = (own <= quotient + rest).astype(jnp.float32).astype(low)

    for head in range(heads):
        cols = slice(head * HEAD, (head + 1) * HEAD)
        gc_h = gc_ref[:, cols]
        grad_attend = dot_nt(gc_h, v_ref[head])
        mean = jnp.sum(gc_h.astype(jnp.float32) * ctx_ref[head].astype(jnp.float32), axis=-1, keepdims=True)
        mat_ref[0, :slots, :] = (attend_ref[head].astype(jnp.float32) * (grad_attend - mean)).astype(low)
        gv_ref[:, cols] = dot_tn(attend_ref[head], gc_h)[:slots].astype(low)
        for big in range(chunks):
            for chunk in range(chunks):
                here = slice(big * LANES, (big + 1) * LANES)
                there = slice(chunk * LANES, (chunk + 1) * LANES)
                mat_ref[1, there, here] = mat_ref[0, here, there].T

        for side in range(2):
            for kind in range(2):
                fold_ref[kind] = dot_nn(mat_ref[side, :slots, :], step_ref[kind])

            for big in range(chunks):
                rows_here = min(LANES, slots - big * LANES)

                @pl.loop(0, rows_here // block)
                def _(step, big=big, side=side):
                    local = step * block
                    at = pl.ds(pl.multiple_of(big * LANES + local, block), block)
                    lane = lax.broadcasted_iota(jnp.int32, (block, NB), 1)
                    row = lax.broadcasted_iota(jnp.int32, (block, NB), 0) + local
                    part = [
                        mat_ref[side, at, c * LANES : (c + 1) * LANES].astype(jnp.float32)
                        for c in range(chunks)
                    ]
                    zero = jnp.zeros((block, LANES), jnp.float32)
                    before = part[big - 1] if big >= 1 else zero
                    after = part[big + 1] if big + 1 < chunks else zero
                    mid = part[big]
                    delta = lane - row
                    window = jnp.where(
                        delta > NB // 2, before, jnp.where(delta < 1 - NB // 2, after, mid)
                    )
                    spread = lane_gather(window, (row + NB // 2 - lane) & (NB - 1))
                    under = jnp.where(delta <= NB // 2 + 1, before, 0.0) + jnp.where(
                        delta <= 1 - NB // 2, mid, 0.0
                    )
                    over = jnp.where(delta >= NB // 2, mid, 0.0) + jnp.where(
                        delta >= -(NB // 2), after, 0.0
                    )
                    for c in range(big - 1):
                        under = under + part[c]
                    for c in range(big + 2, chunks):
                        over = over + part[c]
                    under = jnp.sum(under, axis=-1, keepdims=True)
                    over = jnp.sum(over, axis=-1, keepdims=True)
                    spread = jnp.where(lane == 0, over, jnp.where(lane == NB - 1, under, spread))
                    hist_ref[side, at, 0:NB] = spread.astype(low)
                    for kind in range(2):
                        own = col_ref[at, kind : kind + 1]
                        rest = jnp.broadcast_to(own & (BOX_STEP - 1), (block, NB))
                        whole = jnp.broadcast_to(own >> 3, (block, NB))
                        groups = [
                            fold_ref[kind, at, r * NB : (r + 1) * NB] for r in range(BOX_STEP)
                        ]
                        every = groups[-1][:, NB - 1 : NB]
                        for bit in range(3):
                            odd = (rest & (1 << bit)) != 0
                            groups = [
                                jnp.where(odd, groups[g + 1], groups[g])
                                for g in range(0, len(groups), 2)
                            ]
                        index = whole + NB // 2 - lane
                        found = lane_gather(groups[0], index & (NB - 1))
                        found = jnp.where(index < 0, 0.0, found)
                        found = jnp.where((index >= NB) | (lane == 0), every, found)
                        following = pltpu.roll(found, NB - 1, 1)
                        found = found - jnp.where(lane == NB - 1, 0.0, following)
                        hist_ref[side, at, (kind + 1) * NB : (kind + 2) * NB] = found.astype(low)

        q_h, k_h = q_ref[head, :slots, :], k_ref[head, :slots, :]
        gq = dot_nn(mat_ref[0, :slots, :], k_ref[head]) + dot_nn(hist_ref[0], krel_ref[head])
        gk = dot_nn(mat_ref[1, :slots, :slots], q_h) + dot_nn(hist_ref[1], qrel_ref[head])
        gq_ref[:, cols] = (gq * scale).astype(low)
        gk_ref[:, cols] = (gk * scale).astype(low)
        gkrel_ref[:, cols] = (dot_tn(hist_ref[0], q_h) * scale).astype(low)
        gqrel_ref[:, cols] = (dot_tn(hist_ref[1], k_h) * scale).astype(low)

    tok, rel = tok_ref[...], rel_ref[...]
    gwq_ref[...] = dot_tn(tok, gq_ref[...]) + dot_tn(rel, gqrel_ref[...])
    gwk_ref[...] = dot_tn(tok, gk_ref[...]) + dot_tn(rel, gkrel_ref[...])
    gwv_ref[...] = dot_tn(tok, gv_ref[...])
    gin_ref[...] = (
        dot_nt(gq_ref[...], wq_ref[...])
        + dot_nt(gk_ref[...], wk_ref[...])
        + dot_nt(gv_ref[...], wv_ref[...])
    )
    grel_ref[...] = dot_nt(gkrel_ref[...], wk_ref[...]) + dot_nt(gqrel_ref[...], wq_ref[...])


def attention_backward(
    grad, tokens, w_query, w_key, w_value, w_output, rel, corner_col, q, k, v, krel, qrel, attend, ctx
):
    slots, width = tokens.shape
    mine = w_query.shape[1]
    wide = attend.shape[2]
    low, full = jnp.bfloat16, jnp.float32
    vmem = pl.BlockSpec(memory_space=pltpu.VMEM)
    return pl.pallas_call(
        attention_backward_kernel,
        out_shape=(
            jax.ShapeDtypeStruct((width, mine), full),
            jax.ShapeDtypeStruct((width, mine), full),
            jax.ShapeDtypeStruct((width, mine), full),
            jax.ShapeDtypeStruct((width, mine), full),
            jax.ShapeDtypeStruct((slots, width), full),
            jax.ShapeDtypeStruct((3 * NB, width), full),
        ),
        in_specs=[vmem] * 15,
        out_specs=(vmem,) * 6,
        scratch_shapes=[
            pltpu.VMEM((slots, mine), low),
            pltpu.VMEM((2, wide, BOX_STEP * NB), low),
            pltpu.VMEM((2, wide, wide), low),
            pltpu.VMEM((2, slots, BOX_STEP * NB), full),
            pltpu.VMEM((2, slots, 3 * NB), low),
            pltpu.VMEM((slots, mine), low),
            pltpu.VMEM((slots, mine), low),
            pltpu.VMEM((slots, mine), low),
            pltpu.VMEM((3 * NB, mine), low),
            pltpu.VMEM((3 * NB, mine), low),
        ],
        compiler_params=pltpu.CompilerParams(vmem_limit_bytes=VMEM_LIMIT),
        name="attention_backward",
    )(grad, tokens, w_query, w_key, w_value, w_output, rel, corner_col, q, k, v, krel, qrel, attend, ctx)


class Halving:
    def __init__(self, order, source, got, out, send, recv):
        self.order, self.source, self.got, self.out = order, source, got, out
        self.send, self.recv = send, recv
        self.b = lax.axis_index("batch")

    def part(self, stage, flip):
        bit = self.order[stage]
        rest = sorted(self.order[stage:], reverse=True)
        mine = (self.b >> bit) & 1
        pick = 1 - mine if flip else mine
        return tuple(pick if k == bit else slice(None) for k in rest)

    def copy(self, stage):
        source = self.source if stage == 0 else self.got[stage - 1]
        return pltpu.make_async_remote_copy(
            src_ref=source.at[self.part(stage, True)],
            dst_ref=self.got[stage],
            send_sem=self.send.at[stage],
            recv_sem=self.recv.at[stage],
            device_id={"batch": self.b ^ (1 << self.order[stage])},
            device_id_type=MESH,
        )

    def start(self):
        self.copy(0).start()

    def turn(self, stage):
        self.copy(stage).wait_recv()
        kept = self.source if stage == 0 else self.got[stage - 1]
        value = kept[self.part(stage, False)] + self.got[stage][...]
        if stage + 1 < len(self.order):
            self.got[stage][...] = value
            self.copy(stage + 1).start()
        else:
            self.out[...] = value

    def drain(self):
        for stage in range(len(self.order)):
            self.copy(stage).wait_send()


def final_kernel(
    gin_ref, grad_ref, gwq_ref, gwk_ref, gwv_ref, gwo_ref,
    hidden_ref, active_ref, mid_low_ref, inner_low_ref, grel_ref, small_ref,
    gtok_ref, owq_ref, owk_ref, owv_ref, owo_ref, owi_ref, owu_ref, orel_ref, osmall_ref,
    inner, outer, gwi_ref, gwu_ref, rel_own, rel_in, rel_out, rel_all, small_sum, small_got,
    *rest,
    bits, pieces,
):
    got = [rest[at * bits : (at + 1) * bits] for at in range(len(pieces) + 1)]
    (in_send, in_recv, out_send, out_recv, rin_send, rin_recv, rout_send, rout_recv,
     piece_send, piece_recv, back_send, back_recv, small_send, small_recv) = rest[(len(pieces) + 1) * bits :]
    chunks = gin_ref.shape[0]
    low, full = jnp.bfloat16, jnp.float32
    line = Line("head", gin_ref, inner, outer, (in_send, in_recv, out_send, out_recv))
    rel_line = Line("head", rel_own, rel_in, rel_out, (rin_send, rin_recv, rout_send, rout_recv))
    b = lax.axis_index("batch")
    barrier = pltpu.get_barrier_semaphore()
    line.greet(barrier)
    for k in range(bits):
        pl.semaphore_signal(barrier, inc=1, device_id={"batch": b ^ (1 << k)}, device_id_type=MESH)
    pl.semaphore_wait(barrier, line.greeted() + bits)

    orders = (list(range(bits)), [0] + list(range(bits - 1, 0, -1)))
    sources = (gwq_ref, gwk_ref, gwv_ref, gwo_ref, gwi_ref, gwu_ref)
    outs = (owq_ref, owk_ref, owv_ref, owo_ref, owi_ref, owu_ref)
    whole = (slice(None),) * (bits + 1)
    jobs = []
    for at, (which, start, size) in enumerate(pieces):
        lanes = slice(start, start + size)
        jobs.append(
            Halving(
                orders[at % 2],
                sources[which].at[whole + (lanes,)],
                got[at],
                outs[which].at[:, lanes],
                piece_send.at[at],
                piece_recv.at[at],
            )
        )
    rel_job = Halving(
        orders[0], grel_ref, got[-1], rel_own.at[0], piece_send.at[len(pieces)], piece_recv.at[len(pieces)]
    )

    def make(at):
        which, start, size = pieces[at]
        lanes = slice(start, start + size)
        if which == 4:
            value = dot_tn(hidden_ref[...], inner_low_ref[:, lanes])
        elif which == 5:
            value = dot_tn(mid_low_ref[...], active_ref[:, lanes])
        else:
            return
        target = sources[which]
        target[whole + (lanes,)] = value.reshape(target.shape[:-1] + (size,))

    def small_copy(k):
        return pltpu.make_async_remote_copy(
            src_ref=small_sum.at[k],
            dst_ref=small_got.at[k],
            send_sem=small_send.at[k],
            recv_sem=small_recv.at[k],
            device_id={"batch": b ^ (1 << k)},
            device_id_type=MESH,
        )

    def small_turn(k):
        small_copy(k).wait_recv()
        value = small_sum[k] + small_got[k]
        if k + 1 < bits:
            small_sum[k + 1] = value
            small_copy(k + 1).start()
        else:
            osmall_ref[...] = value

    def back_copy(k):
        region = tuple(
            slice(None) if other > k else (b >> other) & 1 for other in range(bits - 1, -1, -1)
        )
        return pltpu.make_async_remote_copy(
            src_ref=rel_all.at[region],
            dst_ref=rel_all.at[region],
            send_sem=back_send.at[k],
            recv_sem=back_recv.at[k],
            device_id={"batch": b ^ (1 << k)},
            device_id_type=MESH,
        )

    def back_turn(k):
        back_copy(k).wait_recv()
        if k > 0:
            back_copy(k - 1).start()

    def rel_step(slot):
        rel_line.step(slot, 1)
        if slot == rel_line.n - 1:
            region = tuple((b >> other) & 1 for other in range(bits - 1, -1, -1))
            rel_all[region] = rel_out[0]
            back_copy(bits - 1).start()

    def tokens_step(done):
        gtok_ref[done] = (outer[done] + grad_ref[done]).astype(low)

    small_sum[0] = small_ref[...]
    small_copy(0).start()
    rel_job.start()
    for at in range(len(pieces)):
        if pieces[at][0] < 4:
            jobs[at].start()

    early = [at for at in range(len(pieces)) if pieces[at][0] < 4]
    late = [at for at in range(len(pieces)) if pieces[at][0] >= 4]
    tasks = {}

    def add(slot, task):
        tasks.setdefault(slot, []).append(task)

    total = chunks + line.n - 1
    for at in late:
        add(0, lambda at=at: (make(at), jobs[at].start()))
    add(1, lambda: rel_job.turn(0))
    add(1, lambda: small_turn(0))
    for at in early:
        add(1, lambda at=at: jobs[at].turn(0))
    for at in late:
        add(2, lambda at=at: jobs[at].turn(0))
    for k in range(1, bits):
        add(1 + k, lambda k=k: rel_job.turn(k))
        add(1 + k, lambda k=k: small_turn(k))
    for step in range(line.n):
        add(1 + bits + step, lambda step=step: rel_step(step))
    for k in range(bits - 1, -1, -1):
        add(1 + bits + line.n + bits - k, lambda k=k: back_turn(k))
    for stage in range(1, bits):
        for place, at in enumerate(early):
            add(1 + 2 * stage + place // 2, lambda at=at, stage=stage: jobs[at].turn(stage))
        for place, at in enumerate(late):
            add(2 + 3 * stage + 2 * (place // 2) , lambda at=at, stage=stage: jobs[at].turn(stage))

    for slot in range(max(total, max(tasks) + 1)):
        if slot < total:
            line.step(jnp.int32(slot), chunks)
            if slot >= line.n - 1:
                tokens_step(slot - (line.n - 1))
        for task in tasks.get(slot, ()):
            task()
    orel_ref[...] = rel_all[...]
    line.drain(chunks)
    rel_line.drain(1)
    for job in jobs:
        job.drain()
    rel_job.drain()
    for k in range(bits):
        small_copy(k).wait_send()
        back_copy(k).wait_send()


def final(gin, grad, gwq, gwk, gwv, gwo, hidden, active, mid_low, inner_low, grel, small, batch):
    slots, width = gin.shape
    mine, units = gwq.shape[1], active.shape[1]
    bits = batch.bit_length() - 1
    assert 1 << bits == batch
    low, full = jnp.bfloat16, jnp.float32
    vmem = pl.BlockSpec(memory_space=pltpu.VMEM)
    chunks = slots // CHUNK
    split = (2,) * bits
    part = width // batch
    rel_part = grel.shape[0] // batch
    piece = 512
    pieces = [(which, 0, mine) for which in range(4)]
    for start in range(0, units, piece):
        pieces += [(4, start, piece), (5, start, piece)]
    shape = jax.ShapeDtypeStruct
    got = []
    for _, _, size in pieces:
        got += [pltpu.VMEM((2,) * (bits - 1 - s) + (part, size), full) for s in range(bits)]
    got += [pltpu.VMEM((2,) * (bits - 1 - s) + (rel_part, width), full) for s in range(bits)]
    dma = pltpu.SemaphoreType.DMA
    by_block = lambda a: a.reshape(split + (a.shape[0] // batch, a.shape[1]))
    by_chunk = lambda a: a.reshape(chunks, CHUNK, width)
    outs = pl.pallas_call(
        functools.partial(final_kernel, bits=bits, pieces=pieces),
        out_shape=(
            shape((chunks, CHUNK, width), low),
            shape((part, mine), full),
            shape((part, mine), full),
            shape((part, mine), full),
            shape((part, mine), full),
            shape((part, units), full),
            shape((part, units), full),
            shape(split + (rel_part, width), full),
            shape((8, width), full),
        ),
        in_specs=[vmem] * 12,
        out_specs=(vmem,) * 9,
        scratch_shapes=[
            pltpu.VMEM((chunks, CHUNK, width), full),
            pltpu.VMEM((chunks, CHUNK, width), full),
            pltpu.VMEM(split + (part, units), full),
            pltpu.VMEM(split + (part, units), full),
            pltpu.VMEM((1, rel_part, width), full),
            pltpu.VMEM((1, rel_part, width), full),
            pltpu.VMEM((1, rel_part, width), full),
            pltpu.VMEM(split + (rel_part, width), full),
            pltpu.VMEM((bits, 8, width), full),
            pltpu.VMEM((bits, 8, width), full),
        ]
        + got
        + [dma((chunks,))] * 4
        + [dma((1,))] * 4
        + [dma((len(pieces) + 1, bits))] * 2
        + [dma((bits,))] * 4,
        compiler_params=pltpu.CompilerParams(
            vmem_limit_bytes=VMEM_LIMIT, collective_id=2, has_side_effects=True
        ),
        name="final",
    )(
        by_chunk(gin), by_chunk(grad), by_block(gwq), by_block(gwk), by_block(gwv), by_block(gwo),
        hidden, active, mid_low, inner_low, by_block(grel), small,
    )
    return (outs[0].reshape(slots, width),) + tuple(outs[1:7]) + (outs[7].reshape(grel.shape), outs[8])


def shards(
    tokens,
    page_lengths,
    corners,
    w_query,
    w_key,
    w_value,
    w_output,
    b_output,
    gain_attn,
    shift_attn,
    w_inner,
    b_inner,
    w_outer,
    b_outer,
    gain_ffn,
    shift_ffn,
    rel_tables,
    cotangent,
):
    slots_page = tokens.shape[0]
    wide = -(-slots_page // LANES) * LANES
    rel_rows = rel_tables.reshape(3 * NB, rel_tables.shape[2])
    corner_col = corners.T
    corner_row = jnp.pad(corners, ((0, 0), (0, wide - slots_page)))
    vectors = (b_output, gain_attn, shift_attn, b_inner, b_outer, gain_ffn, shift_ffn)
    kept = layer(
        tokens, page_lengths, corner_col, corner_row, w_query, w_key, w_value, rel_rows,
        w_output, cotangent, w_inner, w_outer, vectors,
    )
    output, grad_attn, grad_low, hidden, active, mid_low, inner_low, small = kept[7:]
    kept = kept[:7]
    grads = attention_backward(
        grad_low, tokens, w_query, w_key, w_value, w_output, rel_rows, corner_col, *kept
    )
    done = final(
        grads[4], grad_attn, *grads[:4], hidden, active, mid_low, inner_low, grads[5], small,
        lax.axis_size("batch"),
    )
    small = done[8]
    return (
        output,
        done[0],
        done[1],
        done[2],
        done[3],
        done[4].T,
        small[0],
        small[1],
        small[2],
        done[5],
        small[3],
        done[6].T,
        small[4],
        small[5],
        small[6],
        done[7].reshape(rel_tables.shape),
    )


def solution(mesh):
    in_specs = (
        P("batch", None),
        P("batch"),
        P(None, "batch"),
        P(None, "head"),
        P(None, "head"),
        P(None, "head"),
        P("head", None),
        P(),
        P(),
        P(),
        P(None, "head"),
        P("head"),
        P("head", None),
        P(),
        P(),
        P(),
        P(),
        P("batch", None),
    )
    out_specs = (
        P("batch", None),
        P("batch", None),
        P("batch", "head"),
        P("batch", "head"),
        P("batch", "head"),
        P("head", "batch"),
        P(),
        P(),
        P(),
        P("batch", "head"),
        P("head"),
        P("head", "batch"),
        P(),
        P(),
        P(),
        P(),
    )
    return jax.shard_map(shards, mesh=mesh, in_specs=in_specs, out_specs=out_specs, check_vma=False)
```

```python
import functools

import jax
import jax.numpy as jnp
from jax import lax
from jax.experimental import pallas as pl
from jax.experimental.pallas import tpu as pltpu
from jax.sharding import PartitionSpec as P

HEAD = 64
NB = 128
BOX_STEP = 8
NEG_FILL = -1000000000.0
LANES = 128
HOP = 32
PAIR = 64
LAG = 2
PIECE = 256
VMEM_LIMIT = 60 * 1024 * 1024
MESH = pl.DeviceIdType.MESH
LOW = jnp.bfloat16
FULL = jnp.float32


def dot_nn(a, b):
    return lax.dot_general(a, b, (((1,), (0,)), ((), ())), preferred_element_type=FULL)


def dot_nt(a, b):
    return lax.dot_general(a, b, (((1,), (1,)), ((), ())), preferred_element_type=FULL)


def dot_tn(a, b):
    return lax.dot_general(a, b, (((0,), (0,)), ((), ())), preferred_element_type=FULL)


def lane_gather(table, index):
    return jnp.take_along_axis(table, index, axis=1, mode="promise_in_bounds")


def bucket(step):
    return jnp.clip(step, -(NB // 2), NB // 2 - 1) + NB // 2


def span(start, size):
    return pl.ds(pl.multiple_of(start, size), size)


class Line:
    def __init__(self, axis, own, inner, outer, sems, lag=LAG):
        self.axis, self.own, self.inner, self.outer, self.lag = axis, own, inner, outer, lag
        self.in_send, self.in_recv, self.out_send, self.out_recv = sems
        self.ring, self.wide_ring = own.shape[0], outer.shape[0]
        self.n = lax.axis_size(axis)
        me = lax.axis_index(axis)
        left = me < self.n // 2
        self.depth = jnp.where(left, me, self.n - 1 - me)
        self.inward = jnp.where(left, me + 1, me - 1)
        self.outward = jnp.where(self.depth == 0, self.inward, jnp.where(left, me - 1, me + 1))
        self.last = self.n // 2 - 1
        self.trip = self.lag * (self.n - 1)

    def greet(self, barrier):
        pl.semaphore_signal(barrier, inc=1, device_id={self.axis: self.inward}, device_id_type=MESH)

        @pl.when(self.depth > 0)
        def _():
            pl.semaphore_signal(
                barrier, inc=1, device_id={self.axis: self.outward}, device_id_type=MESH
            )

    def greeted(self):
        return jnp.where(self.depth > 0, 2, 1)

    def copy(self, source, target, send, recv, to):
        return pltpu.make_async_remote_copy(
            src_ref=source,
            dst_ref=target,
            send_sem=send,
            recv_sem=recv,
            device_id={self.axis: to},
            device_id_type=MESH,
        )

    def total(self, u):
        return lax.rem(u, self.wide_ring)

    def out_copy(self, u):
        o = self.total(u)
        return self.copy(
            self.outer.at[o], self.outer.at[o], self.out_send.at[o], self.out_recv.at[o], self.outward
        )

    def in_copy(self, c, source):
        return self.copy(
            source, self.inner.at[c], self.in_send.at[c], self.in_recv.at[c], self.inward
        )

    def send_in(self, u, c, source):
        @pl.when(self.depth < self.last)
        def _():
            self.in_copy(c, source).start()

        @pl.when(self.depth == self.last)
        def _():
            o = self.total(u)
            self.copy(
                source, self.outer.at[o], self.in_send.at[c], self.out_recv.at[o], self.inward
            ).start()

    def step(self, slot, count):
        here = slot - self.lag * self.depth

        @pl.when((here >= 0) & (here < count))
        def _():
            u = here
            c = lax.rem(u, self.ring)

            @pl.when(self.depth == 0)
            def _():
                self.send_in(u, c, self.own.at[c])

            @pl.when(self.depth > 0)
            def _():
                @pl.when(u >= self.ring)
                def _():
                    self.out_copy(u - self.ring).wait_send()

                self.in_copy(c, self.own.at[c]).wait_recv()
                self.inner[c] += self.own[c]
                self.send_in(u, c, self.inner.at[c])

        back = slot - self.lag * (self.n - 1 - self.depth)

        @pl.when((back >= 0) & (back < count))
        def _():
            u = back
            c = lax.rem(u, self.ring)
            self.in_copy(c, self.own.at[c]).wait_send()
            self.out_copy(u).wait_recv()

            @pl.when(self.depth == self.last)
            def _():
                self.outer[self.total(u)] += self.inner[c] if self.last > 0 else self.own[c]

            @pl.when(self.depth > 0)
            def _():
                self.out_copy(u).start()

    def drain(self, count):
        @pl.when(self.depth > 0)
        def _():
            @pl.loop(count - self.ring, count)
            def _(u):
                self.out_copy(u).wait_send()


def centre(values):
    average = jnp.mean(values, axis=-1, keepdims=True)
    centered = values - average
    spread = jnp.mean(centered * centered, axis=-1, keepdims=True)
    scaling = lax.rsqrt(spread + 1e-05)
    return centered * scaling, scaling


def norm_inward(scaled, normed, scaling):
    return scaling * (
        scaled
        - jnp.mean(scaled, axis=-1, keepdims=True)
        - normed * jnp.mean(scaled * normed, axis=-1, keepdims=True)
    )


def fold_rows(values):
    rows, width = values.shape
    return jnp.sum(values.reshape(rows // 8, 8, width), axis=0)


def attention_setup(tok_ref, wq_ref, wk_ref, wv_ref, rel_ref, corner_ref,
                    q_ref, k_ref, v_ref, krel_ref, qrel_ref, tq_ref, tk_ref, idx_ref, col_ref, row_ref):
    slots = tok_ref.shape[0]
    heads, wide = q_ref.shape[0], q_ref.shape[1]
    chunks = wide // LANES
    for weight, target in ((wq_ref, q_ref), (wk_ref, k_ref), (wv_ref, v_ref)):
        value = dot_nn(tok_ref[...], weight[...]).astype(LOW)
        for head in range(heads):
            target[head, :slots, :] = value[:, head * HEAD : (head + 1) * HEAD]
            if wide > slots:
                target[head, slots:, :] = jnp.zeros((wide - slots, HEAD), LOW)
    for weight, target in ((wk_ref, krel_ref), (wq_ref, qrel_ref)):
        value = dot_nn(rel_ref[...], weight[...]).astype(LOW)
        for head in range(heads):
            target[head] = value[:, head * HEAD : (head + 1) * HEAD]
    for head in range(heads):
        tq_ref[head] = dot_nt(q_ref[head], krel_ref[head])
        tk_ref[head] = dot_nt(k_ref[head], qrel_ref[head])
    row_ref[...] = jnp.zeros_like(row_ref)
    row_ref[:, :slots] = corner_ref[...]
    for kind in range(2):
        for big in range(chunks):
            here = slice(big * LANES, (big + 1) * LANES)
            col_ref[kind, here, :] = jnp.broadcast_to(row_ref[kind : kind + 1, here], (LANES, LANES)).T

    @pl.loop(0, chunks)
    def _(big):
        at = span(big * LANES, LANES)
        for kind in range(2):
            own = col_ref[kind, at, :]
            for chunk in range(chunks):
                other = row_ref[kind : kind + 1, chunk * LANES : (chunk + 1) * LANES]
                idx_ref[kind, chunk, at, :] = bucket((own - other) >> 3)


def attention_block(big, head, length, q_ref, k_ref, v_ref, tq_ref, tk_ref, idx_ref, log_ref, attend_ref, ctx_ref):
    wide = q_ref.shape[1]
    chunks = wide // LANES
    slots = attend_ref.shape[1]
    scale = (7.0 * HEAD) ** (-0.5)
    rows = min(LANES, slots - big * LANES)
    some = slice(big * LANES, big * LANES + rows)
    slant = lax.broadcasted_iota(jnp.int32, (LANES, LANES), 0) - lax.broadcasted_iota(
        jnp.int32, (LANES, LANES), 1
    )
    log_ref[:rows, :] = dot_nt(q_ref[head, some, :], k_ref[head])
    for chunk in range(chunks):
        there = slice(chunk * LANES, (chunk + 1) * LANES)
        away = (big - chunk) * LANES
        toward = log_ref[:rows, there]
        if abs(big - chunk) >= 2:
            lane = NB - 1 if away > 0 else 0
            toward = toward + tq_ref[head, some, lane : lane + 1]
            lane = NB - 1 - lane
            beside = jnp.broadcast_to(tk_ref[head, there, lane : lane + 1], (LANES, LANES))
        else:
            toward = toward + lane_gather(tq_ref[head, some, :NB], bucket(slant + away)[:rows])
            beside = lane_gather(tk_ref[head, there, :NB], bucket(slant - away))
        for kind in range(2):
            lanes = slice((kind + 1) * NB, (kind + 2) * NB)
            toward = toward + lane_gather(tq_ref[head, some, lanes], idx_ref[kind, chunk, some, :])
            beside = beside + lane_gather(tk_ref[head, there, lanes], idx_ref[kind, big, there, :])
        log_ref[:rows, there] = toward + beside.T[:rows]
    block = 32
    for start in range(0, rows, block):
        at = slice(start, start + block)
        j_at = lax.broadcasted_iota(jnp.int32, (block, wide), 1)
        masked = jnp.where(j_at < length, log_ref[at, :], NEG_FILL)
        peak = jnp.max(masked, axis=-1, keepdims=True)
        grown = jnp.exp((masked - peak) * scale)
        total = jnp.sum(grown, axis=-1, keepdims=True)
        attend_ref[head, big * LANES + start : big * LANES + start + block, :] = (
            grown * (1.0 / total)
        ).astype(LOW)
    ctx_ref[head, some, :] = dot_nn(attend_ref[head, some, :], v_ref[head]).astype(LOW)


def make_steps(step_ref, col_ref, slots):
    wide = step_ref.shape[1]
    block = 64
    if wide > slots:
        step_ref[:, slots:, :] = jnp.zeros_like(step_ref[:, slots:, :])

    @pl.loop(0, slots // block)
    def _(step):
        at = span(step * block, block)
        quotient = lax.broadcasted_iota(jnp.int32, (block, NB), 1) * BOX_STEP
        for kind in range(2):
            own = col_ref[kind, at, :]
            for rest in range(BOX_STEP):
                lanes = slice(rest * NB, (rest + 1) * NB)
                step_ref[kind, at, lanes] = (own <= quotient + rest).astype(FULL).astype(LOW)


def fold_at(kind, r, at):
    return (kind, at, slice(r % 3 * NB, (r % 3 + 1) * NB))


def bucket_sums(big, rows, mat, step_ref, col_ref, fold_ref, hist_ref):
    chunks = step_ref.shape[1] // LANES
    for kind in range(2):
        value = dot_nn(mat[...], step_ref[kind])
        for r in range(BOX_STEP):
            fold_ref[fold_at(kind, r, slice(r // 3 * LANES, r // 3 * LANES + rows))] = value[
                :, r * NB : (r + 1) * NB
            ]
    block = 32

    @pl.loop(0, rows // block)
    def _(step):
        local = step * block
        at = span(local, block)
        far = span(big * LANES + local, block)
        lane = lax.broadcasted_iota(jnp.int32, (block, NB), 1)
        row = lax.broadcasted_iota(jnp.int32, (block, NB), 0) + local
        part = [mat[at, c * LANES : (c + 1) * LANES].astype(FULL) for c in range(chunks)]
        zero = jnp.zeros((block, LANES), FULL)
        before = part[big - 1] if big >= 1 else zero
        after = part[big + 1] if big + 1 < chunks else zero
        mid = part[big]
        delta = lane - row
        window = jnp.where(delta > NB // 2, before, jnp.where(delta < 1 - NB // 2, after, mid))
        spread = lane_gather(window, (row + NB // 2 - lane) & (NB - 1))
        under = jnp.where(delta <= NB // 2 + 1, before, 0.0) + jnp.where(
            delta <= 1 - NB // 2, mid, 0.0
        )
        over = jnp.where(delta >= NB // 2, mid, 0.0) + jnp.where(delta >= -(NB // 2), after, 0.0)
        for c in range(big - 1):
            under = under + part[c]
        for c in range(big + 2, chunks):
            over = over + part[c]
        under = jnp.sum(under, axis=-1, keepdims=True)
        over = jnp.sum(over, axis=-1, keepdims=True)
        spread = jnp.where(lane == 0, over, jnp.where(lane == NB - 1, under, spread))
        hist_ref[at, 0:NB] = spread.astype(LOW)
        for kind in range(2):
            own = col_ref[kind, far, :]
            groups = [
                fold_ref[fold_at(kind, r, span(r // 3 * LANES + local, block))]
                for r in range(BOX_STEP)
            ]
            every = groups[-1][:, NB - 1 : NB]
            for bit in range(3):
                odd = (own & (1 << bit)) != 0
                groups = [
                    jnp.where(odd, groups[g + 1], groups[g]) for g in range(0, len(groups), 2)
                ]
            index = (own >> 3) + NB // 2 - lane
            found = lane_gather(groups[0], index & (NB - 1))
            found = jnp.where(index < 0, 0.0, found)
            found = jnp.where((index >= NB) | (lane == 0), every, found)
            following = pltpu.roll(found, NB - 1, 1)
            found = found - jnp.where(lane == NB - 1, 0.0, following)
            hist_ref[at, (kind + 1) * NB : (kind + 2) * NB] = found.astype(LOW)


def layer_kernel(
    length_ref, tok_ref, wq_ref, wk_ref, wv_ref, rel_ref, corner_ref,
    wo_ref, cot_ref, wi_ref, wu_ref, bo_ref, ga_ref, sa_ref, bi_ref, bu_ref, gf_ref, sf_ref,
    q_ref, k_ref, qrel_ref, ctx_ref, out_ref, grad_ref, grad_low_ref, hidden_ref, active_ref,
    mid_low_ref, inner_low_ref, small_ref, mat_ref, gq_ref, gv_ref, gkrel_ref, step_ref, col_ref,
    v_ref, krel_ref, attend_ref, tq_ref, tk_ref, idx_ref, row_ref, log_ref,
    own, inner, outer, normed_ref, scale_ref, sums_ref, gc_ref, hist_ref, gv_sum, gkrel_sum,
    in_send, in_recv, out_send, out_recv,
):
    slots = tok_ref.shape[0]
    chunks = slots // HOP
    heads, wide = q_ref.shape[0], q_ref.shape[1]
    blocks = wide // LANES
    per = LANES // HOP
    scale = (7.0 * HEAD) ** (-0.5)
    line = Line("head", own, inner, outer, (in_send, in_recv, out_send, out_recv))
    barrier = pltpu.get_barrier_semaphore()
    line.greet(barrier)
    sums_ref[...] = jnp.zeros_like(sums_ref)
    gv_sum[...] = jnp.zeros_like(gv_sum)
    gkrel_sum[...] = jnp.zeros_like(gkrel_sum)
    if wide > slots:
        mat_ref[:, slots:, :] = jnp.zeros_like(mat_ref[:, slots:, :])
    attention_setup(tok_ref, wq_ref, wk_ref, wv_ref, rel_ref, corner_ref,
                    q_ref, k_ref, v_ref, krel_ref, qrel_ref, tq_ref, tk_ref, idx_ref, col_ref, row_ref)
    pl.semaphore_wait(barrier, line.greeted())
    root = 0.5**0.5
    bell = (0.5 / jnp.pi) ** 0.5

    def forward_head(big, head):
        attention_block(big, head, length_ref[0], q_ref, k_ref, v_ref, tq_ref, tk_ref, idx_ref, log_ref,
                        attend_ref, ctx_ref)

    def put(c, value):
        for part in range(PAIR // HOP):
            own[c * (PAIR // HOP) + part] = value[part * HOP : (part + 1) * HOP]

    def got(u):
        first = line.total(u * (PAIR // HOP))
        return jnp.concatenate([outer[first + part] for part in range(PAIR // HOP)], axis=0)

    def project(c):
        at = span(c * PAIR, PAIR)
        context = jnp.concatenate([ctx_ref[head, at, :] for head in range(heads)], axis=1)
        put(c, dot_nn(context, wo_ref[...]))

    def after_attention(c, u):
        at = span(c * PAIR, PAIR)
        normed, scaling = centre(got(u) + bo_ref[...] + tok_ref[at, :].astype(FULL))
        normed_ref[at, :] = normed
        scale_ref[at, :] = scaling
        hidden_low = (normed * ga_ref[...] + sa_ref[...]).astype(LOW)
        hidden_ref[at, :] = hidden_low
        pre = dot_nn(hidden_low, wi_ref[...]) + bi_ref[...]
        grad_ref[at, :] = pre
        active = (pre * (1.0 + lax.erf(pre * root)) * 0.5).astype(LOW)
        active_ref[at, :] = active
        put(c, dot_nn(active, wu_ref[...]))

    def after_ffn(c, u):
        at = span(c * PAIR, PAIR)
        hidden = normed_ref[at, :] * ga_ref[...] + sa_ref[...]
        normed, scaling = centre(got(u) + bu_ref[...] + hidden)
        out_ref[at, :] = (normed * gf_ref[...] + sf_ref[...]).astype(LOW)
        upstream = cot_ref[at, :].astype(FULL)
        grad_mid = norm_inward(upstream * gf_ref[...], normed, scaling)
        sums_ref[4] += fold_rows(grad_mid)
        sums_ref[5] += fold_rows(upstream * normed)
        sums_ref[6] += fold_rows(upstream)
        pre = grad_ref[at, :]
        grad_ref[at, :] = grad_mid
        mid_low = grad_mid.astype(LOW)
        mid_low_ref[at, :] = mid_low
        grad_active = dot_nt(mid_low, wu_ref[...])
        slope = (1.0 + lax.erf(pre * root)) * 0.5 + pre * jnp.exp(-0.5 * pre * pre) * bell
        inner_low = (grad_active * slope).astype(LOW)
        sums_ref[3] += fold_rows(inner_low.astype(FULL))
        inner_low_ref[at, :] = inner_low
        put(c, dot_nt(inner_low, wi_ref[...]))

    def after_hidden(c, u):
        at = span(c * PAIR, PAIR)
        upstream = got(u) + grad_ref[at, :]
        normed = normed_ref[at, :]
        grad_attn = norm_inward(upstream * ga_ref[...], normed, scale_ref[at, :])
        sums_ref[0] += fold_rows(grad_attn)
        sums_ref[1] += fold_rows(upstream * normed)
        sums_ref[2] += fold_rows(upstream)
        grad_ref[at, :] = grad_attn
        grad_low_ref[at, :] = grad_attn.astype(LOW)

    def backward_block(big):
        rows = min(LANES, slots - big * LANES)
        some = slice(big * LANES, big * LANES + rows)
        value = dot_nt(grad_low_ref[some, :], wo_ref[...]).astype(LOW)
        for head in range(heads):
            gc_ref[head, :rows, :] = value[:, head * HEAD : (head + 1) * HEAD]

    def backward_head(big, head):
        rows = min(LANES, slots - big * LANES)
        some = slice(big * LANES, big * LANES + rows)
        gc = gc_ref[head, :rows, :]
        grad_attend = dot_nt(gc, v_ref[head])
        mean = jnp.sum(gc.astype(FULL) * ctx_ref[head, some, :].astype(FULL), axis=-1, keepdims=True)
        attend = attend_ref[head, some, :]
        mat_ref[head, some, :] = (attend.astype(FULL) * (grad_attend - mean)).astype(LOW)
        gv_sum[head] += dot_tn(attend, gc)
        bucket_sums(big, rows, mat_ref.at[head, some, :], step_ref, col_ref, tq_ref, hist_ref)
        hist = hist_ref[:rows, :]
        gq = dot_nn(mat_ref[head, some, :], k_ref[head]) + dot_nn(hist, krel_ref[head])
        gq_ref[head, some, :] = (gq * scale).astype(LOW)
        gkrel_sum[head] += dot_tn(hist, q_ref[head, some, :])

    for head in range(heads):
        forward_head(0, head)
    count = 3 * chunks
    ratio = PAIR // HOP
    first_back = 2 * chunks + line.trip + per
    last_slot = first_back + (blocks - 1) * per + heads

    @pl.loop(0, max(count + line.trip, last_slot))
    def _(slot):
        @pl.when((slot < chunks) & (lax.rem(slot, ratio) == 0))
        def _():
            project(slot // ratio)

        line.step(slot, count)
        ahead = slot + per
        for big in range(1, blocks):

            @pl.when(ahead // per == big)
            def _(big=big):
                forward_head(big, lax.rem(ahead, per))

        done = slot - line.trip - (ratio - 1)
        pair = done // ratio
        ready = (done >= 0) & (lax.rem(done + ratio, ratio) == 0)
        pairs = chunks // ratio

        @pl.when(ready & (pair < pairs))
        def _():
            after_attention(pair, pair)

        @pl.when(ready & (pair >= pairs) & (pair < 2 * pairs))
        def _():
            after_ffn(pair - pairs, pair)

        @pl.when(ready & (pair >= 2 * pairs) & (pair < 3 * pairs))
        def _():
            after_hidden(pair - 2 * pairs, pair)

        @pl.when(slot == 2 * chunks)
        def _():
            make_steps(step_ref, col_ref, slots)

        since = slot - first_back
        for big in range(blocks):

            @pl.when((since >= 0) & (since // per == big))
            def _(big=big):
                at_head = lax.rem(since, per)

                @pl.when(at_head == 0)
                def _():
                    backward_block(big)

                backward_head(big, at_head)

    for at in range(7):
        small_ref[at : at + 1, :] = jnp.sum(sums_ref[at], axis=0, keepdims=True)
    small_ref[7:8, :] = jnp.zeros_like(small_ref[7:8, :])
    for head in range(heads):
        gv_ref[head] = gv_sum[head, :slots, :].astype(LOW)
        gkrel_ref[head] = (gkrel_sum[head] * scale).astype(LOW)
    line.drain(count)


def layer(tokens, length, corners, w_query, w_key, w_value, rel, w_output, cotangent, w_inner, w_outer, vectors):
    slots, width = tokens.shape
    units = w_inner.shape[1]
    mine = w_query.shape[1]
    heads = mine // HEAD
    wide = -(-slots // LANES) * LANES
    assert units == width and heads == LANES // HOP and slots % PAIR == 0
    vmem = pl.BlockSpec(memory_space=pltpu.VMEM)
    chunks = slots // HOP
    shape = jax.ShapeDtypeStruct
    dma = pltpu.SemaphoreType.DMA
    return pl.pallas_call(
        layer_kernel,
        out_shape=(
            shape((heads, wide, HEAD), LOW),
            shape((heads, wide, HEAD), LOW),
            shape((heads, 3 * NB, HEAD), LOW),
            shape((heads, slots, HEAD), LOW),
            shape((slots, width), LOW),
            shape((slots, width), FULL),
            shape((slots, width), LOW),
            shape((slots, width), LOW),
            shape((slots, units), LOW),
            shape((slots, width), LOW),
            shape((slots, units), LOW),
            shape((8, width), FULL),
            shape((heads, wide, wide), LOW),
            shape((heads, slots, HEAD), LOW),
            shape((heads, slots, HEAD), LOW),
            shape((heads, 3 * NB, HEAD), LOW),
            shape((2, wide, BOX_STEP * NB), LOW),
            shape((2, wide, LANES), jnp.int32),
        ),
        in_specs=[pl.BlockSpec(memory_space=pltpu.SMEM)] + [vmem] * 17,
        out_specs=(vmem,) * 18,
        scratch_shapes=[
            pltpu.VMEM((heads, wide, HEAD), LOW),
            pltpu.VMEM((heads, 3 * NB, HEAD), LOW),
            pltpu.VMEM((heads, slots, wide), LOW),
            pltpu.VMEM((heads, wide, 3 * NB), FULL),
            pltpu.VMEM((heads, wide, 3 * NB), FULL),
            pltpu.VMEM((2, wide // LANES, wide, LANES), jnp.int32),
            pltpu.VMEM((2, wide), jnp.int32),
            pltpu.VMEM((LANES, wide), FULL),
            pltpu.VMEM((chunks, HOP, width), FULL),
            pltpu.VMEM((chunks, HOP, width), FULL),
            pltpu.VMEM((2 * chunks, HOP, width), FULL),
            pltpu.VMEM((slots, width), FULL),
            pltpu.VMEM((slots, 1), FULL),
            pltpu.VMEM((7, 8, width), FULL),
            pltpu.VMEM((heads, LANES, HEAD), LOW),
            pltpu.VMEM((LANES, 3 * NB), LOW),
            pltpu.VMEM((heads, wide, HEAD), FULL),
            pltpu.VMEM((heads, 3 * NB, HEAD), FULL),
            dma((chunks,)),
            dma((chunks,)),
            dma((2 * chunks,)),
            dma((2 * chunks,)),
        ],
        compiler_params=pltpu.CompilerParams(
            vmem_limit_bytes=VMEM_LIMIT, collective_id=1, has_side_effects=True
        ),
        name="layer",
    )(length, tokens, w_query, w_key, w_value, rel, corners,
      w_output, cotangent, w_inner, w_outer, *[v.reshape(1, -1) for v in vectors])


class Halving:
    def __init__(self, order, source, got, out, send, recv):
        self.order, self.source, self.got, self.out = order, source, got, out
        self.send, self.recv = send, recv
        self.b = lax.axis_index("batch")

    def part(self, stage, flip):
        bit = self.order[stage]
        rest = sorted(self.order[stage:], reverse=True)
        mine = (self.b >> bit) & 1
        pick = 1 - mine if flip else mine
        return tuple(pick if k == bit else slice(None) for k in rest)

    def copy(self, stage):
        source = self.source if stage == 0 else self.got[stage - 1]
        return pltpu.make_async_remote_copy(
            src_ref=source.at[self.part(stage, True)],
            dst_ref=self.got[stage],
            send_sem=self.send.at[stage],
            recv_sem=self.recv.at[stage],
            device_id={"batch": self.b ^ (1 << self.order[stage])},
            device_id_type=MESH,
        )

    def start(self):
        self.copy(0).start()

    def turn(self, stage):
        self.copy(stage).wait_recv()
        kept = self.source if stage == 0 else self.got[stage - 1]
        value = kept[self.part(stage, False)] + self.got[stage][...]
        if stage == 0:
            self.copy(0).wait_send()
        if stage + 1 < len(self.order):
            self.got[stage][...] = value
            self.copy(stage + 1).start()
        else:
            self.out[...] = value

    def drain(self):
        for stage in range(1, len(self.order)):
            self.copy(stage).wait_send()


def gradient_kernel(
    tok_ref, wq_ref, wk_ref, wv_ref, rel_ref,
    q_ref, k_ref, qrel_ref, ctx_ref, grad_ref, grad_low_ref, hidden_ref, active_ref,
    mid_low_ref, inner_low_ref, small_ref, mat_ref, gq_ref, gv_ref, gkrel_ref, step_ref, col_ref,
    gtok_ref, owq_ref, owk_ref, owv_ref, owo_ref, owi_ref, owu_ref, orel_ref, osmall_ref,
    own, inner, outer, turned_ref, fold_ref, hist_ref, gk_ref, gk_low_ref, gqrel_sum, gqrel_ref,
    work_ref, grel_ref, rel_own, rel_in, rel_out, rel_all, small_sum, small_got,
    *rest,
    bits, pieces, buffers,
):
    jobs_all = len(pieces) + 2
    got = [rest[at * bits : (at + 1) * bits] for at in range(jobs_all)]
    (in_send, in_recv, out_send, out_recv, rin_send, rin_recv, rout_send, rout_recv,
     piece_send, piece_recv, back_send, back_recv, small_send, small_recv) = rest[jobs_all * bits :]
    slots, width = tok_ref.shape
    chunks = slots // HOP
    heads, wide = q_ref.shape[0], q_ref.shape[1]
    blocks = wide // LANES
    per = LANES // HOP
    scale = (7.0 * HEAD) ** (-0.5)
    line = Line("head", own, inner, outer, (in_send, in_recv, out_send, out_recv))
    rel_line = Line("head", rel_own, rel_in, rel_out, (rin_send, rin_recv, rout_send, rout_recv), 1)
    b = lax.axis_index("batch")
    barrier = pltpu.get_barrier_semaphore()
    line.greet(barrier)
    for k in range(bits):
        pl.semaphore_signal(barrier, inc=1, device_id={"batch": b ^ (1 << k)}, device_id_type=MESH)

    orders = (list(range(bits)), [0] + list(range(bits - 1, 0, -1)))
    outs = (owq_ref, owk_ref, owv_ref, owo_ref, owi_ref, owu_ref)
    whole = (slice(None),) * (bits + 1)
    jobs = []
    for at, (which, start, size) in enumerate(pieces):
        jobs.append(
            Halving(
                orders[at % 2],
                work_ref.at[at % buffers],
                got[at],
                outs[which].at[:, start : start + size],
                piece_send.at[at],
                piece_recv.at[at],
            )
        )
    half = width // 2
    rel_jobs = []
    for side in range(2):
        lanes = slice(side * half, (side + 1) * half)
        at = len(pieces) + side
        rel_jobs.append(
            Halving(
                orders[side],
                grel_ref.at[whole + (lanes,)],
                got[at],
                rel_own.at[0, :, lanes],
                piece_send.at[at],
                piece_recv.at[at],
            )
        )

    def heads_of(ref):
        return jnp.concatenate([ref[head] for head in range(heads)], axis=1)

    def make(at):
        which, start, size = pieces[at]
        lanes = slice(start, start + size)
        if which == 0:
            value = dot_tn(tok_ref[...], heads_of(gq_ref)) + dot_tn(rel_ref[...], heads_of(gqrel_ref))
        elif which == 1:
            value = dot_tn(tok_ref[...], gk_ref[...]) + dot_tn(rel_ref[...], heads_of(gkrel_ref))
        elif which == 2:
            value = dot_tn(tok_ref[...], heads_of(gv_ref))
        elif which == 3:
            value = dot_tn(grad_low_ref[...], heads_of(ctx_ref))
        elif which == 4:
            value = dot_tn(hidden_ref[...], inner_low_ref[:, lanes])
        else:
            value = dot_tn(mid_low_ref[...], active_ref[:, lanes])
        target = work_ref.at[at % buffers]
        target[...] = value.reshape(target.shape)
        jobs[at].start()

    def small_copy(k):
        return pltpu.make_async_remote_copy(
            src_ref=small_sum.at[k],
            dst_ref=small_got.at[k],
            send_sem=small_send.at[k],
            recv_sem=small_recv.at[k],
            device_id={"batch": b ^ (1 << k)},
            device_id_type=MESH,
        )

    def small_turn(k):
        small_copy(k).wait_recv()
        value = small_sum[k] + small_got[k]
        if k + 1 < bits:
            small_sum[k + 1] = value
            small_copy(k + 1).start()
        else:
            osmall_ref[...] = value

    def back_copy(k):
        region = tuple(
            slice(None) if other > k else (b >> other) & 1 for other in range(bits - 1, -1, -1)
        )
        return pltpu.make_async_remote_copy(
            src_ref=rel_all.at[region],
            dst_ref=rel_all.at[region],
            send_sem=back_send.at[k],
            recv_sem=back_recv.at[k],
            device_id={"batch": b ^ (1 << k)},
            device_id_type=MESH,
        )

    def back_turn(k):
        back_copy(k).wait_recv()
        if k > 0:
            back_copy(k - 1).start()

    def rel_start():
        for head in range(heads):
            gqrel_ref[head] = (gqrel_sum[head] * scale).astype(LOW)
        value = dot_nt(heads_of(gkrel_ref), wk_ref[...]) + dot_nt(heads_of(gqrel_ref), wq_ref[...])
        grel_ref[...] = value.reshape(grel_ref.shape)
        for job in rel_jobs:
            job.start()

    def rel_turn(stage):
        for job in rel_jobs:
            job.turn(stage)

    def rel_step(slot):
        rel_line.step(jnp.int32(slot), 1)
        if slot == rel_line.trip:
            region = tuple((b >> other) & 1 for other in range(bits - 1, -1, -1))
            rel_all[region] = rel_out[0]
            back_copy(bits - 1).start()

    def column_head(big, head):
        rows = min(LANES, slots - big * LANES)
        some = slice(big * LANES, big * LANES + rows)
        lanes = slice(big * LANES, (big + 1) * LANES)
        for chunk in range(blocks):
            there = slice(chunk * LANES, (chunk + 1) * LANES)
            turned_ref[:, there] = mat_ref[head, there, lanes].T
        bucket_sums(big, rows, turned_ref.at[:rows, :], step_ref, col_ref, fold_ref, hist_ref)
        hist = hist_ref[:rows, :]
        gk = dot_nn(turned_ref[:rows, :], q_ref[head]) + dot_nn(hist, qrel_ref[head])
        gk_low_ref[head, :rows, :] = (gk * scale).astype(LOW)
        gqrel_sum[head] += dot_tn(hist, k_ref[head, some, :])

    def inputs_block(big):
        rows = min(LANES, slots - big * LANES)
        some = slice(big * LANES, big * LANES + rows)
        gk = jnp.concatenate([gk_low_ref[head, :rows, :] for head in range(heads)], axis=1)
        gk_ref[some, :] = gk
        gq = jnp.concatenate([gq_ref[head, some, :] for head in range(heads)], axis=1)
        gv = jnp.concatenate([gv_ref[head, some, :] for head in range(heads)], axis=1)
        value = dot_nt(gq, wq_ref[...]) + dot_nt(gk, wk_ref[...]) + dot_nt(gv, wv_ref[...])
        for part in range(rows // HOP):
            own[big * per + part] = value[part * HOP : (part + 1) * HOP]

    gqrel_sum[...] = jnp.zeros_like(gqrel_sum)
    small_sum[0] = small_ref[...]
    pl.semaphore_wait(barrier, line.greeted() + bits)
    small_copy(0).start()
    early = len(pieces) - 2
    make(0)
    make(1)

    @pl.loop(0, heads)
    def _(head):
        column_head(0, head)

    inputs_block(0)

    tasks = {}

    def add(slot, task):
        tasks.setdefault(slot, []).append(task)

    for at in range(2, early):
        add(at - 2, lambda at=at: make(at))
    for at in range(early):
        add(at, lambda at=at: jobs[at].turn(0))
        if bits > 1:
            for stage in range(1, bits):
                add(1 + 3 * (at // 2) + 3 * stage, lambda at=at, stage=stage: jobs[at].turn(stage))
    for k in range(bits):
        add(2 + 2 * k, lambda k=k: small_turn(k))
    ended = (blocks - 1) * per
    add(ended, rel_start)
    add(ended, lambda: make(early))
    add(ended, lambda: make(early + 1))
    for stage in range(bits):
        add(ended + 1 + 2 * stage, lambda stage=stage: rel_turn(stage))
    for side in range(2):
        for stage in range(bits):
            add(ended + 2 + 3 * stage, lambda side=side, stage=stage: jobs[early + side].turn(stage))
    for hop in range(rel_line.trip + 1):
        add(ended + 2 * bits + 1 + hop, lambda hop=hop: rel_step(hop))
    for k in range(bits - 1, -1, -1):
        add(ended + 2 * bits + 1 + rel_line.trip + bits - k, lambda k=k: back_turn(k))
    total = chunks + line.trip

    @pl.loop(0, max(total, max(tasks) + 1))
    def _(slot):
        line.step(slot, chunks)
        ahead = slot + per
        for big in range(1, blocks):

            @pl.when(ahead // per == big)
            def _(big=big):
                head = lax.rem(ahead, per)
                column_head(big, head)

                @pl.when(head == per - 1)
                def _():
                    inputs_block(big)

        for when in sorted(tasks):

            @pl.when(slot == when)
            def _(when=when):
                for task in tasks[when]:
                    task()

        done = slot - line.trip

        @pl.when((done >= 0) & (done < chunks))
        def _():
            at = span(done * HOP, HOP)
            gtok_ref[at, :] = (outer[done] + grad_ref[at, :]).astype(LOW)

    orel_ref[...] = rel_all[...]
    line.drain(chunks)
    rel_line.drain(1)
    for job in jobs + rel_jobs:
        job.drain()
    for k in range(bits):
        small_copy(k).wait_send()
        back_copy(k).wait_send()


def gradients(tokens, w_query, w_key, w_value, rel, kept, batch):
    slots, width = tokens.shape
    q, active = kept[0], kept[7]
    heads, wide = q.shape[:2]
    mine, units = heads * HEAD, active.shape[1]
    bits = batch.bit_length() - 1
    assert 1 << bits == batch
    vmem = pl.BlockSpec(memory_space=pltpu.VMEM)
    chunks = slots // HOP
    split = (2,) * bits
    part = width // batch
    rel_part = rel.shape[0] // batch
    assert mine == PIECE
    pieces = [(2, 0, PIECE), (3, 0, PIECE)]
    for start in range(0, units, PIECE):
        pieces += [(4, start, PIECE), (5, start, PIECE)]
    pieces += [(0, 0, PIECE), (1, 0, PIECE)]
    buffers = 4
    shape = jax.ShapeDtypeStruct
    got = []
    for _ in pieces:
        got += [pltpu.VMEM((2,) * (bits - 1 - s) + (part, PIECE), FULL) for s in range(bits)]
    for _ in range(2):
        got += [pltpu.VMEM((2,) * (bits - 1 - s) + (rel_part, width // 2), FULL) for s in range(bits)]
    dma = pltpu.SemaphoreType.DMA
    return pl.pallas_call(
        functools.partial(gradient_kernel, bits=bits, pieces=pieces, buffers=buffers),
        out_shape=(
            shape((slots, width), LOW),
            shape((part, mine), FULL),
            shape((part, mine), FULL),
            shape((part, mine), FULL),
            shape((part, mine), FULL),
            shape((part, units), FULL),
            shape((part, units), FULL),
            shape(split + (rel_part, width), FULL),
            shape((8, width), FULL),
        ),
        in_specs=[vmem] * 22,
        out_specs=(vmem,) * 9,
        scratch_shapes=[
            pltpu.VMEM((chunks, HOP, width), FULL),
            pltpu.VMEM((chunks, HOP, width), FULL),
            pltpu.VMEM((chunks, HOP, width), FULL),
            pltpu.VMEM((LANES, wide), LOW),
            pltpu.VMEM((2, 3 * LANES, 3 * NB), FULL),
            pltpu.VMEM((LANES, 3 * NB), LOW),
            pltpu.VMEM((slots, mine), LOW),
            pltpu.VMEM((heads, LANES, HEAD), LOW),
            pltpu.VMEM((heads, 3 * NB, HEAD), FULL),
            pltpu.VMEM((heads, 3 * NB, HEAD), LOW),
            pltpu.VMEM((buffers,) + split + (part, PIECE), FULL),
            pltpu.VMEM(split + (rel_part, width), FULL),
            pltpu.VMEM((1, rel_part, width), FULL),
            pltpu.VMEM((1, rel_part, width), FULL),
            pltpu.VMEM((1, rel_part, width), FULL),
            pltpu.VMEM(split + (rel_part, width), FULL),
            pltpu.VMEM((bits, 8, width), FULL),
            pltpu.VMEM((bits, 8, width), FULL),
        ]
        + got
        + [dma((chunks,))] * 4
        + [dma((1,))] * 4
        + [dma((len(pieces) + 2, bits))] * 2
        + [dma((bits,))] * 4,
        compiler_params=pltpu.CompilerParams(
            vmem_limit_bytes=VMEM_LIMIT, collective_id=2, has_side_effects=True
        ),
        name="gradients",
    )(tokens, w_query, w_key, w_value, rel, *kept)


def finish_kernel(out, gtok, gwq, gwk, gwv, gwo, gwi, gwu, grel, small, *targets):
    (o_out, o_gtok, o_gwq, o_gwk, o_gwv, o_gwo, o_gwi, o_gwu, o_grel) = targets[:9]
    o_out[...] = out[...]
    o_gtok[...] = gtok[...]
    o_gwq[...] = gwq[...]
    o_gwk[...] = gwk[...]
    o_gwv[...] = gwv[...]
    o_gwo[...] = gwo[...].T
    o_gwi[...] = gwi[...]
    o_gwu[...] = gwu[...].T
    o_grel[...] = grel[...]
    for at, target in enumerate(targets[9:]):
        target[...] = small[at]


def finish(out, gtok, gwq, gwk, gwv, gwo, gwi, gwu, grel, small):
    vmem = pl.BlockSpec(memory_space=pltpu.VMEM)
    shape = jax.ShapeDtypeStruct
    same = lambda a: shape(a.shape, a.dtype)
    turn = lambda a: shape(a.shape[::-1], a.dtype)
    return pl.pallas_call(
        finish_kernel,
        out_shape=(same(out), same(gtok), same(gwq), same(gwk), same(gwv), turn(gwo), same(gwi), turn(gwu), same(grel))
        + (shape(small.shape[1:], FULL),) * 7,
        in_specs=[vmem] * 10,
        out_specs=(vmem,) * 16,
        compiler_params=pltpu.CompilerParams(vmem_limit_bytes=VMEM_LIMIT),
        name="finish",
    )(out, gtok, gwq, gwk, gwv, gwo, gwi, gwu, grel, small)


def shards(
    tokens,
    page_lengths,
    corners,
    w_query,
    w_key,
    w_value,
    w_output,
    b_output,
    gain_attn,
    shift_attn,
    w_inner,
    b_inner,
    w_outer,
    b_outer,
    gain_ffn,
    shift_ffn,
    rel_tables,
    cotangent,
):
    rel = rel_tables.reshape(3 * NB, rel_tables.shape[2])
    vectors = (b_output, gain_attn, shift_attn, b_inner, b_outer, gain_ffn, shift_ffn)
    q, k, qrel, ctx, output, *kept = layer(
        tokens, page_lengths, corners, w_query, w_key, w_value, rel,
        w_output, cotangent, w_inner, w_outer, vectors,
    )
    done = gradients(
        tokens, w_query, w_key, w_value, rel, (q, k, qrel, ctx, *kept), lax.axis_size("batch")
    )
    gtok, gwq, gwk, gwv, gwo, gwi, gwu, grel, small = done
    grel = grel.reshape(rel_tables.shape)
    (output, gtok, gwq, gwk, gwv, gwo, gwi, gwu, grel, gbo, gga, gsa, gbi, gbu, ggf, gsf) = finish(
        output, gtok, gwq, gwk, gwv, gwo, gwi, gwu, grel, small
    )
    return (output, gtok, gwq, gwk, gwv, gwo, gbo, gga, gsa, gwi, gbi, gwu, gbu, ggf, gsf, grel)


def solution(mesh):
    in_specs = (
        P("batch", None),
        P("batch"),
        P(None, "batch"),
        P(None, "head"),
        P(None, "head"),
        P(None, "head"),
        P("head", None),
        P(),
        P(),
        P(),
        P(None, "head"),
        P("head"),
        P("head", None),
        P(),
        P(),
        P(),
        P(),
        P("batch", None),
    )
    out_specs = (
        P("batch", None),
        P("batch", None),
        P("batch", "head"),
        P("batch", "head"),
        P("batch", "head"),
        P("head", "batch"),
        P(),
        P(),
        P(),
        P("batch", "head"),
        P("head"),
        P("head", "batch"),
        P(),
        P(),
        P(),
        P(),
    )
    return jax.shard_map(shards, mesh=mesh, in_specs=in_specs, out_specs=out_specs, check_vma=False)
```

```python
import functools

import jax
import jax.numpy as jnp
from jax import lax
from jax.experimental import pallas as pl
from jax.experimental.pallas import tpu as pltpu
from jax.sharding import PartitionSpec as P

HEAD = 64
NB = 128
BOX_STEP = 8
NEG_FILL = -1000000000.0
LANES = 128
HOP = 32
PAIR = 64
LAG = 2
PIECE = 256
STRIP = 128
RELAYS = 2
VMEM_LIMIT = 61 * 1024 * 1024
MESH = pl.DeviceIdType.MESH
LOW = jnp.bfloat16
FULL = jnp.float32


def dot_nn(a, b):
    return lax.dot_general(a, b, (((1,), (0,)), ((), ())), preferred_element_type=FULL)


def dot_nt(a, b):
    return lax.dot_general(a, b, (((1,), (1,)), ((), ())), preferred_element_type=FULL)


def dot_tn(a, b):
    return lax.dot_general(a, b, (((0,), (0,)), ((), ())), preferred_element_type=FULL)


def lane_gather(table, index):
    return jnp.take_along_axis(table, index, axis=1, mode="promise_in_bounds")


def bucket(step):
    return jnp.clip(step, -(NB // 2), NB // 2 - 1) + NB // 2


def span(start, size):
    return pl.ds(pl.multiple_of(start, size), size)


class Line:
    def __init__(self, axis, own, inner, outer, sems, lag=LAG):
        self.axis, self.own, self.inner, self.outer, self.lag = axis, own, inner, outer, lag
        self.in_send, self.in_recv, self.out_send, self.out_recv = sems
        self.ring, self.wide_ring = own.shape[0], outer.shape[0]
        self.n = lax.axis_size(axis)
        me = lax.axis_index(axis)
        left = me < self.n // 2
        self.depth = jnp.where(left, me, self.n - 1 - me)
        self.inward = jnp.where(left, me + 1, me - 1)
        self.outward = jnp.where(self.depth == 0, self.inward, jnp.where(left, me - 1, me + 1))
        self.last = self.n // 2 - 1
        self.trip = self.lag * (self.n - 1)

    def greet(self, barrier):
        pl.semaphore_signal(barrier, inc=1, device_id={self.axis: self.inward}, device_id_type=MESH)

        @pl.when(self.depth > 0)
        def _():
            pl.semaphore_signal(
                barrier, inc=1, device_id={self.axis: self.outward}, device_id_type=MESH
            )

    def greeted(self):
        return jnp.where(self.depth > 0, 2, 1)

    def copy(self, source, target, send, recv, to):
        return pltpu.make_async_remote_copy(
            src_ref=source,
            dst_ref=target,
            send_sem=send,
            recv_sem=recv,
            device_id={self.axis: to},
            device_id_type=MESH,
        )

    def total(self, u):
        return lax.rem(u, self.wide_ring)

    def out_copy(self, u):
        o = self.total(u)
        return self.copy(
            self.outer.at[o], self.outer.at[o], self.out_send.at[o], self.out_recv.at[o], self.outward
        )

    def in_copy(self, c, source):
        return self.copy(
            source, self.inner.at[c], self.in_send.at[c], self.in_recv.at[c], self.inward
        )

    def send_in(self, u, c, source):
        @pl.when(self.depth < self.last)
        def _():
            self.in_copy(c, source).start()

        @pl.when(self.depth == self.last)
        def _():
            o = self.total(u)
            self.copy(
                source, self.outer.at[o], self.in_send.at[c], self.out_recv.at[o], self.inward
            ).start()

    def step(self, slot, count):
        here = slot - self.lag * self.depth

        @pl.when((here >= 0) & (here < count))
        def _():
            u = here
            c = lax.rem(u, self.ring)

            @pl.when(self.depth == 0)
            def _():
                self.send_in(u, c, self.own.at[c])

            @pl.when(self.depth > 0)
            def _():
                @pl.when(u >= self.ring)
                def _():
                    self.out_copy(u - self.ring).wait_send()

                self.in_copy(c, self.own.at[c]).wait_recv()
                self.inner[c] += self.own[c]
                self.send_in(u, c, self.inner.at[c])

        back = slot - self.lag * (self.n - 1 - self.depth)

        @pl.when((back >= 0) & (back < count))
        def _():
            u = back
            c = lax.rem(u, self.ring)
            self.in_copy(c, self.own.at[c]).wait_send()
            self.out_copy(u).wait_recv()

            @pl.when(self.depth == self.last)
            def _():
                self.outer[self.total(u)] += self.inner[c] if self.last > 0 else self.own[c]

            @pl.when(self.depth > 0)
            def _():
                self.out_copy(u).start()

    def drain(self, count):
        @pl.when(self.depth > 0)
        def _():
            @pl.loop(count - self.ring, count)
            def _(u):
                self.out_copy(u).wait_send()


class Rounds:
    def __init__(self, order, work, got, out, rounds, send, recv, credit):
        self.order, self.work, self.got, self.out, self.rounds = order, work, got, out, rounds
        self.send, self.recv, self.credit = send, recv, credit
        self.b = lax.axis_index("batch")

    def partner(self, stage):
        return {"batch": self.b ^ (1 << self.order[stage])}

    def part(self, stage, flip):
        bit = self.order[stage]
        rest = sorted(self.order[stage:], reverse=True)
        mine = (self.b >> bit) & 1
        pick = 1 - mine if flip else mine
        return tuple(pick if k == bit else slice(None) for k in rest)

    def source(self, stage):
        return self.work if stage == 0 else self.got[stage - 1]

    def copy(self, stage):
        return pltpu.make_async_remote_copy(
            src_ref=self.source(stage).at[self.part(stage, True)],
            dst_ref=self.got[stage],
            send_sem=self.send.at[stage],
            recv_sem=self.recv.at[stage],
            device_id=self.partner(stage),
            device_id_type=MESH,
        )

    def start(self, stage, number):
        if number > 0:
            pl.semaphore_wait(self.credit.at[stage], 1)
        self.copy(stage).start()

    def free(self, stage, number):
        if number + 1 < self.rounds:
            pl.semaphore_signal(
                self.credit.at[stage], inc=1, device_id=self.partner(stage), device_id_type=MESH
            )

    def begin(self, number, value):
        self.work[...] = value.reshape(self.work.shape)
        self.start(0, number)

    def turn(self, stage, number):
        self.copy(stage).wait_recv()
        value = self.source(stage)[self.part(stage, False)] + self.got[stage][...]
        last = stage + 1 == len(self.order)
        if last:
            size = value.shape[1]
            self.out[:, number * size : (number + 1) * size] = value
        else:
            self.got[stage][...] = value
        self.copy(stage).wait_send()
        if stage > 0:
            self.free(stage - 1, number)
        if last:
            self.free(stage, number)
        else:
            self.start(stage + 1, number)


def batch_orders(bits):
    return (list(range(bits)), [0] + list(range(bits - 1, 0, -1)))


def greet_batch(barrier, bits):
    b = lax.axis_index("batch")
    for k in range(bits):
        pl.semaphore_signal(barrier, inc=1, device_id={"batch": b ^ (1 << k)}, device_id_type=MESH)


def centre(values):
    average = jnp.mean(values, axis=-1, keepdims=True)
    centered = values - average
    spread = jnp.mean(centered * centered, axis=-1, keepdims=True)
    scaling = lax.rsqrt(spread + 1e-05)
    return centered * scaling, scaling


def norm_inward(scaled, normed, scaling):
    return scaling * (
        scaled
        - jnp.mean(scaled, axis=-1, keepdims=True)
        - normed * jnp.mean(scaled * normed, axis=-1, keepdims=True)
    )


def fold_rows(values):
    rows, width = values.shape
    return jnp.sum(values.reshape(rows // 8, 8, width), axis=0)


def attention_setup(tok_ref, wq_ref, wk_ref, wv_ref, rel_ref, corner_ref,
                    q_ref, k_ref, v_ref, krel_ref, qrel_ref, tq_ref, tk_ref, idx_ref, col_ref, row_ref):
    slots = tok_ref.shape[0]
    heads, wide = q_ref.shape[0], q_ref.shape[1]
    chunks = wide // LANES
    for weight, target in ((wq_ref, q_ref), (wk_ref, k_ref), (wv_ref, v_ref)):
        value = dot_nn(tok_ref[...], weight[...]).astype(LOW)
        for head in range(heads):
            target[head, :slots, :] = value[:, head * HEAD : (head + 1) * HEAD]
            if wide > slots:
                target[head, slots:, :] = jnp.zeros((wide - slots, HEAD), LOW)
    for weight, target in ((wk_ref, krel_ref), (wq_ref, qrel_ref)):
        value = dot_nn(rel_ref[...], weight[...]).astype(LOW)
        for head in range(heads):
            target[head] = value[:, head * HEAD : (head + 1) * HEAD]
    for head in range(heads):
        tq_ref[head] = dot_nt(q_ref[head, :slots, :], krel_ref[head])
        tk_ref[head] = dot_nt(k_ref[head], qrel_ref[head])
    row_ref[...] = jnp.zeros_like(row_ref)
    row_ref[:, :slots] = corner_ref[...]
    for kind in range(2):
        for big in range(chunks):
            here = slice(big * LANES, (big + 1) * LANES)
            col_ref[kind, here, :] = jnp.broadcast_to(row_ref[kind : kind + 1, here], (LANES, LANES)).T

    @pl.loop(0, chunks)
    def _(big):
        at = span(big * LANES, LANES)
        for kind in range(2):
            own = col_ref[kind, at, :]
            for chunk in range(chunks):
                other = row_ref[kind : kind + 1, chunk * LANES : (chunk + 1) * LANES]
                idx_ref[kind, chunk, at, :] = bucket((own - other) >> 3)


def attention_block(big, head, length, q_ref, k_ref, v_ref, tq_ref, tk_ref, idx_ref, log_ref, attend_ref, ctx_ref):
    wide = q_ref.shape[1]
    chunks = wide // LANES
    slots = attend_ref.shape[1]
    scale = (7.0 * HEAD) ** (-0.5)
    rows = min(LANES, slots - big * LANES)
    some = slice(big * LANES, big * LANES + rows)
    slant = lax.broadcasted_iota(jnp.int32, (LANES, LANES), 0) - lax.broadcasted_iota(
        jnp.int32, (LANES, LANES), 1
    )
    log_ref[:rows, :] = dot_nt(q_ref[head, some, :], k_ref[head])
    for chunk in range(chunks):
        there = slice(chunk * LANES, (chunk + 1) * LANES)
        away = (big - chunk) * LANES
        toward = log_ref[:rows, there]
        if abs(big - chunk) >= 2:
            lane = NB - 1 if away > 0 else 0
            toward = toward + tq_ref[head, some, lane : lane + 1]
            lane = NB - 1 - lane
            beside = jnp.broadcast_to(tk_ref[head, there, lane : lane + 1], (LANES, LANES))
        else:
            toward = toward + lane_gather(tq_ref[head, some, :NB], bucket(slant + away)[:rows])
            beside = lane_gather(tk_ref[head, there, :NB], bucket(slant - away))
        for kind in range(2):
            lanes = slice((kind + 1) * NB, (kind + 2) * NB)
            toward = toward + lane_gather(tq_ref[head, some, lanes], idx_ref[kind, chunk, some, :])
            beside = beside + lane_gather(tk_ref[head, there, lanes], idx_ref[kind, big, there, :])
        log_ref[:rows, there] = toward + beside.T[:rows]
    block = 32
    for start in range(0, rows, block):
        at = slice(start, start + block)
        j_at = lax.broadcasted_iota(jnp.int32, (block, wide), 1)
        masked = jnp.where(j_at < length, log_ref[at, :], NEG_FILL)
        peak = jnp.max(masked, axis=-1, keepdims=True)
        grown = jnp.exp((masked - peak) * scale)
        total = jnp.sum(grown, axis=-1, keepdims=True)
        attend_ref[head, big * LANES + start : big * LANES + start + block, :] = (
            grown * (1.0 / total)
        ).astype(LOW)
    ctx_ref[head, some, :] = dot_nn(attend_ref[head, some, :], v_ref[head]).astype(LOW)


def make_steps(step_ref, col_ref, slots):
    wide = step_ref.shape[1]
    block = 64
    if wide > slots:
        step_ref[:, slots:, :] = jnp.zeros_like(step_ref[:, slots:, :])

    @pl.loop(0, slots // block)
    def _(step):
        at = span(step * block, block)
        quotient = lax.broadcasted_iota(jnp.int32, (block, NB), 1) * BOX_STEP
        for kind in range(2):
            own = col_ref[kind, at, :]
            for rest in range(BOX_STEP):
                lanes = slice(rest * NB, (rest + 1) * NB)
                step_ref[kind, at, lanes] = (own <= quotient + rest).astype(FULL).astype(LOW)


def fold_at(kind, r, at):
    return (kind, at, slice(r % 3 * NB, (r % 3 + 1) * NB))


def bucket_sums(big, rows, mat, step_ref, col_ref, fold_ref, hist_ref):
    chunks = step_ref.shape[1] // LANES
    for kind in range(2):
        value = dot_nn(mat[...], step_ref[kind])
        for r in range(BOX_STEP):
            fold_ref[fold_at(kind, r, slice(r // 3 * LANES, r // 3 * LANES + rows))] = value[
                :, r * NB : (r + 1) * NB
            ]
    block = 32

    def some(local):
        at = span(local, block)
        far = span(big * LANES + local, block)
        lane = lax.broadcasted_iota(jnp.int32, (block, NB), 1)
        row = lax.broadcasted_iota(jnp.int32, (block, NB), 0) + local
        part = [mat[at, c * LANES : (c + 1) * LANES].astype(FULL) for c in range(chunks)]
        zero = jnp.zeros((block, LANES), FULL)
        before = part[big - 1] if big >= 1 else zero
        after = part[big + 1] if big + 1 < chunks else zero
        mid = part[big]
        delta = lane - row
        window = jnp.where(delta > NB // 2, before, jnp.where(delta < 1 - NB // 2, after, mid))
        spread = lane_gather(window, (row + NB // 2 - lane) & (NB - 1))
        under = jnp.where(delta <= NB // 2 + 1, before, 0.0) + jnp.where(
            delta <= 1 - NB // 2, mid, 0.0
        )
        over = jnp.where(delta >= NB // 2, mid, 0.0) + jnp.where(delta >= -(NB // 2), after, 0.0)
        for c in range(big - 1):
            under = under + part[c]
        for c in range(big + 2, chunks):
            over = over + part[c]
        under = jnp.sum(under, axis=-1, keepdims=True)
        over = jnp.sum(over, axis=-1, keepdims=True)
        spread = jnp.where(lane == 0, over, jnp.where(lane == NB - 1, under, spread))
        hist_ref[at, 0:NB] = spread.astype(LOW)
        for kind in range(2):
            own = col_ref[kind, far, :]
            groups = [
                fold_ref[fold_at(kind, r, span(r // 3 * LANES + local, block))]
                for r in range(BOX_STEP)
            ]
            every = groups[-1][:, NB - 1 : NB]
            for bit in range(3):
                odd = (own & (1 << bit)) != 0
                groups = [
                    jnp.where(odd, groups[g + 1], groups[g]) for g in range(0, len(groups), 2)
                ]
            index = (own >> 3) + NB // 2 - lane
            found = lane_gather(groups[0], index & (NB - 1))
            found = jnp.where(index < 0, 0.0, found)
            found = jnp.where((index >= NB) | (lane == 0), every, found)
            following = pltpu.roll(found, NB - 1, 1)
            found = found - jnp.where(lane == NB - 1, 0.0, following)
            hist_ref[at, (kind + 1) * NB : (kind + 2) * NB] = found.astype(LOW)

    @pl.loop(0, rows // (2 * block))
    def _(step):
        for part in range(2):
            some((2 * step + part) * block)


def layer_kernel(
    length_ref, tok_ref, wq_ref, wk_ref, wv_ref, rel_ref, corner_ref,
    wo_ref, cot_ref, wi_ref, wu_ref, bo_ref, ga_ref, sa_ref, bi_ref, bu_ref, gf_ref, sf_ref,
    q_ref, k_ref, qrel_ref, ctx_ref, out_ref, grad_ref, grad_low_ref, small_ref, mat_ref,
    gq_ref, gv_ref, gkrel_ref, step_ref, col_ref, owi_ref, owu_ref,
    hidden_ref, active_ref, mid_low_ref, inner_low_ref, v_ref, krel_ref, attend_ref, tq_ref, tk_ref, idx_ref, row_ref, log_ref,
    own, inner, outer, normed_ref, scale_ref, sums_ref, gc_ref, hist_ref, gv_sum, block_ref,
    in_send, in_recv, out_send, out_recv, block_sem, *rest,
    bits,
):
    slots = tok_ref.shape[0]
    chunks = slots // HOP
    heads, wide = q_ref.shape[0], q_ref.shape[1]
    blocks = wide // LANES
    per = LANES // HOP
    scale = (7.0 * HEAD) ** (-0.5)
    line = Line("head", own, inner, outer, (in_send, in_recv, out_send, out_recv))
    barrier = pltpu.get_barrier_semaphore()
    line.greet(barrier)
    greet_batch(barrier, bits)
    share = owi_ref.shape[1] // RELAYS
    rounds = share // STRIP
    relays = []
    for at in range(2 * RELAYS):
        work, *got = rest[at * (bits + 1) : (at + 1) * (bits + 1)]
        first = 2 * RELAYS * (bits + 1) + 3 * at
        sems = rest[first : first + 3]
        start = at // 2 * share
        out = (owi_ref, owu_ref)[at % 2].at[:, start : start + share]
        relays.append(Rounds(batch_orders(bits)[at % 2], work, got, out, rounds, *sems))
    sums_ref[...] = jnp.zeros_like(sums_ref)
    gv_sum[...] = jnp.zeros_like(gv_sum)
    gkrel_ref[...] = jnp.zeros_like(gkrel_ref)
    attention_setup(tok_ref, wq_ref, wk_ref, wv_ref, rel_ref, corner_ref,
                    q_ref, k_ref, v_ref, krel_ref, qrel_ref, tq_ref, tk_ref, idx_ref, col_ref, row_ref)
    pl.semaphore_wait(barrier, line.greeted() + bits)
    root = 0.5**0.5
    bell = (0.5 / jnp.pi) ** 0.5

    def forward_head(big, head):
        attention_block(big, head, length_ref[0], q_ref, k_ref, v_ref, tq_ref, tk_ref, idx_ref, log_ref,
                        attend_ref, ctx_ref)

    def put(c, value):
        for part in range(PAIR // HOP):
            own[c * (PAIR // HOP) + part] = value[part * HOP : (part + 1) * HOP]

    def got(u):
        first = line.total(u * (PAIR // HOP))
        return jnp.concatenate([outer[first + part] for part in range(PAIR // HOP)], axis=0)

    def project(c):
        at = span(c * PAIR, PAIR)
        context = jnp.concatenate([ctx_ref[head, at, :] for head in range(heads)], axis=1)
        put(c, dot_nn(context, wo_ref[...]))

    def after_attention(c, u):
        at = span(c * PAIR, PAIR)
        normed, scaling = centre(got(u) + bo_ref[...] + tok_ref[at, :].astype(FULL))
        normed_ref[at, :] = normed
        scale_ref[at, :] = scaling
        hidden_low = (normed * ga_ref[...] + sa_ref[...]).astype(LOW)
        hidden_ref[at, :] = hidden_low
        pre = dot_nn(hidden_low, wi_ref[...]) + bi_ref[...]
        grad_ref[at, :] = pre
        active = (pre * (1.0 + lax.erf(pre * root)) * 0.5).astype(LOW)
        active_ref[at, :] = active
        put(c, dot_nn(active, wu_ref[...]))

    def after_ffn(c, u):
        at = span(c * PAIR, PAIR)
        hidden = normed_ref[at, :] * ga_ref[...] + sa_ref[...]
        normed, scaling = centre(got(u) + bu_ref[...] + hidden)
        out_ref[at, :] = (normed * gf_ref[...] + sf_ref[...]).astype(LOW)
        upstream = cot_ref[at, :].astype(FULL)
        grad_mid = norm_inward(upstream * gf_ref[...], normed, scaling)
        sums_ref[4] += fold_rows(grad_mid)
        sums_ref[5] += fold_rows(upstream * normed)
        sums_ref[6] += fold_rows(upstream)
        pre = grad_ref[at, :]
        grad_ref[at, :] = grad_mid
        mid_low = grad_mid.astype(LOW)
        mid_low_ref[at, :] = mid_low
        grad_active = dot_nt(mid_low, wu_ref[...])
        slope = (1.0 + lax.erf(pre * root)) * 0.5 + pre * jnp.exp(-0.5 * pre * pre) * bell
        inner_low = (grad_active * slope).astype(LOW)
        sums_ref[3] += fold_rows(inner_low.astype(FULL))
        inner_low_ref[at, :] = inner_low
        put(c, dot_nt(inner_low, wi_ref[...]))

    def after_hidden(c, u):
        at = span(c * PAIR, PAIR)
        upstream = got(u) + grad_ref[at, :]
        normed = normed_ref[at, :]
        grad_attn = norm_inward(upstream * ga_ref[...], normed, scale_ref[at, :])
        sums_ref[0] += fold_rows(grad_attn)
        sums_ref[1] += fold_rows(upstream * normed)
        sums_ref[2] += fold_rows(upstream)
        grad_ref[at, :] = grad_attn
        grad_low_ref[at, :] = grad_attn.astype(LOW)

    def backward_block(big):
        rows = min(LANES, slots - big * LANES)
        some = slice(big * LANES, big * LANES + rows)
        value = dot_nt(grad_low_ref[some, :], wo_ref[...]).astype(LOW)
        for head in range(heads):
            gc_ref[head, :rows, :] = value[:, head * HEAD : (head + 1) * HEAD]

    def block_copy(big, head, rows):
        buffer = lax.rem(head, 2)
        return pltpu.make_async_copy(
            block_ref.at[buffer, :rows, :],
            mat_ref.at[head, pl.ds(big * LANES, rows), :],
            block_sem.at[buffer],
        )

    def backward_head(big, head):
        rows = min(LANES, slots - big * LANES)
        some = slice(big * LANES, big * LANES + rows)

        @pl.when(head >= 2)
        def _():
            block_copy(big, head - 2, rows).wait()

        if big > 0:

            @pl.when(head < 2)
            def _():
                block_copy(big - 1, head + 2, LANES).wait()

        gc = gc_ref[head, :rows, :]
        grad_attend = dot_nt(gc, v_ref[head])
        mean = jnp.sum(gc.astype(FULL) * ctx_ref[head, some, :].astype(FULL), axis=-1, keepdims=True)
        attend = attend_ref[head, some, :]
        mat = block_ref.at[lax.rem(head, 2), :rows, :]
        mat[...] = (attend.astype(FULL) * (grad_attend - mean)).astype(LOW)
        block_copy(big, head, rows).start()
        gv_sum[head] += dot_tn(attend, gc)
        bucket_sums(big, rows, mat, step_ref, col_ref, tq_ref, hist_ref)
        hist = hist_ref[:rows, :]
        gq = dot_nn(mat[...], k_ref[head]) + dot_nn(hist, krel_ref[head])
        gq_ref[head, some, :] = (gq * scale).astype(LOW)
        gkrel_ref[head] += dot_tn(hist, q_ref[head, some, :])

    def relay_begin(at, number):
        start = at // 2 * share + number * STRIP
        lanes = slice(start, start + STRIP)
        if at % 2 == 0:
            value = dot_tn(hidden_ref[...], inner_low_ref[:, lanes])
        else:
            value = dot_tn(mid_low_ref[...], active_ref[:, lanes])
        relays[at].begin(number, value)

    for head in range(heads):
        forward_head(0, head)
    count = 3 * chunks
    ratio = PAIR // HOP
    first_back = 2 * chunks + line.trip + per
    last_slot = first_back + (blocks - 1) * per + heads
    tasks = {}

    def add(when, task):
        tasks.setdefault(when, []).append(task)

    after = 2 * chunks + line.trip
    for number in range(rounds):
        for at in range(2 * RELAYS):
            base = after + 5 * number + at
            add(base, lambda at=at, number=number: relay_begin(at, number))
            for stage in range(bits):
                when = base + 1 + 2 * stage
                add(when, lambda at=at, stage=stage, number=number: relays[at].turn(stage, number))

    @pl.loop(0, max(count + line.trip, last_slot, max(tasks) + 1))
    def _(slot):
        @pl.when((slot < chunks) & (lax.rem(slot, ratio) == 0))
        def _():
            project(slot // ratio)

        line.step(slot, count)
        ahead = slot + per
        for big in range(1, blocks):

            @pl.when(ahead // per == big)
            def _(big=big):
                forward_head(big, lax.rem(ahead, per))

        done = slot - line.trip - (ratio - 1)
        pair = done // ratio
        ready = (done >= 0) & (lax.rem(done + ratio, ratio) == 0)
        pairs = chunks // ratio

        @pl.when(ready & (pair < pairs))
        def _():
            after_attention(pair, pair)

        @pl.when(ready & (pair >= pairs) & (pair < 2 * pairs))
        def _():
            after_ffn(pair - pairs, pair)

        @pl.when(ready & (pair >= 2 * pairs) & (pair < 3 * pairs))
        def _():
            after_hidden(pair - 2 * pairs, pair)

        @pl.when(slot == 2 * chunks)
        def _():
            make_steps(step_ref, col_ref, slots)

        for when in sorted(tasks):

            @pl.when(slot == when)
            def _(when=when):
                for task in tasks[when]:
                    task()

        since = slot - first_back
        for big in range(blocks):

            @pl.when((since >= 0) & (since // per == big))
            def _(big=big):
                at_head = lax.rem(since, per)

                @pl.when(at_head == 0)
                def _():
                    backward_block(big)

                backward_head(big, at_head)

    for at in range(7):
        small_ref[at : at + 1, :] = jnp.sum(sums_ref[at], axis=0, keepdims=True)
    small_ref[7:8, :] = jnp.zeros_like(small_ref[7:8, :])
    for head in range(heads):
        gv_ref[head] = gv_sum[head, :slots, :].astype(LOW)
        gkrel_ref[head] = gkrel_ref[head] * scale
    for head in range(heads - 2, heads):
        block_copy(blocks - 1, head, slots - (blocks - 1) * LANES).wait()
    line.drain(count)


def layer(
    tokens, length, corners, w_query, w_key, w_value, rel, w_output, cotangent, w_inner, w_outer, vectors, batch
):
    slots, width = tokens.shape
    units = w_inner.shape[1]
    mine = w_query.shape[1]
    heads = mine // HEAD
    wide = -(-slots // LANES) * LANES
    assert units == width and heads == LANES // HOP and slots % PAIR == 0
    vmem = pl.BlockSpec(memory_space=pltpu.VMEM)
    chunks = slots // HOP
    shape = jax.ShapeDtypeStruct
    dma = pltpu.SemaphoreType.DMA
    bits = batch.bit_length() - 1
    assert 1 << bits == batch
    part = width // batch
    relay = [pltpu.VMEM((2,) * (bits - s) + (part, STRIP), FULL) for s in range(bits + 1)]
    return pl.pallas_call(
        functools.partial(layer_kernel, bits=bits),
        out_shape=(
            shape((heads, wide, HEAD), LOW),
            shape((heads, wide, HEAD), LOW),
            shape((heads, 3 * NB, HEAD), LOW),
            shape((heads, slots, HEAD), LOW),
            shape((slots, width), LOW),
            shape((slots, width), FULL),
            shape((slots, width), LOW),
            shape((8, width), FULL),
            shape((heads, slots, wide), LOW),
            shape((heads, slots, HEAD), LOW),
            shape((heads, slots, HEAD), LOW),
            shape((heads, 3 * NB, HEAD), FULL),
            shape((2, wide, BOX_STEP * NB), LOW),
            shape((2, wide, LANES), jnp.int32),
            shape((part, units), FULL),
            shape((part, units), FULL),
        ),
        in_specs=[pl.BlockSpec(memory_space=pltpu.SMEM)] + [vmem] * 17,
        out_specs=(vmem,) * 8 + (pl.BlockSpec(memory_space=pl.ANY),) + (vmem,) * 7,
        scratch_shapes=[
            pltpu.VMEM((slots, width), LOW),
            pltpu.VMEM((slots, units), LOW),
            pltpu.VMEM((slots, width), LOW),
            pltpu.VMEM((slots, units), LOW),
            pltpu.VMEM((heads, wide, HEAD), LOW),
            pltpu.VMEM((heads, 3 * NB, HEAD), LOW),
            pltpu.VMEM((heads, slots, wide), LOW),
            pltpu.VMEM((heads, slots, 3 * NB), FULL),
            pltpu.VMEM((heads, wide, 3 * NB), FULL),
            pltpu.VMEM((2, wide // LANES, wide, LANES), jnp.int32),
            pltpu.VMEM((2, wide), jnp.int32),
            pltpu.VMEM((LANES, wide), FULL),
            pltpu.VMEM((chunks, HOP, width), FULL),
            pltpu.VMEM((chunks, HOP, width), FULL),
            pltpu.VMEM((2 * chunks, HOP, width), FULL),
            pltpu.VMEM((slots, width), FULL),
            pltpu.VMEM((slots, 1), FULL),
            pltpu.VMEM((7, 8, width), FULL),
            pltpu.VMEM((heads, LANES, HEAD), LOW),
            pltpu.VMEM((LANES, 3 * NB), LOW),
            pltpu.VMEM((heads, wide, HEAD), FULL),
            pltpu.VMEM((2, LANES, wide), LOW),
            dma((chunks,)),
            dma((chunks,)),
            dma((2 * chunks,)),
            dma((2 * chunks,)),
            dma((2,)),
        ]
        + relay * (2 * RELAYS)
        + [dma((bits,)), dma((bits,)), pltpu.SemaphoreType.REGULAR((bits,))] * (2 * RELAYS),
        compiler_params=pltpu.CompilerParams(
            vmem_limit_bytes=VMEM_LIMIT, collective_id=1, has_side_effects=True
        ),
        name="layer",
    )(length, tokens, w_query, w_key, w_value, rel, corners,
      w_output, cotangent, w_inner, w_outer, *[v.reshape(1, -1) for v in vectors])


class Halving:
    def __init__(self, order, source, got, out, send, recv):
        self.order, self.source, self.got, self.out = order, source, got, out
        self.send, self.recv = send, recv
        self.b = lax.axis_index("batch")

    def part(self, stage, flip):
        bit = self.order[stage]
        rest = sorted(self.order[stage:], reverse=True)
        mine = (self.b >> bit) & 1
        pick = 1 - mine if flip else mine
        return tuple(pick if k == bit else slice(None) for k in rest)

    def copy(self, stage):
        source = self.source if stage == 0 else self.got[stage - 1]
        return pltpu.make_async_remote_copy(
            src_ref=source.at[self.part(stage, True)],
            dst_ref=self.got[stage],
            send_sem=self.send.at[stage],
            recv_sem=self.recv.at[stage],
            device_id={"batch": self.b ^ (1 << self.order[stage])},
            device_id_type=MESH,
        )

    def start(self):
        self.copy(0).start()

    def turn(self, stage):
        self.copy(stage).wait_recv()
        kept = self.source if stage == 0 else self.got[stage - 1]
        value = kept[self.part(stage, False)] + self.got[stage][...]
        if stage == 0:
            self.copy(0).wait_send()
        if stage + 1 < len(self.order):
            self.got[stage][...] = value
            self.copy(stage + 1).start()
        else:
            self.out[...] = value

    def drain(self):
        for stage in range(1, len(self.order)):
            self.copy(stage).wait_send()


def gradient_kernel(
    tok_ref, wq_ref, wk_ref, wv_ref, rel_ref,
    q_ref, k_ref, qrel_ref, ctx_ref, grad_ref, grad_low_ref, small_ref, mat_ref,
    gq_ref, gv_ref, gkrel_ref, step_ref, col_ref,
    gtok_ref, owq_ref, owk_ref, owv_ref, owo_ref, orel_ref, osmall_ref,
    own, inner, outer, turned_ref, fold_ref, hist_ref, gk_ref, gk_low_ref, gqrel_sum,
    work_ref, rel_work, rel_sum, rel_own, rel_in, rel_out, rel_all, small_sum, small_got,
    *rest,
    bits, pieces,
):
    jobs_all = len(pieces) + 2
    got = [rest[at * bits : (at + 1) * bits] for at in range(jobs_all)]
    (in_send, in_recv, out_send, out_recv, rin_send, rin_recv, rout_send, rout_recv,
     piece_send, piece_recv, back_send, back_recv, small_send, small_recv) = rest[jobs_all * bits :]
    slots, width = tok_ref.shape
    chunks = slots // HOP
    heads, wide = q_ref.shape[0], q_ref.shape[1]
    blocks = wide // LANES
    per = LANES // HOP
    scale = (7.0 * HEAD) ** (-0.5)
    line = Line("head", own, inner, outer, (in_send, in_recv, out_send, out_recv))
    rel_line = Line("head", rel_own, rel_in, rel_out, (rin_send, rin_recv, rout_send, rout_recv), 1)
    b = lax.axis_index("batch")
    barrier = pltpu.get_barrier_semaphore()
    line.greet(barrier)
    greet_batch(barrier, bits)
    orders = batch_orders(bits)
    outs = (owq_ref, owk_ref, owv_ref, owo_ref)
    jobs = []
    for at, which in enumerate(pieces):
        jobs.append(
            Halving(orders[at % 2], work_ref.at[at], got[at], outs[which], piece_send.at[at], piece_recv.at[at])
        )
    rel_jobs = []
    for side in range(2):
        at = len(pieces) + side
        rel_jobs.append(
            Halving(orders[side], rel_work.at[side], got[at], rel_sum.at[side], piece_send.at[at], piece_recv.at[at])
        )

    def heads_of(ref):
        return jnp.concatenate([ref[head] for head in range(heads)], axis=1)

    def make(at):
        which = pieces[at]
        if which == 0:
            value = dot_tn(tok_ref[...], heads_of(gq_ref)) + dot_tn(rel_ref[...], rel_low(1))
        elif which == 1:
            value = dot_tn(tok_ref[...], gk_ref[...]) + dot_tn(rel_ref[...], rel_low(0))
        elif which == 2:
            value = dot_tn(tok_ref[...], heads_of(gv_ref))
        else:
            value = dot_tn(grad_low_ref[...], heads_of(ctx_ref))
        target = work_ref.at[at]
        target[...] = value.reshape(target.shape)
        jobs[at].start()

    def rel_low(side):
        return heads_of(gqrel_sum if side else gkrel_ref).astype(LOW)

    def rel_start(side):
        if side:
            for head in range(heads):
                gqrel_sum[head] = gqrel_sum[head] * scale
        target = rel_work.at[side]
        target[...] = heads_of(gqrel_sum if side else gkrel_ref).reshape(target.shape)
        rel_jobs[side].start()

    def small_copy(k):
        return pltpu.make_async_remote_copy(
            src_ref=small_sum.at[k],
            dst_ref=small_got.at[k],
            send_sem=small_send.at[k],
            recv_sem=small_recv.at[k],
            device_id={"batch": b ^ (1 << k)},
            device_id_type=MESH,
        )

    def small_turn(k):
        small_copy(k).wait_recv()
        value = small_sum[k] + small_got[k]
        if k + 1 < bits:
            small_sum[k + 1] = value
            small_copy(k + 1).start()
        else:
            osmall_ref[...] = value

    def back_copy(half, turn):
        sequence = orders[half][::-1]
        region = tuple(
            slice(None) if k in sequence[:turn] else (b >> k) & 1 for k in range(bits - 1, -1, -1)
        )
        target = rel_all.at[(half,) + region]
        return pltpu.make_async_remote_copy(
            src_ref=target,
            dst_ref=target,
            send_sem=back_send.at[half, turn],
            recv_sem=back_recv.at[half, turn],
            device_id={"batch": b ^ (1 << sequence[turn])},
            device_id_type=MESH,
        )

    def back_turn(half, turn):
        back_copy(half, turn).wait_recv()
        if turn + 1 < bits:
            back_copy(half, turn + 1).start()

    def rel_meet():
        value = dot_nt(rel_sum[0].astype(LOW), wk_ref[...]) + dot_nt(rel_sum[1].astype(LOW), wq_ref[...])
        size = width // 2
        for half in range(2):
            rel_own[half] = value[:, half * size : (half + 1) * size]

    def rel_step(hop):
        rel_line.step(jnp.int32(hop), 2)
        half = hop - rel_line.trip
        if half >= 0:
            region = tuple((b >> k) & 1 for k in range(bits - 1, -1, -1))
            rel_all[(half,) + region] = rel_out[half]
            back_copy(half, 0).start()

    def column_head(big, head):
        rows = min(LANES, slots - big * LANES)
        some = slice(big * LANES, big * LANES + rows)
        lanes = slice(big * LANES, (big + 1) * LANES)
        for chunk in range(blocks):
            there = slice(chunk * LANES, min((chunk + 1) * LANES, slots))
            turned_ref[:, there] = mat_ref[head, there, lanes].T
        bucket_sums(big, rows, turned_ref.at[:rows, :], step_ref, col_ref, fold_ref, hist_ref)
        hist = hist_ref[:rows, :]
        gk = dot_nn(turned_ref[:rows, :], q_ref[head]) + dot_nn(hist, qrel_ref[head])
        gk_low_ref[head, :rows, :] = (gk * scale).astype(LOW)
        gqrel_sum[head] += dot_tn(hist, k_ref[head, some, :])

    def inputs_block(big):
        rows = min(LANES, slots - big * LANES)
        some = slice(big * LANES, big * LANES + rows)
        gk = jnp.concatenate([gk_low_ref[head, :rows, :] for head in range(heads)], axis=1)
        gk_ref[some, :] = gk
        gq = jnp.concatenate([gq_ref[head, some, :] for head in range(heads)], axis=1)
        gv = jnp.concatenate([gv_ref[head, some, :] for head in range(heads)], axis=1)
        value = dot_nt(gq, wq_ref[...]) + dot_nt(gk, wk_ref[...]) + dot_nt(gv, wv_ref[...])
        for part in range(rows // HOP):
            own[big * per + part] = value[part * HOP : (part + 1) * HOP]

    gqrel_sum[...] = jnp.zeros_like(gqrel_sum)
    if wide > slots:
        turned_ref[:, slots:] = jnp.zeros((LANES, wide - slots), LOW)
    small_sum[0] = small_ref[...]
    pl.semaphore_wait(barrier, line.greeted() + bits)
    small_copy(0).start()
    rel_start(0)

    @pl.loop(0, heads)
    def _(head):
        column_head(0, head)

    inputs_block(0)

    tasks = {}

    def add(slot, task):
        tasks.setdefault(slot, []).append(task)

    ended = 2 * (blocks - 1)
    add(ended, lambda: rel_start(1))
    for at in range(2):
        add(at, lambda at=at: make(at))
        add(ended + at, lambda at=at: make(2 + at))
        for stage in range(bits):
            after = 4 * stage if stage < 2 else 2 + 2 * stage
            add(2 + at + after, lambda at=at, stage=stage: jobs[at].turn(stage))
            add(ended + 2 + at + after, lambda at=at, stage=stage: jobs[2 + at].turn(stage))
    for stage in range(bits):
        add(2 + 2 * stage, lambda stage=stage: rel_jobs[0].turn(stage))
        add(3 + 2 * stage, lambda stage=stage: small_turn(stage))
        add(ended + 2 + 2 * stage, lambda stage=stage: rel_jobs[1].turn(stage))
    met = ended + 2 * bits
    add(met, rel_meet)
    for hop in range(rel_line.trip + 2):
        add(met + 1 * hop, lambda hop=hop: rel_step(hop))
    for half in range(2):
        for turn in range(bits):
            add(met + 1 * (rel_line.trip + half) + 2 * (1 + turn), lambda half=half, turn=turn: back_turn(half, turn))
    total = chunks + line.trip

    @pl.loop(0, max(total, max(tasks) + 1))
    def _(slot):
        line.step(slot, chunks)
        for big in range(1, blocks):

            @pl.when(slot // 2 + 1 == big)
            def _(big=big):
                late = lax.rem(slot, 2)

                @pl.loop(0, heads // 2)
                def _(head):
                    column_head(big, late * (heads // 2) + head)

                @pl.when(late == 1)
                def _():
                    inputs_block(big)

        for when in sorted(tasks):

            @pl.when(slot == when)
            def _(when=when):
                for task in tasks[when]:
                    task()

        done = slot - line.trip

        @pl.when((done >= 0) & (done < chunks))
        def _():
            at = span(done * HOP, HOP)
            gtok_ref[at, :] = (outer[done] + grad_ref[at, :]).astype(LOW)

    whole = (slice(None),) * (bits + 1)
    for half in range(2):
        size = width // 2
        orel_ref[whole + (slice(half * size, (half + 1) * size),)] = rel_all[half]
    line.drain(chunks)
    rel_line.drain(2)
    for job in jobs + rel_jobs:
        job.drain()
    for k in range(bits):
        small_copy(k).wait_send()
        for half in range(2):
            back_copy(half, k).wait_send()


def gradients(tokens, w_query, w_key, w_value, rel, kept, batch):
    slots, width = tokens.shape
    q = kept[0]
    heads, wide = q.shape[:2]
    mine = heads * HEAD
    bits = batch.bit_length() - 1
    assert 1 << bits == batch
    vmem = pl.BlockSpec(memory_space=pltpu.VMEM)
    chunks = slots // HOP
    split = (2,) * bits
    part = width // batch
    rel_part = rel.shape[0] // batch
    assert mine == PIECE
    pieces = [2, 3, 0, 1]
    shape = jax.ShapeDtypeStruct
    got = []
    for _ in pieces:
        got += [pltpu.VMEM((2,) * (bits - 1 - s) + (part, PIECE), FULL) for s in range(bits)]
    for _ in range(2):
        got += [pltpu.VMEM((2,) * (bits - 1 - s) + (rel_part, mine), FULL) for s in range(bits)]
    dma = pltpu.SemaphoreType.DMA
    return pl.pallas_call(
        functools.partial(gradient_kernel, bits=bits, pieces=pieces),
        out_shape=(
            shape((slots, width), LOW),
            shape((part, mine), FULL),
            shape((part, mine), FULL),
            shape((part, mine), FULL),
            shape((part, mine), FULL),
            shape(split + (rel_part, width), FULL),
            shape((8, width), FULL),
        ),
        in_specs=[vmem] * 18,
        out_specs=(vmem,) * 7,
        scratch_shapes=[
            pltpu.VMEM((chunks, HOP, width), FULL),
            pltpu.VMEM((chunks, HOP, width), FULL),
            pltpu.VMEM((chunks, HOP, width), FULL),
            pltpu.VMEM((LANES, wide), LOW),
            pltpu.VMEM((2, 3 * LANES, 3 * NB), FULL),
            pltpu.VMEM((LANES, 3 * NB), LOW),
            pltpu.VMEM((slots, mine), LOW),
            pltpu.VMEM((heads, LANES, HEAD), LOW),
            pltpu.VMEM((heads, 3 * NB, HEAD), FULL),
            pltpu.VMEM((len(pieces),) + split + (part, PIECE), FULL),
            pltpu.VMEM((2,) + split + (rel_part, mine), FULL),
            pltpu.VMEM((2, rel_part, mine), FULL),
            pltpu.VMEM((2, rel_part, width // 2), FULL),
            pltpu.VMEM((2, rel_part, width // 2), FULL),
            pltpu.VMEM((2, rel_part, width // 2), FULL),
            pltpu.VMEM((2,) + split + (rel_part, width // 2), FULL),
            pltpu.VMEM((bits, 8, width), FULL),
            pltpu.VMEM((bits, 8, width), FULL),
        ]
        + got
        + [dma((chunks,))] * 4
        + [dma((2,))] * 4
        + [dma((len(pieces) + 2, bits))] * 2
        + [dma((2, bits))] * 2
        + [dma((bits,))] * 2,
        compiler_params=pltpu.CompilerParams(
            vmem_limit_bytes=VMEM_LIMIT, collective_id=2, has_side_effects=True
        ),
        name="gradients",
    )(tokens, w_query, w_key, w_value, rel, *kept)


def finish_kernel(out, gtok, gwq, gwk, gwv, gwo, gwi, gwu, grel, small, *targets):
    (o_out, o_gtok, o_gwq, o_gwk, o_gwv, o_gwo, o_gwi, o_gwu, o_grel) = targets[:9]
    o_out[...] = out[...]
    o_gtok[...] = gtok[...]
    o_gwq[...] = gwq[...]
    o_gwk[...] = gwk[...]
    o_gwv[...] = gwv[...]
    o_gwo[...] = gwo[...].T
    o_gwi[...] = gwi[...]
    o_gwu[...] = gwu[...].T
    o_grel[...] = grel[...]
    for at, target in enumerate(targets[9:]):
        target[...] = small[at]


def finish(out, gtok, gwq, gwk, gwv, gwo, gwi, gwu, grel, small):
    vmem = pl.BlockSpec(memory_space=pltpu.VMEM)
    shape = jax.ShapeDtypeStruct
    same = lambda a: shape(a.shape, a.dtype)
    turn = lambda a: shape(a.shape[::-1], a.dtype)
    return pl.pallas_call(
        finish_kernel,
        out_shape=(same(out), same(gtok), same(gwq), same(gwk), same(gwv), turn(gwo), same(gwi), turn(gwu), same(grel))
        + (shape(small.shape[1:], FULL),) * 7,
        in_specs=[vmem] * 10,
        out_specs=(vmem,) * 16,
        compiler_params=pltpu.CompilerParams(vmem_limit_bytes=VMEM_LIMIT),
        name="finish",
    )(out, gtok, gwq, gwk, gwv, gwo, gwi, gwu, grel, small)


def shards(
    tokens,
    page_lengths,
    corners,
    w_query,
    w_key,
    w_value,
    w_output,
    b_output,
    gain_attn,
    shift_attn,
    w_inner,
    b_inner,
    w_outer,
    b_outer,
    gain_ffn,
    shift_ffn,
    rel_tables,
    cotangent,
):
    rel = rel_tables.reshape(3 * NB, rel_tables.shape[2])
    vectors = (b_output, gain_attn, shift_attn, b_inner, b_outer, gain_ffn, shift_ffn)
    q, k, qrel, ctx, output, *kept, gwi, gwu = layer(
        tokens, page_lengths, corners, w_query, w_key, w_value, rel,
        w_output, cotangent, w_inner, w_outer, vectors, lax.axis_size("batch"),
    )
    done = gradients(
        tokens, w_query, w_key, w_value, rel, (q, k, qrel, ctx, *kept), lax.axis_size("batch")
    )
    gtok, gwq, gwk, gwv, gwo, grel, small = done
    grel = grel.reshape(rel_tables.shape)
    (output, gtok, gwq, gwk, gwv, gwo, gwi, gwu, grel, gbo, gga, gsa, gbi, gbu, ggf, gsf) = finish(
        output, gtok, gwq, gwk, gwv, gwo, gwi, gwu, grel, small
    )
    return (output, gtok, gwq, gwk, gwv, gwo, gbo, gga, gsa, gwi, gbi, gwu, gbu, ggf, gsf, grel)


def solution(mesh):
    in_specs = (
        P("batch", None),
        P("batch"),
        P(None, "batch"),
        P(None, "head"),
        P(None, "head"),
        P(None, "head"),
        P("head", None),
        P(),
        P(),
        P(),
        P(None, "head"),
        P("head"),
        P("head", None),
        P(),
        P(),
        P(),
        P(),
        P("batch", None),
    )
    out_specs = (
        P("batch", None),
        P("batch", None),
        P("batch", "head"),
        P("batch", "head"),
        P("batch", "head"),
        P("head", "batch"),
        P(),
        P(),
        P(),
        P("batch", "head"),
        P("head"),
        P("head", "batch"),
        P(),
        P(),
        P(),
        P(),
    )
    return jax.shard_map(shards, mesh=mesh, in_specs=in_specs, out_specs=out_specs, check_vma=False)
```

```python
import functools

import jax
import jax.numpy as jnp
from jax import lax
from jax.experimental import pallas as pl
from jax.experimental.pallas import tpu as pltpu
from jax.sharding import PartitionSpec as P

HEAD = 64
NB = 128
BOX_STEP = 8
NEG_FILL = -1000000000.0
LANES = 128
HOP = 32
PAIR = 64
LAG = 2
PIECE = 256
STRIP = 128
RELAYS = 2
VMEM_LIMIT = 61 * 1024 * 1024
MESH = pl.DeviceIdType.MESH
LOW = jnp.bfloat16
FULL = jnp.float32


def dot_nn(a, b):
    return lax.dot_general(a, b, (((1,), (0,)), ((), ())), preferred_element_type=FULL)


def dot_nt(a, b):
    return lax.dot_general(a, b, (((1,), (1,)), ((), ())), preferred_element_type=FULL)


def dot_tn(a, b):
    return lax.dot_general(a, b, (((0,), (0,)), ((), ())), preferred_element_type=FULL)


def lane_gather(table, index):
    return jnp.take_along_axis(table, index, axis=1, mode="promise_in_bounds")


def bucket(step):
    return jnp.clip(step, -(NB // 2), NB // 2 - 1) + NB // 2


def span(start, size):
    return pl.ds(pl.multiple_of(start, size), size)


class Line:
    def __init__(self, axis, own, inner, outer, sems, lag=LAG):
        self.axis, self.own, self.inner, self.outer, self.lag = axis, own, inner, outer, lag
        self.in_send, self.in_recv, self.out_send, self.out_recv = sems
        self.ring, self.wide_ring = own.shape[0], outer.shape[0]
        self.n = lax.axis_size(axis)
        me = lax.axis_index(axis)
        left = me < self.n // 2
        self.depth = jnp.where(left, me, self.n - 1 - me)
        self.inward = jnp.where(left, me + 1, me - 1)
        self.outward = jnp.where(self.depth == 0, self.inward, jnp.where(left, me - 1, me + 1))
        self.last = self.n // 2 - 1
        self.trip = self.lag * (self.n - 1)

    def greet(self, barrier):
        pl.semaphore_signal(barrier, inc=1, device_id={self.axis: self.inward}, device_id_type=MESH)

        @pl.when(self.depth > 0)
        def _():
            pl.semaphore_signal(
                barrier, inc=1, device_id={self.axis: self.outward}, device_id_type=MESH
            )

    def greeted(self):
        return jnp.where(self.depth > 0, 2, 1)

    def copy(self, source, target, send, recv, to):
        return pltpu.make_async_remote_copy(
            src_ref=source,
            dst_ref=target,
            send_sem=send,
            recv_sem=recv,
            device_id={self.axis: to},
            device_id_type=MESH,
        )

    def total(self, u):
        return lax.rem(u, self.wide_ring)

    def out_copy(self, u):
        o = self.total(u)
        return self.copy(
            self.outer.at[o], self.outer.at[o], self.out_send.at[o], self.out_recv.at[o], self.outward
        )

    def in_copy(self, c, source):
        return self.copy(
            source, self.inner.at[c], self.in_send.at[c], self.in_recv.at[c], self.inward
        )

    def send_in(self, u, c, source):
        @pl.when(self.depth < self.last)
        def _():
            self.in_copy(c, source).start()

        @pl.when(self.depth == self.last)
        def _():
            o = self.total(u)
            self.copy(
                source, self.outer.at[o], self.in_send.at[c], self.out_recv.at[o], self.inward
            ).start()

    def step(self, slot, count):
        here = slot - self.lag * self.depth

        @pl.when((here >= 0) & (here < count))
        def _():
            u = here
            c = lax.rem(u, self.ring)

            @pl.when(self.depth == 0)
            def _():
                self.send_in(u, c, self.own.at[c])

            @pl.when(self.depth > 0)
            def _():
                @pl.when(u >= self.ring)
                def _():
                    self.out_copy(u - self.ring).wait_send()

                self.in_copy(c, self.own.at[c]).wait_recv()
                self.inner[c] += self.own[c]
                self.send_in(u, c, self.inner.at[c])

        back = slot - self.lag * (self.n - 1 - self.depth)

        @pl.when((back >= 0) & (back < count))
        def _():
            u = back
            c = lax.rem(u, self.ring)
            self.in_copy(c, self.own.at[c]).wait_send()
            self.out_copy(u).wait_recv()

            @pl.when(self.depth == self.last)
            def _():
                self.outer[self.total(u)] += self.inner[c] if self.last > 0 else self.own[c]

            @pl.when(self.depth > 0)
            def _():
                self.out_copy(u).start()

    def drain(self, count):
        @pl.when(self.depth > 0)
        def _():
            @pl.loop(count - self.ring, count)
            def _(u):
                self.out_copy(u).wait_send()


class Rounds:
    def __init__(self, order, work, got, out, rounds, send, recv, credit):
        self.order, self.work, self.got, self.out, self.rounds = order, work, got, out, rounds
        self.send, self.recv, self.credit = send, recv, credit
        self.b = lax.axis_index("batch")

    def partner(self, stage):
        return {"batch": self.b ^ (1 << self.order[stage])}

    def part(self, stage, flip):
        bit = self.order[stage]
        rest = sorted(self.order[stage:], reverse=True)
        mine = (self.b >> bit) & 1
        pick = 1 - mine if flip else mine
        return tuple(pick if k == bit else slice(None) for k in rest)

    def source(self, stage):
        return self.work if stage == 0 else self.got[stage - 1]

    def copy(self, stage):
        return pltpu.make_async_remote_copy(
            src_ref=self.source(stage).at[self.part(stage, True)],
            dst_ref=self.got[stage],
            send_sem=self.send.at[stage],
            recv_sem=self.recv.at[stage],
            device_id=self.partner(stage),
            device_id_type=MESH,
        )

    def start(self, stage, number):
        if number > 0:
            pl.semaphore_wait(self.credit.at[stage], 1)
        self.copy(stage).start()

    def free(self, stage, number):
        if number + 1 < self.rounds:
            pl.semaphore_signal(
                self.credit.at[stage], inc=1, device_id=self.partner(stage), device_id_type=MESH
            )

    def begin(self, number, value):
        self.work[...] = value.reshape(self.work.shape)
        self.start(0, number)

    def turn(self, stage, number):
        self.copy(stage).wait_recv()
        value = self.source(stage)[self.part(stage, False)] + self.got[stage][...]
        last = stage + 1 == len(self.order)
        if last:
            size = value.shape[1]
            self.out[:, number * size : (number + 1) * size] = value
        else:
            self.got[stage][...] = value
        self.copy(stage).wait_send()
        if stage > 0:
            self.free(stage - 1, number)
        if last:
            self.free(stage, number)
        else:
            self.start(stage + 1, number)


def batch_orders(bits):
    return (list(range(bits)), [0] + list(range(bits - 1, 0, -1)))


def greet_batch(barrier, bits):
    b = lax.axis_index("batch")
    for k in range(bits):
        pl.semaphore_signal(barrier, inc=1, device_id={"batch": b ^ (1 << k)}, device_id_type=MESH)


def centre(values):
    average = jnp.mean(values, axis=-1, keepdims=True)
    centered = values - average
    spread = jnp.mean(centered * centered, axis=-1, keepdims=True)
    scaling = lax.rsqrt(spread + 1e-05)
    return centered * scaling, scaling


def norm_inward(scaled, normed, scaling):
    return scaling * (
        scaled
        - jnp.mean(scaled, axis=-1, keepdims=True)
        - normed * jnp.mean(scaled * normed, axis=-1, keepdims=True)
    )


def fold_rows(values):
    rows, width = values.shape
    return jnp.sum(values.reshape(rows // 8, 8, width), axis=0)


def attention_setup(tok_ref, wq_ref, wk_ref, wv_ref, rel_ref, corner_ref,
                    q_ref, k_ref, v_ref, krel_ref, qrel_ref, tq_ref, tk_ref, idx_ref, col_ref, row_ref):
    slots = tok_ref.shape[0]
    heads, wide = q_ref.shape[0], q_ref.shape[1]
    chunks = wide // LANES
    for weight, target in ((wq_ref, q_ref), (wk_ref, k_ref), (wv_ref, v_ref)):
        value = dot_nn(tok_ref[...], weight[...]).astype(LOW)
        for head in range(heads):
            target[head, :slots, :] = value[:, head * HEAD : (head + 1) * HEAD]
            if wide > slots:
                target[head, slots:, :] = jnp.zeros((wide - slots, HEAD), LOW)
    for weight, target in ((wk_ref, krel_ref), (wq_ref, qrel_ref)):
        value = dot_nn(rel_ref[...], weight[...]).astype(LOW)
        for head in range(heads):
            target[head] = value[:, head * HEAD : (head + 1) * HEAD]
    for head in range(heads):
        tq_ref[head] = dot_nt(q_ref[head, :slots, :], krel_ref[head])
        tk_ref[head] = dot_nt(k_ref[head], qrel_ref[head])
    row_ref[...] = jnp.zeros_like(row_ref)
    row_ref[:, :slots] = corner_ref[...]
    for kind in range(2):
        for big in range(chunks):
            here = slice(big * LANES, (big + 1) * LANES)
            col_ref[kind, here, :] = jnp.broadcast_to(row_ref[kind : kind + 1, here], (LANES, LANES)).T

    @pl.loop(0, chunks)
    def _(big):
        at = span(big * LANES, LANES)
        for kind in range(2):
            own = col_ref[kind, at, :]
            for chunk in range(chunks):
                other = row_ref[kind : kind + 1, chunk * LANES : (chunk + 1) * LANES]
                idx_ref[kind, chunk, at, :] = bucket((own - other) >> 3)


def attention_block(big, head, length, q_ref, k_ref, v_ref, tq_ref, tk_ref, idx_ref, log_ref, attend_ref, ctx_ref):
    wide = q_ref.shape[1]
    chunks = wide // LANES
    slots = attend_ref.shape[1]
    scale = (7.0 * HEAD) ** (-0.5)
    rows = min(LANES, slots - big * LANES)
    some = slice(big * LANES, big * LANES + rows)
    slant = lax.broadcasted_iota(jnp.int32, (LANES, LANES), 0) - lax.broadcasted_iota(
        jnp.int32, (LANES, LANES), 1
    )
    log_ref[:rows, :] = dot_nt(q_ref[head, some, :], k_ref[head])
    for chunk in range(chunks):
        there = slice(chunk * LANES, (chunk + 1) * LANES)
        away = (big - chunk) * LANES
        toward = log_ref[:rows, there]
        if abs(big - chunk) >= 2:
            lane = NB - 1 if away > 0 else 0
            toward = toward + tq_ref[head, some, lane : lane + 1]
            lane = NB - 1 - lane
            beside = jnp.broadcast_to(tk_ref[head, there, lane : lane + 1], (LANES, LANES))
        else:
            toward = toward + lane_gather(tq_ref[head, some, :NB], bucket(slant + away)[:rows])
            beside = lane_gather(tk_ref[head, there, :NB], bucket(slant - away))
        for kind in range(2):
            lanes = slice((kind + 1) * NB, (kind + 2) * NB)
            toward = toward + lane_gather(tq_ref[head, some, lanes], idx_ref[kind, chunk, some, :])
            beside = beside + lane_gather(tk_ref[head, there, lanes], idx_ref[kind, big, there, :])
        log_ref[:rows, there] = toward + beside.T[:rows]
    block = 32
    for start in range(0, rows, block):
        at = slice(start, start + block)
        j_at = lax.broadcasted_iota(jnp.int32, (block, wide), 1)
        masked = jnp.where(j_at < length, log_ref[at, :], NEG_FILL)
        peak = jnp.max(masked, axis=-1, keepdims=True)
        grown = jnp.exp((masked - peak) * scale)
        total = jnp.sum(grown, axis=-1, keepdims=True)
        attend_ref[head, big * LANES + start : big * LANES + start + block, :] = (
            grown * (1.0 / total)
        ).astype(LOW)
    ctx_ref[head, some, :] = dot_nn(attend_ref[head, some, :], v_ref[head]).astype(LOW)


def make_steps(step_ref, col_ref, slots):
    wide = step_ref.shape[1]
    block = 64
    if wide > slots:
        step_ref[:, slots:, :] = jnp.zeros_like(step_ref[:, slots:, :])

    @pl.loop(0, slots // block)
    def _(step):
        at = span(step * block, block)
        quotient = lax.broadcasted_iota(jnp.int32, (block, NB), 1) * BOX_STEP
        for kind in range(2):
            own = col_ref[kind, at, :]
            for rest in range(BOX_STEP):
                lanes = slice(rest * NB, (rest + 1) * NB)
                step_ref[kind, at, lanes] = (own <= quotient + rest).astype(FULL).astype(LOW)


def fold_at(kind, r, at):
    return (kind, at, slice(r % 3 * NB, (r % 3 + 1) * NB))


def bucket_sums(big, rows, mat, step_ref, col_ref, fold_ref, hist_ref):
    chunks = step_ref.shape[1] // LANES
    for kind in range(2):
        value = dot_nn(mat[...], step_ref[kind])
        for r in range(BOX_STEP):
            fold_ref[fold_at(kind, r, slice(r // 3 * LANES, r // 3 * LANES + rows))] = value[
                :, r * NB : (r + 1) * NB
            ]
    block = rows

    def some(local):
        at = slice(local, local + block)
        far = slice(big * LANES + local, big * LANES + local + block)
        lane = lax.broadcasted_iota(jnp.int32, (block, NB), 1)
        row = lax.broadcasted_iota(jnp.int32, (block, NB), 0) + local
        part = [mat[at, c * LANES : (c + 1) * LANES].astype(FULL) for c in range(chunks)]
        zero = jnp.zeros((block, LANES), FULL)
        before = part[big - 1] if big >= 1 else zero
        after = part[big + 1] if big + 1 < chunks else zero
        mid = part[big]
        delta = lane - row
        window = jnp.where(delta > NB // 2, before, jnp.where(delta < 1 - NB // 2, after, mid))
        spread = lane_gather(window, (row + NB // 2 - lane) & (NB - 1))
        under = jnp.where(delta <= NB // 2 + 1, before, 0.0) + jnp.where(
            delta <= 1 - NB // 2, mid, 0.0
        )
        over = jnp.where(delta >= NB // 2, mid, 0.0) + jnp.where(delta >= -(NB // 2), after, 0.0)
        for c in range(big - 1):
            under = under + part[c]
        for c in range(big + 2, chunks):
            over = over + part[c]
        under = jnp.sum(under, axis=-1, keepdims=True)
        over = jnp.sum(over, axis=-1, keepdims=True)
        spread = jnp.where(lane == 0, over, jnp.where(lane == NB - 1, under, spread))
        hist_ref[at, 0:NB] = spread.astype(LOW)
        for kind in range(2):
            own = col_ref[kind, far, :]
            groups = [
                fold_ref[fold_at(kind, r, slice(r // 3 * LANES + local, r // 3 * LANES + local + block))]
                for r in range(BOX_STEP)
            ]
            every = groups[-1][:, NB - 1 : NB]
            for bit in range(3):
                odd = (own & (1 << bit)) != 0
                groups = [
                    jnp.where(odd, groups[g + 1], groups[g]) for g in range(0, len(groups), 2)
                ]
            index = (own >> 3) + NB // 2 - lane
            found = lane_gather(groups[0], index & (NB - 1))
            found = jnp.where(index < 0, 0.0, found)
            found = jnp.where((index >= NB) | (lane == 0), every, found)
            following = pltpu.roll(found, NB - 1, 1)
            found = found - jnp.where(lane == NB - 1, 0.0, following)
            hist_ref[at, (kind + 1) * NB : (kind + 2) * NB] = found.astype(LOW)

    some(0)


def layer_kernel(
    length_ref, tok_ref, wq_ref, wk_ref, wv_ref, rel_ref, corner_ref,
    wo_ref, cot_ref, wi_ref, wu_ref, bo_ref, ga_ref, sa_ref, bi_ref, bu_ref, gf_ref, sf_ref,
    q_ref, k_ref, qrel_ref, ctx_ref, out_ref, grad_ref, grad_low_ref, small_ref, mat_ref,
    gq_ref, gv_ref, gkrel_ref, step_ref, col_ref, owi_ref, owu_ref,
    hidden_ref, active_ref, mid_low_ref, inner_low_ref, v_ref, krel_ref, attend_ref, tq_ref, tk_ref, idx_ref, row_ref, log_ref,
    own, inner, outer, normed_ref, scale_ref, sums_ref, gc_ref, hist_ref, gv_sum, block_ref,
    in_send, in_recv, out_send, out_recv, block_sem, *rest,
    bits,
):
    slots = tok_ref.shape[0]
    chunks = slots // HOP
    heads, wide = q_ref.shape[0], q_ref.shape[1]
    blocks = wide // LANES
    per = LANES // HOP
    scale = (7.0 * HEAD) ** (-0.5)
    line = Line("head", own, inner, outer, (in_send, in_recv, out_send, out_recv))
    barrier = pltpu.get_barrier_semaphore()
    line.greet(barrier)
    greet_batch(barrier, bits)
    share = owi_ref.shape[1] // RELAYS
    rounds = share // STRIP
    relays = []
    for at in range(2 * RELAYS):
        work, *got = rest[at * (bits + 1) : (at + 1) * (bits + 1)]
        first = 2 * RELAYS * (bits + 1) + 3 * at
        sems = rest[first : first + 3]
        start = at // 2 * share
        out = (owi_ref, owu_ref)[at % 2].at[:, start : start + share]
        relays.append(Rounds(batch_orders(bits)[at % 2], work, got, out, rounds, *sems))
    sums_ref[...] = jnp.zeros_like(sums_ref)
    gv_sum[...] = jnp.zeros_like(gv_sum)
    gkrel_ref[...] = jnp.zeros_like(gkrel_ref)
    attention_setup(tok_ref, wq_ref, wk_ref, wv_ref, rel_ref, corner_ref,
                    q_ref, k_ref, v_ref, krel_ref, qrel_ref, tq_ref, tk_ref, idx_ref, col_ref, row_ref)
    pl.semaphore_wait(barrier, line.greeted() + bits)
    root = 0.5**0.5
    bell = (0.5 / jnp.pi) ** 0.5

    def forward_head(big, head):
        attention_block(big, head, length_ref[0], q_ref, k_ref, v_ref, tq_ref, tk_ref, idx_ref, log_ref,
                        attend_ref, ctx_ref)

    def put(c, value):
        for part in range(PAIR // HOP):
            own[c * (PAIR // HOP) + part] = value[part * HOP : (part + 1) * HOP]

    def got(u):
        first = line.total(u * (PAIR // HOP))
        return jnp.concatenate([outer[first + part] for part in range(PAIR // HOP)], axis=0)

    def project(c):
        at = span(c * PAIR, PAIR)
        context = jnp.concatenate([ctx_ref[head, at, :] for head in range(heads)], axis=1)
        put(c, dot_nn(context, wo_ref[...]))

    def after_attention(c, u):
        at = span(c * PAIR, PAIR)
        normed, scaling = centre(got(u) + bo_ref[...] + tok_ref[at, :].astype(FULL))
        normed_ref[at, :] = normed
        scale_ref[at, :] = scaling
        hidden_low = (normed * ga_ref[...] + sa_ref[...]).astype(LOW)
        hidden_ref[at, :] = hidden_low
        pre = dot_nn(hidden_low, wi_ref[...]) + bi_ref[...]
        grad_ref[at, :] = pre
        active = (pre * (1.0 + lax.erf(pre * root)) * 0.5).astype(LOW)
        active_ref[at, :] = active
        put(c, dot_nn(active, wu_ref[...]))

    def after_ffn(c, u):
        at = span(c * PAIR, PAIR)
        hidden = normed_ref[at, :] * ga_ref[...] + sa_ref[...]
        normed, scaling = centre(got(u) + bu_ref[...] + hidden)
        out_ref[at, :] = (normed * gf_ref[...] + sf_ref[...]).astype(LOW)
        upstream = cot_ref[at, :].astype(FULL)
        grad_mid = norm_inward(upstream * gf_ref[...], normed, scaling)
        sums_ref[4] += fold_rows(grad_mid)
        sums_ref[5] += fold_rows(upstream * normed)
        sums_ref[6] += fold_rows(upstream)
        pre = grad_ref[at, :]
        grad_ref[at, :] = grad_mid
        mid_low = grad_mid.astype(LOW)
        mid_low_ref[at, :] = mid_low
        grad_active = dot_nt(mid_low, wu_ref[...])
        slope = (1.0 + lax.erf(pre * root)) * 0.5 + pre * jnp.exp(-0.5 * pre * pre) * bell
        inner_low = (grad_active * slope).astype(LOW)
        sums_ref[3] += fold_rows(inner_low.astype(FULL))
        inner_low_ref[at, :] = inner_low
        put(c, dot_nt(inner_low, wi_ref[...]))

    def after_hidden(c, u):
        at = span(c * PAIR, PAIR)
        upstream = got(u) + grad_ref[at, :]
        normed = normed_ref[at, :]
        grad_attn = norm_inward(upstream * ga_ref[...], normed, scale_ref[at, :])
        sums_ref[0] += fold_rows(grad_attn)
        sums_ref[1] += fold_rows(upstream * normed)
        sums_ref[2] += fold_rows(upstream)
        grad_ref[at, :] = grad_attn
        grad_low_ref[at, :] = grad_attn.astype(LOW)

    def backward_block(big):
        rows = min(LANES, slots - big * LANES)
        some = slice(big * LANES, big * LANES + rows)
        value = dot_nt(grad_low_ref[some, :], wo_ref[...]).astype(LOW)
        for head in range(heads):
            gc_ref[head, :rows, :] = value[:, head * HEAD : (head + 1) * HEAD]

    def block_copy(big, head, rows):
        buffer = lax.rem(head, 2)
        return pltpu.make_async_copy(
            block_ref.at[buffer, :rows, :],
            mat_ref.at[head, pl.ds(big * LANES, rows), :],
            block_sem.at[buffer],
        )

    def backward_head(big, head):
        rows = min(LANES, slots - big * LANES)
        some = slice(big * LANES, big * LANES + rows)

        @pl.when(head >= 2)
        def _():
            block_copy(big, head - 2, rows).wait()

        if big > 0:

            @pl.when(head < 2)
            def _():
                block_copy(big - 1, head + 2, LANES).wait()

        gc = gc_ref[head, :rows, :]
        grad_attend = dot_nt(gc, v_ref[head])
        mean = jnp.sum(gc.astype(FULL) * ctx_ref[head, some, :].astype(FULL), axis=-1, keepdims=True)
        attend = attend_ref[head, some, :]
        mat = block_ref.at[lax.rem(head, 2), :rows, :]
        mat[...] = (attend.astype(FULL) * (grad_attend - mean)).astype(LOW)
        block_copy(big, head, rows).start()
        gv_sum[head] += dot_tn(attend, gc)
        bucket_sums(big, rows, mat, step_ref, col_ref, tq_ref, hist_ref)
        hist = hist_ref[:rows, :]
        gq = dot_nn(mat[...], k_ref[head]) + dot_nn(hist, krel_ref[head])
        gq_ref[head, some, :] = (gq * scale).astype(LOW)
        gkrel_ref[head] += dot_tn(hist, q_ref[head, some, :])

    def relay_begin(at, number):
        start = at // 2 * share + number * STRIP
        lanes = slice(start, start + STRIP)
        if at % 2 == 0:
            value = dot_tn(hidden_ref[...], inner_low_ref[:, lanes])
        else:
            value = dot_tn(mid_low_ref[...], active_ref[:, lanes])
        relays[at].begin(number, value)

    for head in range(heads):
        forward_head(0, head)
    count = 3 * chunks
    ratio = PAIR // HOP
    first_back = 2 * chunks + line.trip + per
    last_slot = first_back + (blocks - 1) * per + heads
    tasks = {}

    def add(when, task):
        tasks.setdefault(when, []).append(task)

    after = 2 * chunks + line.trip
    for number in range(rounds):
        for at in range(2 * RELAYS):
            base = after + 5 * number + at
            add(base, lambda at=at, number=number: relay_begin(at, number))
            for stage in range(bits):
                when = base + 1 + 2 * stage
                add(when, lambda at=at, stage=stage, number=number: relays[at].turn(stage, number))

    @pl.loop(0, max(count + line.trip, last_slot, max(tasks) + 1))
    def _(slot):
        @pl.when((slot < chunks) & (lax.rem(slot, ratio) == 0))
        def _():
            project(slot // ratio)

        line.step(slot, count)
        ahead = slot + per
        for big in range(1, blocks):

            @pl.when(ahead // per == big)
            def _(big=big):
                forward_head(big, lax.rem(ahead, per))

        done = slot - line.trip - (ratio - 1)
        pair = done // ratio
        ready = (done >= 0) & (lax.rem(done + ratio, ratio) == 0)
        pairs = chunks // ratio

        @pl.when(ready & (pair < pairs))
        def _():
            after_attention(pair, pair)

        @pl.when(ready & (pair >= pairs) & (pair < 2 * pairs))
        def _():
            after_ffn(pair - pairs, pair)

        @pl.when(ready & (pair >= 2 * pairs) & (pair < 3 * pairs))
        def _():
            after_hidden(pair - 2 * pairs, pair)

        @pl.when(slot == 2 * chunks)
        def _():
            make_steps(step_ref, col_ref, slots)

        for when in sorted(tasks):

            @pl.when(slot == when)
            def _(when=when):
                for task in tasks[when]:
                    task()

        since = slot - first_back
        for big in range(blocks):

            @pl.when((since >= 0) & (since // per == big))
            def _(big=big):
                at_head = lax.rem(since, per)

                @pl.when(at_head == 0)
                def _():
                    backward_block(big)

                backward_head(big, at_head)

    for at in range(7):
        small_ref[at : at + 1, :] = jnp.sum(sums_ref[at], axis=0, keepdims=True)
    small_ref[7:8, :] = jnp.zeros_like(small_ref[7:8, :])
    for head in range(heads):
        gv_ref[head] = gv_sum[head, :slots, :].astype(LOW)
        gkrel_ref[head] = gkrel_ref[head] * scale
    for head in range(heads - 2, heads):
        block_copy(blocks - 1, head, slots - (blocks - 1) * LANES).wait()
    line.drain(count)


def layer(
    tokens, length, corners, w_query, w_key, w_value, rel, w_output, cotangent, w_inner, w_outer, vectors, batch
):
    slots, width = tokens.shape
    units = w_inner.shape[1]
    mine = w_query.shape[1]
    heads = mine // HEAD
    wide = -(-slots // LANES) * LANES
    assert units == width and heads == LANES // HOP and slots % PAIR == 0
    vmem = pl.BlockSpec(memory_space=pltpu.VMEM)
    chunks = slots // HOP
    shape = jax.ShapeDtypeStruct
    dma = pltpu.SemaphoreType.DMA
    bits = batch.bit_length() - 1
    assert 1 << bits == batch
    part = width // batch
    relay = [pltpu.VMEM((2,) * (bits - s) + (part, STRIP), FULL) for s in range(bits + 1)]
    return pl.pallas_call(
        functools.partial(layer_kernel, bits=bits),
        out_shape=(
            shape((heads, wide, HEAD), LOW),
            shape((heads, wide, HEAD), LOW),
            shape((heads, 3 * NB, HEAD), LOW),
            shape((heads, slots, HEAD), LOW),
            shape((slots, width), LOW),
            shape((slots, width), FULL),
            shape((slots, width), LOW),
            shape((8, width), FULL),
            shape((heads, slots, wide), LOW),
            shape((heads, slots, HEAD), LOW),
            shape((heads, slots, HEAD), LOW),
            shape((heads, 3 * NB, HEAD), FULL),
            shape((2, wide, BOX_STEP * NB), LOW),
            shape((2, wide, LANES), jnp.int32),
            shape((part, units), FULL),
            shape((part, units), FULL),
        ),
        in_specs=[pl.BlockSpec(memory_space=pltpu.SMEM)] + [vmem] * 17,
        out_specs=(vmem,) * 8 + (pl.BlockSpec(memory_space=pl.ANY),) + (vmem,) * 7,
        scratch_shapes=[
            pltpu.VMEM((slots, width), LOW),
            pltpu.VMEM((slots, units), LOW),
            pltpu.VMEM((slots, width), LOW),
            pltpu.VMEM((slots, units), LOW),
            pltpu.VMEM((heads, wide, HEAD), LOW),
            pltpu.VMEM((heads, 3 * NB, HEAD), LOW),
            pltpu.VMEM((heads, slots, wide), LOW),
            pltpu.VMEM((heads, slots, 3 * NB), FULL),
            pltpu.VMEM((heads, wide, 3 * NB), FULL),
            pltpu.VMEM((2, wide // LANES, wide, LANES), jnp.int32),
            pltpu.VMEM((2, wide), jnp.int32),
            pltpu.VMEM((LANES, wide), FULL),
            pltpu.VMEM((chunks, HOP, width), FULL),
            pltpu.VMEM((chunks, HOP, width), FULL),
            pltpu.VMEM((2 * chunks, HOP, width), FULL),
            pltpu.VMEM((slots, width), FULL),
            pltpu.VMEM((slots, 1), FULL),
            pltpu.VMEM((7, 8, width), FULL),
            pltpu.VMEM((heads, LANES, HEAD), LOW),
            pltpu.VMEM((LANES, 3 * NB), LOW),
            pltpu.VMEM((heads, wide, HEAD), FULL),
            pltpu.VMEM((2, LANES, wide), LOW),
            dma((chunks,)),
            dma((chunks,)),
            dma((2 * chunks,)),
            dma((2 * chunks,)),
            dma((2,)),
        ]
        + relay * (2 * RELAYS)
        + [dma((bits,)), dma((bits,)), pltpu.SemaphoreType.REGULAR((bits,))] * (2 * RELAYS),
        compiler_params=pltpu.CompilerParams(
            vmem_limit_bytes=VMEM_LIMIT, collective_id=1, has_side_effects=True
        ),
        name="layer",
    )(length, tokens, w_query, w_key, w_value, rel, corners,
      w_output, cotangent, w_inner, w_outer, *[v.reshape(1, -1) for v in vectors])


class Halving:
    def __init__(self, order, source, got, out, send, recv):
        self.order, self.source, self.got, self.out = order, source, got, out
        self.send, self.recv = send, recv
        self.b = lax.axis_index("batch")

    def part(self, stage, flip):
        bit = self.order[stage]
        rest = sorted(self.order[stage:], reverse=True)
        mine = (self.b >> bit) & 1
        pick = 1 - mine if flip else mine
        return tuple(pick if k == bit else slice(None) for k in rest)

    def copy(self, stage):
        source = self.source if stage == 0 else self.got[stage - 1]
        return pltpu.make_async_remote_copy(
            src_ref=source.at[self.part(stage, True)],
            dst_ref=self.got[stage],
            send_sem=self.send.at[stage],
            recv_sem=self.recv.at[stage],
            device_id={"batch": self.b ^ (1 << self.order[stage])},
            device_id_type=MESH,
        )

    def start(self):
        self.copy(0).start()

    def turn(self, stage):
        self.copy(stage).wait_recv()
        kept = self.source if stage == 0 else self.got[stage - 1]
        value = kept[self.part(stage, False)] + self.got[stage][...]
        if stage == 0:
            self.copy(0).wait_send()
        if stage + 1 < len(self.order):
            self.got[stage][...] = value
            self.copy(stage + 1).start()
        else:
            self.out[...] = value

    def drain(self):
        for stage in range(1, len(self.order)):
            self.copy(stage).wait_send()


def gradient_kernel(
    tok_ref, wq_ref, wk_ref, wv_ref, rel_ref,
    q_ref, k_ref, qrel_ref, ctx_ref, grad_ref, grad_low_ref, small_ref, mat_ref,
    gq_ref, gv_ref, gkrel_ref, step_ref, col_ref,
    gtok_ref, owq_ref, owk_ref, owv_ref, owo_ref, orel_ref, osmall_ref,
    own, inner, outer, turned_ref, fold_ref, hist_ref, gk_ref, gk_low_ref, gqrel_sum,
    work_ref, rel_work, rel_sum, rel_own, rel_in, rel_out, rel_all, small_sum, small_got,
    *rest,
    bits, pieces,
):
    jobs_all = len(pieces) + 2
    got = [rest[at * bits : (at + 1) * bits] for at in range(jobs_all)]
    (in_send, in_recv, out_send, out_recv, rin_send, rin_recv, rout_send, rout_recv,
     piece_send, piece_recv, back_send, back_recv, small_send, small_recv) = rest[jobs_all * bits :]
    slots, width = tok_ref.shape
    chunks = slots // HOP
    heads, wide = q_ref.shape[0], q_ref.shape[1]
    blocks = wide // LANES
    per = LANES // HOP
    scale = (7.0 * HEAD) ** (-0.5)
    line = Line("head", own, inner, outer, (in_send, in_recv, out_send, out_recv))
    rel_line = Line("head", rel_own, rel_in, rel_out, (rin_send, rin_recv, rout_send, rout_recv), 1)
    b = lax.axis_index("batch")
    barrier = pltpu.get_barrier_semaphore()
    line.greet(barrier)
    greet_batch(barrier, bits)
    orders = batch_orders(bits)
    outs = (owq_ref, owk_ref, owv_ref, owo_ref)
    jobs = []
    for at, which in enumerate(pieces):
        jobs.append(
            Halving(orders[at % 2], work_ref.at[at], got[at], outs[which], piece_send.at[at], piece_recv.at[at])
        )
    rel_jobs = []
    for side in range(2):
        at = len(pieces) + side
        rel_jobs.append(
            Halving(orders[side], rel_work.at[side], got[at], rel_sum.at[side], piece_send.at[at], piece_recv.at[at])
        )

    def heads_of(ref):
        return jnp.concatenate([ref[head] for head in range(heads)], axis=1)

    def make(at):
        which = pieces[at]
        if which == 0:
            value = dot_tn(tok_ref[...], heads_of(gq_ref)) + dot_tn(rel_ref[...], rel_low(1))
        elif which == 1:
            value = dot_tn(tok_ref[...], gk_ref[...]) + dot_tn(rel_ref[...], rel_low(0))
        elif which == 2:
            value = dot_tn(tok_ref[...], heads_of(gv_ref))
        else:
            value = dot_tn(grad_low_ref[...], heads_of(ctx_ref))
        target = work_ref.at[at]
        target[...] = value.reshape(target.shape)
        jobs[at].start()

    def rel_low(side):
        return heads_of(gqrel_sum if side else gkrel_ref).astype(LOW)

    def rel_start(side):
        if side:
            for head in range(heads):
                gqrel_sum[head] = gqrel_sum[head] * scale
        target = rel_work.at[side]
        target[...] = heads_of(gqrel_sum if side else gkrel_ref).reshape(target.shape)
        rel_jobs[side].start()

    def small_copy(k):
        return pltpu.make_async_remote_copy(
            src_ref=small_sum.at[k],
            dst_ref=small_got.at[k],
            send_sem=small_send.at[k],
            recv_sem=small_recv.at[k],
            device_id={"batch": b ^ (1 << k)},
            device_id_type=MESH,
        )

    def small_turn(k):
        small_copy(k).wait_recv()
        value = small_sum[k] + small_got[k]
        if k + 1 < bits:
            small_sum[k + 1] = value
            small_copy(k + 1).start()
        else:
            osmall_ref[...] = value

    def back_copy(half, turn):
        sequence = orders[half][::-1]
        region = tuple(
            slice(None) if k in sequence[:turn] else (b >> k) & 1 for k in range(bits - 1, -1, -1)
        )
        target = rel_all.at[(half,) + region]
        return pltpu.make_async_remote_copy(
            src_ref=target,
            dst_ref=target,
            send_sem=back_send.at[half, turn],
            recv_sem=back_recv.at[half, turn],
            device_id={"batch": b ^ (1 << sequence[turn])},
            device_id_type=MESH,
        )

    def back_turn(half, turn):
        back_copy(half, turn).wait_recv()
        if turn + 1 < bits:
            back_copy(half, turn + 1).start()

    def rel_meet():
        value = dot_nt(rel_sum[0].astype(LOW), wk_ref[...]) + dot_nt(rel_sum[1].astype(LOW), wq_ref[...])
        size = width // 2
        for half in range(2):
            rel_own[half] = value[:, half * size : (half + 1) * size]

    def rel_step(hop):
        rel_line.step(jnp.int32(hop), 2)
        half = hop - rel_line.trip
        if half >= 0:
            region = tuple((b >> k) & 1 for k in range(bits - 1, -1, -1))
            rel_all[(half,) + region] = rel_out[half]
            back_copy(half, 0).start()

    def column_head(big, head):
        rows = min(LANES, slots - big * LANES)
        some = slice(big * LANES, big * LANES + rows)
        lanes = slice(big * LANES, (big + 1) * LANES)
        for chunk in range(blocks):
            there = slice(chunk * LANES, min((chunk + 1) * LANES, slots))
            turned_ref[:, there] = mat_ref[head, there, lanes].T
        bucket_sums(big, rows, turned_ref.at[:rows, :], step_ref, col_ref, fold_ref, hist_ref)
        hist = hist_ref[:rows, :]
        gk = dot_nn(turned_ref[:rows, :], q_ref[head]) + dot_nn(hist, qrel_ref[head])
        gk_low_ref[head, :rows, :] = (gk * scale).astype(LOW)
        gqrel_sum[head] += dot_tn(hist, k_ref[head, some, :])

    def inputs_block(big):
        rows = min(LANES, slots - big * LANES)
        some = slice(big * LANES, big * LANES + rows)
        gk = jnp.concatenate([gk_low_ref[head, :rows, :] for head in range(heads)], axis=1)
        gk_ref[some, :] = gk
        gq = jnp.concatenate([gq_ref[head, some, :] for head in range(heads)], axis=1)
        gv = jnp.concatenate([gv_ref[head, some, :] for head in range(heads)], axis=1)
        value = dot_nt(gq, wq_ref[...]) + dot_nt(gk, wk_ref[...]) + dot_nt(gv, wv_ref[...])
        for part in range(rows // HOP):
            own[big * per + part] = value[part * HOP : (part + 1) * HOP]

    gqrel_sum[...] = jnp.zeros_like(gqrel_sum)
    if wide > slots:
        turned_ref[:, slots:] = jnp.zeros((LANES, wide - slots), LOW)
    small_sum[0] = small_ref[...]
    pl.semaphore_wait(barrier, line.greeted() + bits)
    small_copy(0).start()
    rel_start(0)

    @pl.loop(0, heads)
    def _(head):
        column_head(0, head)

    inputs_block(0)

    tasks = {}

    def add(slot, task):
        tasks.setdefault(slot, []).append(task)

    ended = 2 * (blocks - 1)
    add(ended, lambda: rel_start(1))
    for at in range(2):
        add(at, lambda at=at: make(at))
        add(ended + at, lambda at=at: make(2 + at))
        for stage in range(bits):
            after = 4 * stage if stage < 2 else 2 + 2 * stage
            add(2 + at + after, lambda at=at, stage=stage: jobs[at].turn(stage))
            add(ended + 2 + at + after, lambda at=at, stage=stage: jobs[2 + at].turn(stage))
    for stage in range(bits):
        add(2 + 2 * stage, lambda stage=stage: rel_jobs[0].turn(stage))
        add(3 + 2 * stage, lambda stage=stage: small_turn(stage))
        add(ended + 2 + 2 * stage, lambda stage=stage: rel_jobs[1].turn(stage))
    met = ended + 2 * bits
    add(met, rel_meet)
    for hop in range(rel_line.trip + 2):
        add(met + 1 * hop, lambda hop=hop: rel_step(hop))
    for half in range(2):
        for turn in range(bits):
            add(met + 1 * (rel_line.trip + half) + 2 * (1 + turn), lambda half=half, turn=turn: back_turn(half, turn))
    total = chunks + line.trip

    @pl.loop(0, max(total, max(tasks) + 1))
    def _(slot):
        line.step(slot, chunks)
        for big in range(1, blocks):

            @pl.when(slot // 2 + 1 == big)
            def _(big=big):
                late = lax.rem(slot, 2)

                @pl.loop(0, heads // 2)
                def _(head):
                    column_head(big, late * (heads // 2) + head)

                @pl.when(late == 1)
                def _():
                    inputs_block(big)

        for when in sorted(tasks):

            @pl.when(slot == when)
            def _(when=when):
                for task in tasks[when]:
                    task()

        done = slot - line.trip

        @pl.when((done >= 0) & (done < chunks))
        def _():
            at = span(done * HOP, HOP)
            gtok_ref[at, :] = (outer[done] + grad_ref[at, :]).astype(LOW)

    whole = (slice(None),) * (bits + 1)
    for half in range(2):
        size = width // 2
        orel_ref[whole + (slice(half * size, (half + 1) * size),)] = rel_all[half]
    line.drain(chunks)
    rel_line.drain(2)
    for job in jobs + rel_jobs:
        job.drain()
    for k in range(bits):
        small_copy(k).wait_send()
        for half in range(2):
            back_copy(half, k).wait_send()


def gradients(tokens, w_query, w_key, w_value, rel, kept, batch):
    slots, width = tokens.shape
    q = kept[0]
    heads, wide = q.shape[:2]
    mine = heads * HEAD
    bits = batch.bit_length() - 1
    assert 1 << bits == batch
    vmem = pl.BlockSpec(memory_space=pltpu.VMEM)
    chunks = slots // HOP
    split = (2,) * bits
    part = width // batch
    rel_part = rel.shape[0] // batch
    assert mine == PIECE
    pieces = [2, 3, 0, 1]
    shape = jax.ShapeDtypeStruct
    got = []
    for _ in pieces:
        got += [pltpu.VMEM((2,) * (bits - 1 - s) + (part, PIECE), FULL) for s in range(bits)]
    for _ in range(2):
        got += [pltpu.VMEM((2,) * (bits - 1 - s) + (rel_part, mine), FULL) for s in range(bits)]
    dma = pltpu.SemaphoreType.DMA
    return pl.pallas_call(
        functools.partial(gradient_kernel, bits=bits, pieces=pieces),
        out_shape=(
            shape((slots, width), LOW),
            shape((part, mine), FULL),
            shape((part, mine), FULL),
            shape((part, mine), FULL),
            shape((part, mine), FULL),
            shape(split + (rel_part, width), FULL),
            shape((8, width), FULL),
        ),
        in_specs=[vmem] * 18,
        out_specs=(vmem,) * 7,
        scratch_shapes=[
            pltpu.VMEM((chunks, HOP, width), FULL),
            pltpu.VMEM((chunks, HOP, width), FULL),
            pltpu.VMEM((chunks, HOP, width), FULL),
            pltpu.VMEM((LANES, wide), LOW),
            pltpu.VMEM((2, 3 * LANES, 3 * NB), FULL),
            pltpu.VMEM((LANES, 3 * NB), LOW),
            pltpu.VMEM((slots, mine), LOW),
            pltpu.VMEM((heads, LANES, HEAD), LOW),
            pltpu.VMEM((heads, 3 * NB, HEAD), FULL),
            pltpu.VMEM((len(pieces),) + split + (part, PIECE), FULL),
            pltpu.VMEM((2,) + split + (rel_part, mine), FULL),
            pltpu.VMEM((2, rel_part, mine), FULL),
            pltpu.VMEM((2, rel_part, width // 2), FULL),
            pltpu.VMEM((2, rel_part, width // 2), FULL),
            pltpu.VMEM((2, rel_part, width // 2), FULL),
            pltpu.VMEM((2,) + split + (rel_part, width // 2), FULL),
            pltpu.VMEM((bits, 8, width), FULL),
            pltpu.VMEM((bits, 8, width), FULL),
        ]
        + got
        + [dma((chunks,))] * 4
        + [dma((2,))] * 4
        + [dma((len(pieces) + 2, bits))] * 2
        + [dma((2, bits))] * 2
        + [dma((bits,))] * 2,
        compiler_params=pltpu.CompilerParams(
            vmem_limit_bytes=VMEM_LIMIT, collective_id=2, has_side_effects=True
        ),
        name="gradients",
    )(tokens, w_query, w_key, w_value, rel, *kept)


def finish_kernel(out, gtok, gwq, gwk, gwv, gwo, gwi, gwu, grel, small, *targets):
    (o_out, o_gtok, o_gwq, o_gwk, o_gwv, o_gwo, o_gwi, o_gwu, o_grel) = targets[:9]
    o_out[...] = out[...]
    o_gtok[...] = gtok[...]
    o_gwq[...] = gwq[...]
    o_gwk[...] = gwk[...]
    o_gwv[...] = gwv[...]
    o_gwo[...] = gwo[...].T
    o_gwi[...] = gwi[...]
    o_gwu[...] = gwu[...].T
    o_grel[...] = grel[...]
    for at, target in enumerate(targets[9:]):
        target[...] = small[at]


def finish(out, gtok, gwq, gwk, gwv, gwo, gwi, gwu, grel, small):
    vmem = pl.BlockSpec(memory_space=pltpu.VMEM)
    shape = jax.ShapeDtypeStruct
    same = lambda a: shape(a.shape, a.dtype)
    turn = lambda a: shape(a.shape[::-1], a.dtype)
    return pl.pallas_call(
        finish_kernel,
        out_shape=(same(out), same(gtok), same(gwq), same(gwk), same(gwv), turn(gwo), same(gwi), turn(gwu), same(grel))
        + (shape(small.shape[1:], FULL),) * 7,
        in_specs=[vmem] * 10,
        out_specs=(vmem,) * 16,
        compiler_params=pltpu.CompilerParams(vmem_limit_bytes=VMEM_LIMIT),
        name="finish",
    )(out, gtok, gwq, gwk, gwv, gwo, gwi, gwu, grel, small)


def shards(
    tokens,
    page_lengths,
    corners,
    w_query,
    w_key,
    w_value,
    w_output,
    b_output,
    gain_attn,
    shift_attn,
    w_inner,
    b_inner,
    w_outer,
    b_outer,
    gain_ffn,
    shift_ffn,
    rel_tables,
    cotangent,
):
    rel = rel_tables.reshape(3 * NB, rel_tables.shape[2])
    vectors = (b_output, gain_attn, shift_attn, b_inner, b_outer, gain_ffn, shift_ffn)
    q, k, qrel, ctx, output, *kept, gwi, gwu = layer(
        tokens, page_lengths, corners, w_query, w_key, w_value, rel,
        w_output, cotangent, w_inner, w_outer, vectors, lax.axis_size("batch"),
    )
    done = gradients(
        tokens, w_query, w_key, w_value, rel, (q, k, qrel, ctx, *kept), lax.axis_size("batch")
    )
    gtok, gwq, gwk, gwv, gwo, grel, small = done
    grel = grel.reshape(rel_tables.shape)
    (output, gtok, gwq, gwk, gwv, gwo, gwi, gwu, grel, gbo, gga, gsa, gbi, gbu, ggf, gsf) = finish(
        output, gtok, gwq, gwk, gwv, gwo, gwi, gwu, grel, small
    )
    return (output, gtok, gwq, gwk, gwv, gwo, gbo, gga, gsa, gwi, gbi, gwu, gbu, ggf, gsf, grel)


def solution(mesh):
    in_specs = (
        P("batch", None),
        P("batch"),
        P(None, "batch"),
        P(None, "head"),
        P(None, "head"),
        P(None, "head"),
        P("head", None),
        P(),
        P(),
        P(),
        P(None, "head"),
        P("head"),
        P("head", None),
        P(),
        P(),
        P(),
        P(),
        P("batch", None),
    )
    out_specs = (
        P("batch", None),
        P("batch", None),
        P("batch", "head"),
        P("batch", "head"),
        P("batch", "head"),
        P("head", "batch"),
        P(),
        P(),
        P(),
        P("batch", "head"),
        P("head"),
        P("head", "batch"),
        P(),
        P(),
        P(),
        P(),
    )
    return jax.shard_map(shards, mesh=mesh, in_specs=in_specs, out_specs=out_specs, check_vma=False)
```

```python
import functools

import jax
import jax.numpy as jnp
from jax import lax
from jax.experimental import pallas as pl
from jax.experimental.pallas import tpu as pltpu
from jax.sharding import PartitionSpec as P

HEAD = 64
NB = 128
BOX_STEP = 8
NEG_FILL = -1000000000.0
LANES = 128
HOP = 32
PAIR = 64
LAG = 2
PIECE = 256
STRIP = 128
RELAYS = 2
VMEM_LIMIT = 61 * 1024 * 1024
MESH = pl.DeviceIdType.MESH
LOW = jnp.bfloat16
FULL = jnp.float32


def dot_nn(a, b):
    return lax.dot_general(a, b, (((1,), (0,)), ((), ())), preferred_element_type=FULL)


def dot_nt(a, b):
    return lax.dot_general(a, b, (((1,), (1,)), ((), ())), preferred_element_type=FULL)


def dot_tn(a, b):
    return lax.dot_general(a, b, (((0,), (0,)), ((), ())), preferred_element_type=FULL)


def lane_gather(table, index):
    return jnp.take_along_axis(table, index, axis=1, mode="promise_in_bounds")


def bucket(step):
    return jnp.clip(step, -(NB // 2), NB // 2 - 1) + NB // 2


def span(start, size):
    return pl.ds(pl.multiple_of(start, size), size)


class Line:
    def __init__(self, axis, own, inner, outer, sems, lag=LAG):
        self.axis, self.own, self.inner, self.outer, self.lag = axis, own, inner, outer, lag
        self.in_send, self.in_recv, self.out_send, self.out_recv = sems
        self.ring, self.wide_ring = own.shape[0], outer.shape[0]
        self.n = lax.axis_size(axis)
        me = lax.axis_index(axis)
        left = me < self.n // 2
        self.depth = jnp.where(left, me, self.n - 1 - me)
        self.inward = jnp.where(left, me + 1, me - 1)
        self.outward = jnp.where(self.depth == 0, self.inward, jnp.where(left, me - 1, me + 1))
        self.last = self.n // 2 - 1
        self.trip = self.lag * (self.n - 1)

    def greet(self, barrier):
        pl.semaphore_signal(barrier, inc=1, device_id={self.axis: self.inward}, device_id_type=MESH)

        @pl.when(self.depth > 0)
        def _():
            pl.semaphore_signal(
                barrier, inc=1, device_id={self.axis: self.outward}, device_id_type=MESH
            )

    def greeted(self):
        return jnp.where(self.depth > 0, 2, 1)

    def copy(self, source, target, send, recv, to):
        return pltpu.make_async_remote_copy(
            src_ref=source,
            dst_ref=target,
            send_sem=send,
            recv_sem=recv,
            device_id={self.axis: to},
            device_id_type=MESH,
        )

    def total(self, u):
        return lax.rem(u, self.wide_ring)

    def out_copy(self, u):
        o = self.total(u)
        return self.copy(
            self.outer.at[o], self.outer.at[o], self.out_send.at[o], self.out_recv.at[o], self.outward
        )

    def in_copy(self, c, source):
        return self.copy(
            source, self.inner.at[c], self.in_send.at[c], self.in_recv.at[c], self.inward
        )

    def send_in(self, u, c, source):
        @pl.when(self.depth < self.last)
        def _():
            self.in_copy(c, source).start()

        @pl.when(self.depth == self.last)
        def _():
            o = self.total(u)
            self.copy(
                source, self.outer.at[o], self.in_send.at[c], self.out_recv.at[o], self.inward
            ).start()

    def step(self, slot, count):
        here = slot - self.lag * self.depth

        @pl.when((here >= 0) & (here < count))
        def _():
            u = here
            c = lax.rem(u, self.ring)

            @pl.when(self.depth == 0)
            def _():
                self.send_in(u, c, self.own.at[c])

            @pl.when(self.depth > 0)
            def _():
                @pl.when(u >= self.ring)
                def _():
                    self.out_copy(u - self.ring).wait_send()

                self.in_copy(c, self.own.at[c]).wait_recv()
                self.inner[c] += self.own[c]
                self.send_in(u, c, self.inner.at[c])

        back = slot - self.lag * (self.n - 1 - self.depth)

        @pl.when((back >= 0) & (back < count))
        def _():
            u = back
            c = lax.rem(u, self.ring)
            self.in_copy(c, self.own.at[c]).wait_send()
            self.out_copy(u).wait_recv()

            @pl.when(self.depth == self.last)
            def _():
                self.outer[self.total(u)] += self.inner[c] if self.last > 0 else self.own[c]

            @pl.when(self.depth > 0)
            def _():
                self.out_copy(u).start()

    def drain(self, count):
        @pl.when(self.depth > 0)
        def _():
            @pl.loop(count - self.ring, count)
            def _(u):
                self.out_copy(u).wait_send()


class Rounds:
    def __init__(self, order, work, got, out, rounds, send, recv, credit):
        self.order, self.work, self.got, self.out, self.rounds = order, work, got, out, rounds
        self.send, self.recv, self.credit = send, recv, credit
        self.b = lax.axis_index("batch")

    def partner(self, stage):
        return {"batch": self.b ^ (1 << self.order[stage])}

    def part(self, stage, flip):
        bit = self.order[stage]
        rest = sorted(self.order[stage:], reverse=True)
        mine = (self.b >> bit) & 1
        pick = 1 - mine if flip else mine
        return tuple(pick if k == bit else slice(None) for k in rest)

    def source(self, stage):
        return self.work if stage == 0 else self.got[stage - 1]

    def copy(self, stage):
        return pltpu.make_async_remote_copy(
            src_ref=self.source(stage).at[self.part(stage, True)],
            dst_ref=self.got[stage],
            send_sem=self.send.at[stage],
            recv_sem=self.recv.at[stage],
            device_id=self.partner(stage),
            device_id_type=MESH,
        )

    def start(self, stage, number):
        if number > 0:
            pl.semaphore_wait(self.credit.at[stage], 1)
        self.copy(stage).start()

    def free(self, stage, number):
        if number + 1 < self.rounds:
            pl.semaphore_signal(
                self.credit.at[stage], inc=1, device_id=self.partner(stage), device_id_type=MESH
            )

    def begin(self, number, value):
        self.work[...] = value.reshape(self.work.shape)
        self.start(0, number)

    def turn(self, stage, number):
        self.copy(stage).wait_recv()
        value = self.source(stage)[self.part(stage, False)] + self.got[stage][...]
        last = stage + 1 == len(self.order)
        if last:
            size = value.shape[1]
            self.out[:, number * size : (number + 1) * size] = value
        else:
            self.got[stage][...] = value
        self.copy(stage).wait_send()
        if stage > 0:
            self.free(stage - 1, number)
        if last:
            self.free(stage, number)
        else:
            self.start(stage + 1, number)


def batch_orders(bits):
    return (list(range(bits)), [0] + list(range(bits - 1, 0, -1)))


def greet_batch(barrier, bits):
    b = lax.axis_index("batch")
    for k in range(bits):
        pl.semaphore_signal(barrier, inc=1, device_id={"batch": b ^ (1 << k)}, device_id_type=MESH)


def centre(values):
    average = jnp.mean(values, axis=-1, keepdims=True)
    centered = values - average
    spread = jnp.mean(centered * centered, axis=-1, keepdims=True)
    scaling = lax.rsqrt(spread + 1e-05)
    return centered * scaling, scaling


def norm_inward(scaled, normed, scaling):
    return scaling * (
        scaled
        - jnp.mean(scaled, axis=-1, keepdims=True)
        - normed * jnp.mean(scaled * normed, axis=-1, keepdims=True)
    )


def fold_rows(values):
    rows, width = values.shape
    return jnp.sum(values.reshape(rows // 8, 8, width), axis=0)


def attention_setup(tok_ref, wq_ref, wk_ref, wv_ref, rel_ref, corner_ref,
                    q_ref, k_ref, v_ref, krel_ref, qrel_ref, tq_ref, tk_ref, idx_ref, col_ref, row_ref):
    slots = tok_ref.shape[0]
    heads, wide = q_ref.shape[0], q_ref.shape[1]
    chunks = wide // LANES
    for weight, target in ((wq_ref, q_ref), (wk_ref, k_ref), (wv_ref, v_ref)):
        value = dot_nn(tok_ref[...], weight[...]).astype(LOW)
        for head in range(heads):
            target[head, :slots, :] = value[:, head * HEAD : (head + 1) * HEAD]
            if wide > slots:
                target[head, slots:, :] = jnp.zeros((wide - slots, HEAD), LOW)
    for weight, target in ((wk_ref, krel_ref), (wq_ref, qrel_ref)):
        value = dot_nn(rel_ref[...], weight[...]).astype(LOW)
        for head in range(heads):
            target[head] = value[:, head * HEAD : (head + 1) * HEAD]
    for head in range(heads):
        tq_ref[head] = dot_nt(q_ref[head, :slots, :], krel_ref[head])
        tk_ref[head] = dot_nt(k_ref[head], qrel_ref[head])
    row_ref[...] = jnp.zeros_like(row_ref)
    row_ref[:, :slots] = corner_ref[...]
    for kind in range(2):
        for big in range(chunks):
            here = slice(big * LANES, (big + 1) * LANES)
            col_ref[kind, here, :] = jnp.broadcast_to(row_ref[kind : kind + 1, here], (LANES, LANES)).T

    @pl.loop(0, chunks)
    def _(big):
        at = span(big * LANES, LANES)
        for kind in range(2):
            own = col_ref[kind, at, :]
            for chunk in range(chunks):
                other = row_ref[kind : kind + 1, chunk * LANES : (chunk + 1) * LANES]
                idx_ref[kind, chunk, at, :] = bucket((own - other) >> 3)


def attention_block(big, head, length, q_ref, k_ref, v_ref, tq_ref, tk_ref, idx_ref, log_ref, attend_ref, ctx_ref):
    wide = q_ref.shape[1]
    chunks = wide // LANES
    slots = attend_ref.shape[1]
    scale = (7.0 * HEAD) ** (-0.5)
    rows = min(LANES, slots - big * LANES)
    some = slice(big * LANES, big * LANES + rows)
    slant = lax.broadcasted_iota(jnp.int32, (LANES, LANES), 0) - lax.broadcasted_iota(
        jnp.int32, (LANES, LANES), 1
    )
    log_ref[:rows, :] = dot_nt(q_ref[head, some, :], k_ref[head])
    for chunk in range(chunks):
        there = slice(chunk * LANES, (chunk + 1) * LANES)
        away = (big - chunk) * LANES
        toward = log_ref[:rows, there]
        if abs(big - chunk) >= 2:
            lane = NB - 1 if away > 0 else 0
            toward = toward + tq_ref[head, some, lane : lane + 1]
            lane = NB - 1 - lane
            beside = jnp.broadcast_to(tk_ref[head, there, lane : lane + 1], (LANES, LANES))
        else:
            toward = toward + lane_gather(tq_ref[head, some, :NB], bucket(slant + away)[:rows])
            beside = lane_gather(tk_ref[head, there, :NB], bucket(slant - away))
        for kind in range(2):
            lanes = slice((kind + 1) * NB, (kind + 2) * NB)
            toward = toward + lane_gather(tq_ref[head, some, lanes], idx_ref[kind, chunk, some, :])
            beside = beside + lane_gather(tk_ref[head, there, lanes], idx_ref[kind, big, there, :])
        log_ref[:rows, there] = toward + beside.T[:rows]
    block = 32
    for start in range(0, rows, block):
        at = slice(start, start + block)
        j_at = lax.broadcasted_iota(jnp.int32, (block, wide), 1)
        masked = jnp.where(j_at < length, log_ref[at, :], NEG_FILL)
        peak = jnp.max(masked, axis=-1, keepdims=True)
        grown = jnp.exp((masked - peak) * scale)
        total = jnp.sum(grown, axis=-1, keepdims=True)
        attend_ref[head, big * LANES + start : big * LANES + start + block, :] = (
            grown * (1.0 / total)
        ).astype(LOW)
    ctx_ref[head, some, :] = dot_nn(attend_ref[head, some, :], v_ref[head]).astype(LOW)


def make_steps(step_ref, col_ref, slots):
    wide = step_ref.shape[1]
    block = 64
    if wide > slots:
        step_ref[:, slots:, :] = jnp.zeros_like(step_ref[:, slots:, :])

    @pl.loop(0, slots // block)
    def _(step):
        at = span(step * block, block)
        quotient = lax.broadcasted_iota(jnp.int32, (block, NB), 1) * BOX_STEP
        for kind in range(2):
            own = col_ref[kind, at, :]
            for rest in range(BOX_STEP):
                lanes = slice(rest * NB, (rest + 1) * NB)
                step_ref[kind, at, lanes] = (own <= quotient + rest).astype(FULL).astype(LOW)


def fold_at(kind, r, at):
    return (kind, at, slice(r % 3 * NB, (r % 3 + 1) * NB))


def bucket_sums(big, rows, mat, step_ref, col_ref, fold_ref, hist_ref):
    chunks = step_ref.shape[1] // LANES
    for kind in range(2):
        value = dot_nn(mat[...], step_ref[kind])
        for r in range(BOX_STEP):
            fold_ref[fold_at(kind, r, slice(r // 3 * LANES, r // 3 * LANES + rows))] = value[
                :, r * NB : (r + 1) * NB
            ]
    block = rows

    def some(local):
        at = slice(local, local + block)
        far = slice(big * LANES + local, big * LANES + local + block)
        lane = lax.broadcasted_iota(jnp.int32, (block, NB), 1)
        row = lax.broadcasted_iota(jnp.int32, (block, NB), 0) + local
        part = [mat[at, c * LANES : (c + 1) * LANES].astype(FULL) for c in range(chunks)]
        zero = jnp.zeros((block, LANES), FULL)
        before = part[big - 1] if big >= 1 else zero
        after = part[big + 1] if big + 1 < chunks else zero
        mid = part[big]
        delta = lane - row
        window = jnp.where(delta > NB // 2, before, jnp.where(delta < 1 - NB // 2, after, mid))
        spread = lane_gather(window, (row + NB // 2 - lane) & (NB - 1))
        under = jnp.where(delta <= NB // 2 + 1, before, 0.0) + jnp.where(
            delta <= 1 - NB // 2, mid, 0.0
        )
        over = jnp.where(delta >= NB // 2, mid, 0.0) + jnp.where(delta >= -(NB // 2), after, 0.0)
        for c in range(big - 1):
            under = under + part[c]
        for c in range(big + 2, chunks):
            over = over + part[c]
        under = jnp.sum(under, axis=-1, keepdims=True)
        over = jnp.sum(over, axis=-1, keepdims=True)
        spread = jnp.where(lane == 0, over, jnp.where(lane == NB - 1, under, spread))
        hist_ref[at, 0:NB] = spread.astype(LOW)
        for kind in range(2):
            own = col_ref[kind, far, :]
            groups = [
                fold_ref[fold_at(kind, r, slice(r // 3 * LANES + local, r // 3 * LANES + local + block))]
                for r in range(BOX_STEP)
            ]
            every = groups[-1][:, NB - 1 : NB]
            for bit in range(3):
                odd = (own & (1 << bit)) != 0
                groups = [
                    jnp.where(odd, groups[g + 1], groups[g]) for g in range(0, len(groups), 2)
                ]
            index = (own >> 3) + NB // 2 - lane
            found = lane_gather(groups[0], index & (NB - 1))
            found = jnp.where(index < 0, 0.0, found)
            found = jnp.where((index >= NB) | (lane == 0), every, found)
            following = pltpu.roll(found, NB - 1, 1)
            found = found - jnp.where(lane == NB - 1, 0.0, following)
            hist_ref[at, (kind + 1) * NB : (kind + 2) * NB] = found.astype(LOW)

    some(0)


def copies(pairs, sems):
    return [
        pltpu.make_async_copy(source, target, sems.at[at]) for at, (source, target) in enumerate(pairs)
    ]


def layer_kernel(
    length_ref, tok_ref, wq_ref, wk_ref, wv_ref, rel_ref, corner_ref,
    wo_in, cot_in, wi_in, wu_in, bo_ref, ga_ref, sa_ref, bi_ref, bu_ref, gf_ref, sf_ref,
    q_out, k_out, qrel_out, ctx_ref, out_ref, grad_ref, grad_low_ref, small_ref, mat_ref,
    gq_ref, gv_ref, gkrel_ref, step_out, col_out, owi_ref, owu_ref,
    hidden_ref, active_ref, mid_low_ref, inner_low_ref, v_ref, krel_ref, attend_ref, tq_ref, tk_ref, idx_ref, row_ref, log_ref,
    own, inner, outer, normed_ref, scale_ref, sums_ref, gc_ref, hist_ref, gv_sum, block_ref,
    wo_ref, cot_ref, wi_ref, wu_ref, q_ref, k_ref, qrel_ref, step_ref, col_ref,
    in_send, in_recv, out_send, out_recv, block_sem, load_sem, save_sem, *rest,
    bits,
):
    slots = tok_ref.shape[0]
    chunks = slots // HOP
    heads, wide = q_ref.shape[0], q_ref.shape[1]
    blocks = wide // LANES
    per = LANES // HOP
    scale = (7.0 * HEAD) ** (-0.5)
    line = Line("head", own, inner, outer, (in_send, in_recv, out_send, out_recv))
    barrier = pltpu.get_barrier_semaphore()
    line.greet(barrier)
    greet_batch(barrier, bits)
    loads = copies(((wo_in, wo_ref), (cot_in, cot_ref), (wi_in, wi_ref), (wu_in, wu_ref)), load_sem)
    saves = copies(
        ((q_ref, q_out), (k_ref, k_out), (qrel_ref, qrel_out), (col_ref, col_out), (step_ref, step_out)),
        save_sem,
    )
    for load in loads:
        load.start()
    share = owi_ref.shape[1] // RELAYS
    rounds = share // STRIP
    relays = []
    for at in range(2 * RELAYS):
        work, *got = rest[at * (bits + 1) : (at + 1) * (bits + 1)]
        first = 2 * RELAYS * (bits + 1) + 3 * at
        sems = rest[first : first + 3]
        start = at // 2 * share
        out = (owi_ref, owu_ref)[at % 2].at[:, start : start + share]
        relays.append(Rounds(batch_orders(bits)[at % 2], work, got, out, rounds, *sems))
    sums_ref[...] = jnp.zeros_like(sums_ref)
    gv_sum[...] = jnp.zeros_like(gv_sum)
    gkrel_ref[...] = jnp.zeros_like(gkrel_ref)
    attention_setup(tok_ref, wq_ref, wk_ref, wv_ref, rel_ref, corner_ref,
                    q_ref, k_ref, v_ref, krel_ref, qrel_ref, tq_ref, tk_ref, idx_ref, col_ref, row_ref)
    for save in saves[:4]:
        save.start()
    for load in loads:
        load.wait()
    pl.semaphore_wait(barrier, line.greeted() + bits)
    root = 0.5**0.5
    bell = (0.5 / jnp.pi) ** 0.5

    def forward_head(big, head):
        attention_block(big, head, length_ref[0], q_ref, k_ref, v_ref, tq_ref, tk_ref, idx_ref, log_ref,
                        attend_ref, ctx_ref)

    def put(c, value):
        for part in range(PAIR // HOP):
            own[c * (PAIR // HOP) + part] = value[part * HOP : (part + 1) * HOP]

    def got(u):
        first = line.total(u * (PAIR // HOP))
        return jnp.concatenate([outer[first + part] for part in range(PAIR // HOP)], axis=0)

    def project(c):
        at = span(c * PAIR, PAIR)
        context = jnp.concatenate([ctx_ref[head, at, :] for head in range(heads)], axis=1)
        put(c, dot_nn(context, wo_ref[...]))

    def after_attention(c, u):
        at = span(c * PAIR, PAIR)
        normed, scaling = centre(got(u) + bo_ref[...] + tok_ref[at, :].astype(FULL))
        normed_ref[at, :] = normed
        scale_ref[at, :] = scaling
        hidden_low = (normed * ga_ref[...] + sa_ref[...]).astype(LOW)
        hidden_ref[at, :] = hidden_low
        pre = dot_nn(hidden_low, wi_ref[...]) + bi_ref[...]
        grad_ref[at, :] = pre
        active = (pre * (1.0 + lax.erf(pre * root)) * 0.5).astype(LOW)
        active_ref[at, :] = active
        put(c, dot_nn(active, wu_ref[...]))

    def after_ffn(c, u):
        at = span(c * PAIR, PAIR)
        hidden = normed_ref[at, :] * ga_ref[...] + sa_ref[...]
        normed, scaling = centre(got(u) + bu_ref[...] + hidden)
        out_ref[at, :] = (normed * gf_ref[...] + sf_ref[...]).astype(LOW)
        upstream = cot_ref[at, :].astype(FULL)
        grad_mid = norm_inward(upstream * gf_ref[...], normed, scaling)
        sums_ref[4] += fold_rows(grad_mid)
        sums_ref[5] += fold_rows(upstream * normed)
        sums_ref[6] += fold_rows(upstream)
        pre = grad_ref[at, :]
        grad_ref[at, :] = grad_mid
        mid_low = grad_mid.astype(LOW)
        mid_low_ref[at, :] = mid_low
        grad_active = dot_nt(mid_low, wu_ref[...])
        slope = (1.0 + lax.erf(pre * root)) * 0.5 + pre * jnp.exp(-0.5 * pre * pre) * bell
        inner_low = (grad_active * slope).astype(LOW)
        sums_ref[3] += fold_rows(inner_low.astype(FULL))
        inner_low_ref[at, :] = inner_low
        put(c, dot_nt(inner_low, wi_ref[...]))

    def after_hidden(c, u):
        at = span(c * PAIR, PAIR)
        upstream = got(u) + grad_ref[at, :]
        normed = normed_ref[at, :]
        grad_attn = norm_inward(upstream * ga_ref[...], normed, scale_ref[at, :])
        sums_ref[0] += fold_rows(grad_attn)
        sums_ref[1] += fold_rows(upstream * normed)
        sums_ref[2] += fold_rows(upstream)
        grad_ref[at, :] = grad_attn
        grad_low_ref[at, :] = grad_attn.astype(LOW)

    def backward_block(big):
        rows = min(LANES, slots - big * LANES)
        some = slice(big * LANES, big * LANES + rows)
        value = dot_nt(grad_low_ref[some, :], wo_ref[...]).astype(LOW)
        for head in range(heads):
            gc_ref[head, :rows, :] = value[:, head * HEAD : (head + 1) * HEAD]

    def block_copy(big, head, rows):
        buffer = lax.rem(head, 2)
        return pltpu.make_async_copy(
            block_ref.at[buffer, :rows, :],
            mat_ref.at[head, pl.ds(big * LANES, rows), :],
            block_sem.at[buffer],
        )

    def backward_head(big, head):
        rows = min(LANES, slots - big * LANES)
        some = slice(big * LANES, big * LANES + rows)

        @pl.when(head >= 2)
        def _():
            block_copy(big, head - 2, rows).wait()

        if big > 0:

            @pl.when(head < 2)
            def _():
                block_copy(big - 1, head + 2, LANES).wait()

        gc = gc_ref[head, :rows, :]
        grad_attend = dot_nt(gc, v_ref[head])
        mean = jnp.sum(gc.astype(FULL) * ctx_ref[head, some, :].astype(FULL), axis=-1, keepdims=True)
        attend = attend_ref[head, some, :]
        mat = block_ref.at[lax.rem(head, 2), :rows, :]
        mat[...] = (attend.astype(FULL) * (grad_attend - mean)).astype(LOW)
        block_copy(big, head, rows).start()
        gv_sum[head] += dot_tn(attend, gc)
        bucket_sums(big, rows, mat, step_ref, col_ref, tq_ref, hist_ref)
        hist = hist_ref[:rows, :]
        gq = dot_nn(mat[...], k_ref[head]) + dot_nn(hist, krel_ref[head])
        gq_ref[head, some, :] = (gq * scale).astype(LOW)
        gkrel_ref[head] += dot_tn(hist, q_ref[head, some, :])

    def relay_begin(at, number):
        start = at // 2 * share + number * STRIP
        lanes = slice(start, start + STRIP)
        if at % 2 == 0:
            value = dot_tn(hidden_ref[...], inner_low_ref[:, lanes])
        else:
            value = dot_tn(mid_low_ref[...], active_ref[:, lanes])
        relays[at].begin(number, value)

    for head in range(heads):
        forward_head(0, head)
    count = 3 * chunks
    ratio = PAIR // HOP
    first_back = 2 * chunks + line.trip + per
    last_slot = first_back + (blocks - 1) * per + heads
    tasks = {}

    def add(when, task):
        tasks.setdefault(when, []).append(task)

    after = 2 * chunks + line.trip
    for number in range(rounds):
        for at in range(2 * RELAYS):
            base = after + 5 * number + at
            add(base, lambda at=at, number=number: relay_begin(at, number))
            for stage in range(bits):
                when = base + 1 + 2 * stage
                add(when, lambda at=at, stage=stage, number=number: relays[at].turn(stage, number))

    @pl.loop(0, max(count + line.trip, last_slot, max(tasks) + 1))
    def _(slot):
        @pl.when((slot < chunks) & (lax.rem(slot, ratio) == 0))
        def _():
            project(slot // ratio)

        line.step(slot, count)
        ahead = slot + per
        for big in range(1, blocks):

            @pl.when(ahead // per == big)
            def _(big=big):
                forward_head(big, lax.rem(ahead, per))

        done = slot - line.trip - (ratio - 1)
        pair = done // ratio
        ready = (done >= 0) & (lax.rem(done + ratio, ratio) == 0)
        pairs = chunks // ratio

        @pl.when(ready & (pair < pairs))
        def _():
            after_attention(pair, pair)

        @pl.when(ready & (pair >= pairs) & (pair < 2 * pairs))
        def _():
            after_ffn(pair - pairs, pair)

        @pl.when(ready & (pair >= 2 * pairs) & (pair < 3 * pairs))
        def _():
            after_hidden(pair - 2 * pairs, pair)

        @pl.when(slot == 2 * chunks)
        def _():
            make_steps(step_ref, col_ref, slots)
            saves[4].start()

        for when in sorted(tasks):

            @pl.when(slot == when)
            def _(when=when):
                for task in tasks[when]:
                    task()

        since = slot - first_back
        for big in range(blocks):

            @pl.when((since >= 0) & (since // per == big))
            def _(big=big):
                at_head = lax.rem(since, per)

                @pl.when(at_head == 0)
                def _():
                    backward_block(big)

                backward_head(big, at_head)

    for at in range(7):
        small_ref[at : at + 1, :] = jnp.sum(sums_ref[at], axis=0, keepdims=True)
    small_ref[7:8, :] = jnp.zeros_like(small_ref[7:8, :])
    for head in range(heads):
        gv_ref[head] = gv_sum[head, :slots, :].astype(LOW)
        gkrel_ref[head] = gkrel_ref[head] * scale
    for head in range(heads - 2, heads):
        block_copy(blocks - 1, head, slots - (blocks - 1) * LANES).wait()
    line.drain(count)
    for save in saves:
        save.wait()


def layer(
    tokens, length, corners, w_query, w_key, w_value, rel, w_output, cotangent, w_inner, w_outer, vectors, batch
):
    slots, width = tokens.shape
    units = w_inner.shape[1]
    mine = w_query.shape[1]
    heads = mine // HEAD
    wide = -(-slots // LANES) * LANES
    assert units == width and heads == LANES // HOP and slots % PAIR == 0
    vmem = pl.BlockSpec(memory_space=pltpu.VMEM)
    far = pl.BlockSpec(memory_space=pl.ANY)
    chunks = slots // HOP
    shape = jax.ShapeDtypeStruct
    dma = pltpu.SemaphoreType.DMA
    bits = batch.bit_length() - 1
    assert 1 << bits == batch
    part = width // batch
    relay = [pltpu.VMEM((2,) * (bits - s) + (part, STRIP), FULL) for s in range(bits + 1)]
    return pl.pallas_call(
        functools.partial(layer_kernel, bits=bits),
        out_shape=(
            shape((heads, wide, HEAD), LOW),
            shape((heads, wide, HEAD), LOW),
            shape((heads, 3 * NB, HEAD), LOW),
            shape((heads, slots, HEAD), LOW),
            shape((slots, width), LOW),
            shape((slots, width), FULL),
            shape((slots, width), LOW),
            shape((8, width), FULL),
            shape((heads, slots, wide), LOW),
            shape((heads, slots, HEAD), LOW),
            shape((heads, slots, HEAD), LOW),
            shape((heads, 3 * NB, HEAD), FULL),
            shape((2, wide, BOX_STEP * NB), LOW),
            shape((2, wide, LANES), jnp.int32),
            shape((part, units), FULL),
            shape((part, units), FULL),
        ),
        in_specs=[pl.BlockSpec(memory_space=pltpu.SMEM)] + [vmem] * 6 + [far] * 4 + [vmem] * 7,
        out_specs=(far,) * 3 + (vmem,) * 5 + (far,) + (vmem,) * 3 + (far,) * 2 + (vmem,) * 2,
        scratch_shapes=[
            pltpu.VMEM((slots, width), LOW),
            pltpu.VMEM((slots, units), LOW),
            pltpu.VMEM((slots, width), LOW),
            pltpu.VMEM((slots, units), LOW),
            pltpu.VMEM((heads, wide, HEAD), LOW),
            pltpu.VMEM((heads, 3 * NB, HEAD), LOW),
            pltpu.VMEM((heads, slots, wide), LOW),
            pltpu.VMEM((heads, slots, 3 * NB), FULL),
            pltpu.VMEM((heads, wide, 3 * NB), FULL),
            pltpu.VMEM((2, wide // LANES, wide, LANES), jnp.int32),
            pltpu.VMEM((2, wide), jnp.int32),
            pltpu.VMEM((LANES, wide), FULL),
            pltpu.VMEM((chunks, HOP, width), FULL),
            pltpu.VMEM((chunks, HOP, width), FULL),
            pltpu.VMEM((2 * chunks, HOP, width), FULL),
            pltpu.VMEM((slots, width), FULL),
            pltpu.VMEM((slots, 1), FULL),
            pltpu.VMEM((7, 8, width), FULL),
            pltpu.VMEM((heads, LANES, HEAD), LOW),
            pltpu.VMEM((LANES, 3 * NB), LOW),
            pltpu.VMEM((heads, wide, HEAD), FULL),
            pltpu.VMEM((2, LANES, wide), LOW),
            pltpu.VMEM((mine, width), LOW),
            pltpu.VMEM((slots, width), LOW),
            pltpu.VMEM((width, units), LOW),
            pltpu.VMEM((units, width), LOW),
            pltpu.VMEM((heads, wide, HEAD), LOW),
            pltpu.VMEM((heads, wide, HEAD), LOW),
            pltpu.VMEM((heads, 3 * NB, HEAD), LOW),
            pltpu.VMEM((2, wide, BOX_STEP * NB), LOW),
            pltpu.VMEM((2, wide, LANES), jnp.int32),
            dma((chunks,)),
            dma((chunks,)),
            dma((2 * chunks,)),
            dma((2 * chunks,)),
            dma((2,)),
            dma((4,)),
            dma((5,)),
        ]
        + relay * (2 * RELAYS)
        + [dma((bits,)), dma((bits,)), pltpu.SemaphoreType.REGULAR((bits,))] * (2 * RELAYS),
        compiler_params=pltpu.CompilerParams(
            vmem_limit_bytes=VMEM_LIMIT, collective_id=1, has_side_effects=True
        ),
        name="layer",
    )(length, tokens, w_query, w_key, w_value, rel, corners,
      w_output, cotangent, w_inner, w_outer, *[v.reshape(1, -1) for v in vectors])


class Halving:
    def __init__(self, order, source, got, out, send, recv):
        self.order, self.source, self.got, self.out = order, source, got, out
        self.send, self.recv = send, recv
        self.b = lax.axis_index("batch")

    def part(self, stage, flip):
        bit = self.order[stage]
        rest = sorted(self.order[stage:], reverse=True)
        mine = (self.b >> bit) & 1
        pick = 1 - mine if flip else mine
        return tuple(pick if k == bit else slice(None) for k in rest)

    def copy(self, stage):
        source = self.source if stage == 0 else self.got[stage - 1]
        return pltpu.make_async_remote_copy(
            src_ref=source.at[self.part(stage, True)],
            dst_ref=self.got[stage],
            send_sem=self.send.at[stage],
            recv_sem=self.recv.at[stage],
            device_id={"batch": self.b ^ (1 << self.order[stage])},
            device_id_type=MESH,
        )

    def start(self):
        self.copy(0).start()

    def turn(self, stage):
        self.copy(stage).wait_recv()
        kept = self.source if stage == 0 else self.got[stage - 1]
        value = kept[self.part(stage, False)] + self.got[stage][...]
        if stage == 0:
            self.copy(0).wait_send()
        if stage + 1 < len(self.order):
            self.got[stage][...] = value
            self.copy(stage + 1).start()
        else:
            self.out[...] = value

    def drain(self):
        for stage in range(1, len(self.order)):
            self.copy(stage).wait_send()


def gradient_kernel(
    tok_in, wq_in, wk_in, wv_in, rel_in_hbm,
    q_ref, k_ref, qrel_ref, ctx_in, grad_in, grad_low_in, small_ref, mat_ref,
    gq_in, gv_in, gkrel_ref, step_ref, col_ref,
    gtok_ref, owq_ref, owk_ref, owv_ref, owo_ref, orel_ref, osmall_ref,
    own, inner, outer, turned_ref, fold_ref, hist_ref, gk_ref, gk_low_ref, gqrel_sum,
    work_ref, rel_work, rel_sum, rel_own, rel_in, rel_out, rel_all, small_sum, small_got,
    wq_ref, wk_ref, wv_ref, gq_ref, gv_ref, tok_ref, rel_ref, ctx_ref, grad_ref, grad_low_ref, load_sem,
    *rest,
    bits, pieces,
):
    jobs_all = len(pieces) + 2
    got = [rest[at * bits : (at + 1) * bits] for at in range(jobs_all)]
    (in_send, in_recv, out_send, out_recv, rin_send, rin_recv, rout_send, rout_recv,
     piece_send, piece_recv, back_send, back_recv, small_send, small_recv) = rest[jobs_all * bits :]
    slots, width = tok_ref.shape
    chunks = slots // HOP
    heads, wide = q_ref.shape[0], q_ref.shape[1]
    blocks = wide // LANES
    per = LANES // HOP
    scale = (7.0 * HEAD) ** (-0.5)
    line = Line("head", own, inner, outer, (in_send, in_recv, out_send, out_recv))
    rel_line = Line("head", rel_own, rel_in, rel_out, (rin_send, rin_recv, rout_send, rout_recv), 1)
    b = lax.axis_index("batch")
    barrier = pltpu.get_barrier_semaphore()
    line.greet(barrier)
    greet_batch(barrier, bits)
    loads = copies(
        (
            (wq_in, wq_ref), (wk_in, wk_ref), (wv_in, wv_ref), (gq_in, gq_ref), (gv_in, gv_ref),
            (tok_in, tok_ref), (rel_in_hbm, rel_ref), (ctx_in, ctx_ref), (grad_in, grad_ref),
            (grad_low_in, grad_low_ref),
        ),
        load_sem,
    )
    for load in loads:
        load.start()
    orders = batch_orders(bits)
    outs = (owq_ref, owk_ref, owv_ref, owo_ref)
    jobs = []
    for at, which in enumerate(pieces):
        jobs.append(
            Halving(orders[at % 2], work_ref.at[at], got[at], outs[which], piece_send.at[at], piece_recv.at[at])
        )
    rel_jobs = []
    for side in range(2):
        at = len(pieces) + side
        rel_jobs.append(
            Halving(orders[side], rel_work.at[side], got[at], rel_sum.at[side], piece_send.at[at], piece_recv.at[at])
        )

    def heads_of(ref):
        return jnp.concatenate([ref[head] for head in range(heads)], axis=1)

    def make(at):
        which = pieces[at]
        if which == 0:
            value = dot_tn(tok_ref[...], heads_of(gq_ref)) + dot_tn(rel_ref[...], rel_low(1))
        elif which == 1:
            value = dot_tn(tok_ref[...], gk_ref[...]) + dot_tn(rel_ref[...], rel_low(0))
        elif which == 2:
            value = dot_tn(tok_ref[...], heads_of(gv_ref))
        else:
            value = dot_tn(grad_low_ref[...], heads_of(ctx_ref))
        target = work_ref.at[at]
        target[...] = value.reshape(target.shape)
        jobs[at].start()

    def rel_low(side):
        return heads_of(gqrel_sum if side else gkrel_ref).astype(LOW)

    def rel_start(side):
        if side:
            for head in range(heads):
                gqrel_sum[head] = gqrel_sum[head] * scale
        target = rel_work.at[side]
        target[...] = heads_of(gqrel_sum if side else gkrel_ref).reshape(target.shape)
        rel_jobs[side].start()

    def small_copy(k):
        return pltpu.make_async_remote_copy(
            src_ref=small_sum.at[k],
            dst_ref=small_got.at[k],
            send_sem=small_send.at[k],
            recv_sem=small_recv.at[k],
            device_id={"batch": b ^ (1 << k)},
            device_id_type=MESH,
        )

    def small_turn(k):
        small_copy(k).wait_recv()
        value = small_sum[k] + small_got[k]
        if k + 1 < bits:
            small_sum[k + 1] = value
            small_copy(k + 1).start()
        else:
            osmall_ref[...] = value

    def back_copy(half, turn):
        sequence = orders[half][::-1]
        region = tuple(
            slice(None) if k in sequence[:turn] else (b >> k) & 1 for k in range(bits - 1, -1, -1)
        )
        target = rel_all.at[(half,) + region]
        return pltpu.make_async_remote_copy(
            src_ref=target,
            dst_ref=target,
            send_sem=back_send.at[half, turn],
            recv_sem=back_recv.at[half, turn],
            device_id={"batch": b ^ (1 << sequence[turn])},
            device_id_type=MESH,
        )

    def back_turn(half, turn):
        back_copy(half, turn).wait_recv()
        if turn + 1 < bits:
            back_copy(half, turn + 1).start()

    def rel_meet():
        value = dot_nt(rel_sum[0].astype(LOW), wk_ref[...]) + dot_nt(rel_sum[1].astype(LOW), wq_ref[...])
        size = width // 2
        for half in range(2):
            rel_own[half] = value[:, half * size : (half + 1) * size]

    def rel_step(hop):
        rel_line.step(jnp.int32(hop), 2)
        half = hop - rel_line.trip
        if half >= 0:
            region = tuple((b >> k) & 1 for k in range(bits - 1, -1, -1))
            rel_all[(half,) + region] = rel_out[half]
            back_copy(half, 0).start()

    def column_head(big, head):
        rows = min(LANES, slots - big * LANES)
        some = slice(big * LANES, big * LANES + rows)
        lanes = slice(big * LANES, (big + 1) * LANES)
        for chunk in range(blocks):
            there = slice(chunk * LANES, min((chunk + 1) * LANES, slots))
            turned_ref[:, there] = mat_ref[head, there, lanes].T
        bucket_sums(big, rows, turned_ref.at[:rows, :], step_ref, col_ref, fold_ref, hist_ref)
        hist = hist_ref[:rows, :]
        gk = dot_nn(turned_ref[:rows, :], q_ref[head]) + dot_nn(hist, qrel_ref[head])
        gk_low_ref[head, :rows, :] = (gk * scale).astype(LOW)
        gqrel_sum[head] += dot_tn(hist, k_ref[head, some, :])

    def inputs_block(big):
        rows = min(LANES, slots - big * LANES)
        some = slice(big * LANES, big * LANES + rows)
        gk = jnp.concatenate([gk_low_ref[head, :rows, :] for head in range(heads)], axis=1)
        gk_ref[some, :] = gk
        gq = jnp.concatenate([gq_ref[head, some, :] for head in range(heads)], axis=1)
        gv = jnp.concatenate([gv_ref[head, some, :] for head in range(heads)], axis=1)
        value = dot_nt(gq, wq_ref[...]) + dot_nt(gk, wk_ref[...]) + dot_nt(gv, wv_ref[...])
        for part in range(rows // HOP):
            own[big * per + part] = value[part * HOP : (part + 1) * HOP]

    gqrel_sum[...] = jnp.zeros_like(gqrel_sum)
    if wide > slots:
        turned_ref[:, slots:] = jnp.zeros((LANES, wide - slots), LOW)
    small_sum[0] = small_ref[...]
    pl.semaphore_wait(barrier, line.greeted() + bits)
    small_copy(0).start()
    rel_start(0)

    @pl.loop(0, heads)
    def _(head):
        column_head(0, head)

    for load in loads:
        load.wait()
    inputs_block(0)

    tasks = {}

    def add(slot, task):
        tasks.setdefault(slot, []).append(task)

    ended = 2 * (blocks - 1)
    add(ended, lambda: rel_start(1))
    for at in range(2):
        add(at, lambda at=at: make(at))
        add(ended + at, lambda at=at: make(2 + at))
        for stage in range(bits):
            after = 4 * stage if stage < 2 else 2 + 2 * stage
            add(2 + at + after, lambda at=at, stage=stage: jobs[at].turn(stage))
            add(ended + 2 + at + after, lambda at=at, stage=stage: jobs[2 + at].turn(stage))
    for stage in range(bits):
        add(2 + 2 * stage, lambda stage=stage: rel_jobs[0].turn(stage))
        add(3 + 2 * stage, lambda stage=stage: small_turn(stage))
        add(ended + 2 + 2 * stage, lambda stage=stage: rel_jobs[1].turn(stage))
    met = ended + 2 * bits
    add(met, rel_meet)
    for hop in range(rel_line.trip + 2):
        add(met + 1 * hop, lambda hop=hop: rel_step(hop))
    for half in range(2):
        for turn in range(bits):
            add(met + 1 * (rel_line.trip + half) + 2 * (1 + turn), lambda half=half, turn=turn: back_turn(half, turn))
    total = chunks + line.trip

    @pl.loop(0, max(total, max(tasks) + 1))
    def _(slot):
        line.step(slot, chunks)
        for big in range(1, blocks):

            @pl.when(slot // 2 + 1 == big)
            def _(big=big):
                late = lax.rem(slot, 2)

                @pl.loop(0, heads // 2)
                def _(head):
                    column_head(big, late * (heads // 2) + head)

                @pl.when(late == 1)
                def _():
                    inputs_block(big)

        for when in sorted(tasks):

            @pl.when(slot == when)
            def _(when=when):
                for task in tasks[when]:
                    task()

        done = slot - line.trip

        @pl.when((done >= 0) & (done < chunks))
        def _():
            at = span(done * HOP, HOP)
            gtok_ref[at, :] = (outer[done] + grad_ref[at, :]).astype(LOW)

    whole = (slice(None),) * (bits + 1)
    for half in range(2):
        size = width // 2
        orel_ref[whole + (slice(half * size, (half + 1) * size),)] = rel_all[half]
    line.drain(chunks)
    rel_line.drain(2)
    for job in jobs + rel_jobs:
        job.drain()
    for k in range(bits):
        small_copy(k).wait_send()
        for half in range(2):
            back_copy(half, k).wait_send()


def gradients(tokens, w_query, w_key, w_value, rel, kept, batch):
    slots, width = tokens.shape
    q = kept[0]
    heads, wide = q.shape[:2]
    mine = heads * HEAD
    bits = batch.bit_length() - 1
    assert 1 << bits == batch
    vmem = pl.BlockSpec(memory_space=pltpu.VMEM)
    far = pl.BlockSpec(memory_space=pl.ANY)
    chunks = slots // HOP
    split = (2,) * bits
    part = width // batch
    rel_part = rel.shape[0] // batch
    assert mine == PIECE
    pieces = [2, 3, 0, 1]
    shape = jax.ShapeDtypeStruct
    got = []
    for _ in pieces:
        got += [pltpu.VMEM((2,) * (bits - 1 - s) + (part, PIECE), FULL) for s in range(bits)]
    for _ in range(2):
        got += [pltpu.VMEM((2,) * (bits - 1 - s) + (rel_part, mine), FULL) for s in range(bits)]
    dma = pltpu.SemaphoreType.DMA
    return pl.pallas_call(
        functools.partial(gradient_kernel, bits=bits, pieces=pieces),
        out_shape=(
            shape((slots, width), LOW),
            shape((part, mine), FULL),
            shape((part, mine), FULL),
            shape((part, mine), FULL),
            shape((part, mine), FULL),
            shape(split + (rel_part, width), FULL),
            shape((8, width), FULL),
        ),
        in_specs=[far] * 5 + [vmem] * 3 + [far] * 3 + [vmem] * 2 + [far] * 2 + [vmem] * 3,
        out_specs=(vmem,) * 7,
        scratch_shapes=[
            pltpu.VMEM((chunks, HOP, width), FULL),
            pltpu.VMEM((chunks, HOP, width), FULL),
            pltpu.VMEM((chunks, HOP, width), FULL),
            pltpu.VMEM((LANES, wide), LOW),
            pltpu.VMEM((2, 3 * LANES, 3 * NB), FULL),
            pltpu.VMEM((LANES, 3 * NB), LOW),
            pltpu.VMEM((slots, mine), LOW),
            pltpu.VMEM((heads, LANES, HEAD), LOW),
            pltpu.VMEM((heads, 3 * NB, HEAD), FULL),
            pltpu.VMEM((len(pieces),) + split + (part, PIECE), FULL),
            pltpu.VMEM((2,) + split + (rel_part, mine), FULL),
            pltpu.VMEM((2, rel_part, mine), FULL),
            pltpu.VMEM((2, rel_part, width // 2), FULL),
            pltpu.VMEM((2, rel_part, width // 2), FULL),
            pltpu.VMEM((2, rel_part, width // 2), FULL),
            pltpu.VMEM((2,) + split + (rel_part, width // 2), FULL),
            pltpu.VMEM((bits, 8, width), FULL),
            pltpu.VMEM((bits, 8, width), FULL),
            pltpu.VMEM((width, mine), LOW),
            pltpu.VMEM((width, mine), LOW),
            pltpu.VMEM((width, mine), LOW),
            pltpu.VMEM((heads, slots, HEAD), LOW),
            pltpu.VMEM((heads, slots, HEAD), LOW),
            pltpu.VMEM((slots, width), LOW),
            pltpu.VMEM(rel.shape, LOW),
            pltpu.VMEM((heads, slots, HEAD), LOW),
            pltpu.VMEM((slots, width), FULL),
            pltpu.VMEM((slots, width), LOW),
            dma((10,)),
        ]
        + got
        + [dma((chunks,))] * 4
        + [dma((2,))] * 4
        + [dma((len(pieces) + 2, bits))] * 2
        + [dma((2, bits))] * 2
        + [dma((bits,))] * 2,
        compiler_params=pltpu.CompilerParams(
            vmem_limit_bytes=VMEM_LIMIT, collective_id=2, has_side_effects=True
        ),
        name="gradients",
    )(tokens, w_query, w_key, w_value, rel, *kept)


def finish_kernel(out, gtok, gwq, gwk, gwv, gwo, gwi, gwu, grel, small, *targets):
    (o_out, o_gtok, o_gwq, o_gwk, o_gwv, o_gwo, o_gwi, o_gwu, o_grel) = targets[:9]
    o_out[...] = out[...]
    o_gtok[...] = gtok[...]
    o_gwq[...] = gwq[...]
    o_gwk[...] = gwk[...]
    o_gwv[...] = gwv[...]
    o_gwo[...] = gwo[...].T
    o_gwi[...] = gwi[...]
    o_gwu[...] = gwu[...].T
    o_grel[...] = grel[...]
    for at, target in enumerate(targets[9:]):
        target[...] = small[at]


def finish(out, gtok, gwq, gwk, gwv, gwo, gwi, gwu, grel, small):
    vmem = pl.BlockSpec(memory_space=pltpu.VMEM)
    shape = jax.ShapeDtypeStruct
    same = lambda a: shape(a.shape, a.dtype)
    turn = lambda a: shape(a.shape[::-1], a.dtype)
    return pl.pallas_call(
        finish_kernel,
        out_shape=(same(out), same(gtok), same(gwq), same(gwk), same(gwv), turn(gwo), same(gwi), turn(gwu), same(grel))
        + (shape(small.shape[1:], FULL),) * 7,
        in_specs=[vmem] * 10,
        out_specs=(vmem,) * 16,
        compiler_params=pltpu.CompilerParams(vmem_limit_bytes=VMEM_LIMIT),
        name="finish",
    )(out, gtok, gwq, gwk, gwv, gwo, gwi, gwu, grel, small)


def shards(
    tokens,
    page_lengths,
    corners,
    w_query,
    w_key,
    w_value,
    w_output,
    b_output,
    gain_attn,
    shift_attn,
    w_inner,
    b_inner,
    w_outer,
    b_outer,
    gain_ffn,
    shift_ffn,
    rel_tables,
    cotangent,
):
    rel = rel_tables.reshape(3 * NB, rel_tables.shape[2])
    vectors = (b_output, gain_attn, shift_attn, b_inner, b_outer, gain_ffn, shift_ffn)
    q, k, qrel, ctx, output, *kept, gwi, gwu = layer(
        tokens, page_lengths, corners, w_query, w_key, w_value, rel,
        w_output, cotangent, w_inner, w_outer, vectors, lax.axis_size("batch"),
    )
    done = gradients(
        tokens, w_query, w_key, w_value, rel, (q, k, qrel, ctx, *kept), lax.axis_size("batch")
    )
    gtok, gwq, gwk, gwv, gwo, grel, small = done
    grel = grel.reshape(rel_tables.shape)
    (output, gtok, gwq, gwk, gwv, gwo, gwi, gwu, grel, gbo, gga, gsa, gbi, gbu, ggf, gsf) = finish(
        output, gtok, gwq, gwk, gwv, gwo, gwi, gwu, grel, small
    )
    return (output, gtok, gwq, gwk, gwv, gwo, gbo, gga, gsa, gwi, gbi, gwu, gbu, ggf, gsf, grel)


def solution(mesh):
    in_specs = (
        P("batch", None),
        P("batch"),
        P(None, "batch"),
        P(None, "head"),
        P(None, "head"),
        P(None, "head"),
        P("head", None),
        P(),
        P(),
        P(),
        P(None, "head"),
        P("head"),
        P("head", None),
        P(),
        P(),
        P(),
        P(),
        P("batch", None),
    )
    out_specs = (
        P("batch", None),
        P("batch", None),
        P("batch", "head"),
        P("batch", "head"),
        P("batch", "head"),
        P("head", "batch"),
        P(),
        P(),
        P(),
        P("batch", "head"),
        P("head"),
        P("head", "batch"),
        P(),
        P(),
        P(),
        P(),
    )
    return jax.shard_map(shards, mesh=mesh, in_specs=in_specs, out_specs=out_specs, check_vma=False)
```

```python
import functools

import jax
import jax.numpy as jnp
from jax import lax
from jax.experimental import pallas as pl
from jax.experimental.pallas import tpu as pltpu
from jax.sharding import PartitionSpec as P

HEAD = 64
NB = 128
BOX_STEP = 8
NEG_FILL = -1000000000.0
LANES = 128
HOP = 32
PAIR = 64
LAG = 2
PIECE = 256
STRIP = 128
RELAYS = 2
VMEM_LIMIT = 61 * 1024 * 1024
MESH = pl.DeviceIdType.MESH
LOW = jnp.bfloat16
FULL = jnp.float32


def dot_nn(a, b):
    return lax.dot_general(a, b, (((1,), (0,)), ((), ())), preferred_element_type=FULL)


def dot_nt(a, b):
    return lax.dot_general(a, b, (((1,), (1,)), ((), ())), preferred_element_type=FULL)


def dot_tn(a, b):
    return lax.dot_general(a, b, (((0,), (0,)), ((), ())), preferred_element_type=FULL)


def lane_gather(table, index):
    return jnp.take_along_axis(table, index, axis=1, mode="promise_in_bounds")


def bucket(step):
    return jnp.clip(step, -(NB // 2), NB // 2 - 1) + NB // 2


def span(start, size):
    return pl.ds(pl.multiple_of(start, size), size)


class Line:
    def __init__(self, axis, own, inner, outer, sems, lag=LAG):
        self.axis, self.own, self.inner, self.outer, self.lag = axis, own, inner, outer, lag
        self.in_send, self.in_recv, self.out_send, self.out_recv = sems
        self.ring, self.wide_ring = own.shape[0], outer.shape[0]
        self.n = lax.axis_size(axis)
        me = lax.axis_index(axis)
        left = me < self.n // 2
        self.depth = jnp.where(left, me, self.n - 1 - me)
        self.inward = jnp.where(left, me + 1, me - 1)
        self.outward = jnp.where(self.depth == 0, self.inward, jnp.where(left, me - 1, me + 1))
        self.last = self.n // 2 - 1
        self.trip = self.lag * (self.n - 1)

    def greet(self, barrier):
        pl.semaphore_signal(barrier, inc=1, device_id={self.axis: self.inward}, device_id_type=MESH)

        @pl.when(self.depth > 0)
        def _():
            pl.semaphore_signal(
                barrier, inc=1, device_id={self.axis: self.outward}, device_id_type=MESH
            )

    def greeted(self):
        return jnp.where(self.depth > 0, 2, 1)

    def copy(self, source, target, send, recv, to):
        return pltpu.make_async_remote_copy(
            src_ref=source,
            dst_ref=target,
            send_sem=send,
            recv_sem=recv,
            device_id={self.axis: to},
            device_id_type=MESH,
        )

    def total(self, u):
        return lax.rem(u, self.wide_ring)

    def out_copy(self, u):
        o = self.total(u)
        return self.copy(
            self.outer.at[o], self.outer.at[o], self.out_send.at[o], self.out_recv.at[o], self.outward
        )

    def in_copy(self, c, source):
        return self.copy(
            source, self.inner.at[c], self.in_send.at[c], self.in_recv.at[c], self.inward
        )

    def send_in(self, u, c, source):
        @pl.when(self.depth < self.last)
        def _():
            self.in_copy(c, source).start()

        @pl.when(self.depth == self.last)
        def _():
            o = self.total(u)
            self.copy(
                source, self.outer.at[o], self.in_send.at[c], self.out_recv.at[o], self.inward
            ).start()

    def step(self, slot, count):
        here = slot - self.lag * self.depth

        @pl.when((here >= 0) & (here < count))
        def _():
            u = here
            c = lax.rem(u, self.ring)

            @pl.when(self.depth == 0)
            def _():
                self.send_in(u, c, self.own.at[c])

            @pl.when(self.depth > 0)
            def _():
                @pl.when(u >= self.ring)
                def _():
                    self.out_copy(u - self.ring).wait_send()

                self.in_copy(c, self.own.at[c]).wait_recv()
                self.inner[c] += self.own[c]
                self.send_in(u, c, self.inner.at[c])

        back = slot - self.lag * (self.n - 1 - self.depth)

        @pl.when((back >= 0) & (back < count))
        def _():
            u = back
            c = lax.rem(u, self.ring)
            self.in_copy(c, self.own.at[c]).wait_send()
            self.out_copy(u).wait_recv()

            @pl.when(self.depth == self.last)
            def _():
                self.outer[self.total(u)] += self.inner[c] if self.last > 0 else self.own[c]

            @pl.when(self.depth > 0)
            def _():
                self.out_copy(u).start()

    def drain(self, count):
        @pl.when(self.depth > 0)
        def _():
            @pl.loop(count - self.ring, count)
            def _(u):
                self.out_copy(u).wait_send()


class Rounds:
    def __init__(self, order, work, got, out, rounds, send, recv, credit):
        self.order, self.work, self.got, self.out, self.rounds = order, work, got, out, rounds
        self.send, self.recv, self.credit = send, recv, credit
        self.b = lax.axis_index("batch")

    def partner(self, stage):
        return {"batch": self.b ^ (1 << self.order[stage])}

    def part(self, stage, flip):
        bit = self.order[stage]
        rest = sorted(self.order[stage:], reverse=True)
        mine = (self.b >> bit) & 1
        pick = 1 - mine if flip else mine
        return tuple(pick if k == bit else slice(None) for k in rest)

    def source(self, stage):
        return self.work if stage == 0 else self.got[stage - 1]

    def copy(self, stage):
        return pltpu.make_async_remote_copy(
            src_ref=self.source(stage).at[self.part(stage, True)],
            dst_ref=self.got[stage],
            send_sem=self.send.at[stage],
            recv_sem=self.recv.at[stage],
            device_id=self.partner(stage),
            device_id_type=MESH,
        )

    def start(self, stage, number):
        if number > 0:
            pl.semaphore_wait(self.credit.at[stage], 1)
        self.copy(stage).start()

    def free(self, stage, number):
        if number + 1 < self.rounds:
            pl.semaphore_signal(
                self.credit.at[stage], inc=1, device_id=self.partner(stage), device_id_type=MESH
            )

    def begin(self, number, value):
        self.work[...] = value.reshape(self.work.shape)
        self.start(0, number)

    def turn(self, stage, number):
        self.copy(stage).wait_recv()
        value = self.source(stage)[self.part(stage, False)] + self.got[stage][...]
        last = stage + 1 == len(self.order)
        if last:
            size = value.shape[1]
            self.out[:, number * size : (number + 1) * size] = value
        else:
            self.got[stage][...] = value
        self.copy(stage).wait_send()
        if stage > 0:
            self.free(stage - 1, number)
        if last:
            self.free(stage, number)
        else:
            self.start(stage + 1, number)


def batch_orders(bits):
    return (list(range(bits)), [0] + list(range(bits - 1, 0, -1)))


def greet_batch(barrier, bits):
    b = lax.axis_index("batch")
    for k in range(bits):
        pl.semaphore_signal(barrier, inc=1, device_id={"batch": b ^ (1 << k)}, device_id_type=MESH)


def centre(values):
    average = jnp.mean(values, axis=-1, keepdims=True)
    centered = values - average
    spread = jnp.mean(centered * centered, axis=-1, keepdims=True)
    scaling = lax.rsqrt(spread + 1e-05)
    return centered * scaling, scaling


def norm_inward(scaled, normed, scaling):
    return scaling * (
        scaled
        - jnp.mean(scaled, axis=-1, keepdims=True)
        - normed * jnp.mean(scaled * normed, axis=-1, keepdims=True)
    )


def fold_rows(values):
    rows, width = values.shape
    return jnp.sum(values.reshape(rows // 8, 8, width), axis=0)


def attention_setup(tok_ref, wq_ref, wk_ref, wv_ref, rel_ref, corner_ref,
                    q_ref, k_ref, v_ref, krel_ref, qrel_ref, tq_ref, tk_ref, idx_ref, col_ref, row_ref):
    slots = tok_ref.shape[0]
    heads, wide = q_ref.shape[0], q_ref.shape[1]
    chunks = wide // LANES
    for weight, target in ((wq_ref, q_ref), (wk_ref, k_ref), (wv_ref, v_ref)):
        value = dot_nn(tok_ref[...], weight[...]).astype(LOW)
        for head in range(heads):
            target[head, :slots, :] = value[:, head * HEAD : (head + 1) * HEAD]
            if wide > slots:
                target[head, slots:, :] = jnp.zeros((wide - slots, HEAD), LOW)
    for weight, target in ((wk_ref, krel_ref), (wq_ref, qrel_ref)):
        value = dot_nn(rel_ref[...], weight[...]).astype(LOW)
        for head in range(heads):
            target[head] = value[:, head * HEAD : (head + 1) * HEAD]
    for head in range(heads):
        tq_ref[head] = dot_nt(q_ref[head, :slots, :], krel_ref[head])
        tk_ref[head] = dot_nt(k_ref[head], qrel_ref[head])
    row_ref[...] = jnp.zeros_like(row_ref)
    row_ref[:, :slots] = corner_ref[...]
    for kind in range(2):
        for big in range(chunks):
            here = slice(big * LANES, (big + 1) * LANES)
            col_ref[kind, here, :] = jnp.broadcast_to(row_ref[kind : kind + 1, here], (LANES, LANES)).T

    @pl.loop(0, chunks)
    def _(big):
        at = span(big * LANES, LANES)
        for kind in range(2):
            own = col_ref[kind, at, :]
            for chunk in range(chunks):
                other = row_ref[kind : kind + 1, chunk * LANES : (chunk + 1) * LANES]
                idx_ref[kind, chunk, at, :] = bucket((own - other) >> 3)


def attention_block(big, head, length, q_ref, k_ref, v_ref, tq_ref, tk_ref, idx_ref, log_ref, attend_ref, ctx_ref):
    wide = q_ref.shape[1]
    chunks = wide // LANES
    slots = attend_ref.shape[1]
    scale = (7.0 * HEAD) ** (-0.5)
    rows = min(LANES, slots - big * LANES)
    some = slice(big * LANES, big * LANES + rows)
    slant = lax.broadcasted_iota(jnp.int32, (LANES, LANES), 0) - lax.broadcasted_iota(
        jnp.int32, (LANES, LANES), 1
    )
    log_ref[:rows, :] = dot_nt(q_ref[head, some, :], k_ref[head])
    for chunk in range(chunks):
        there = slice(chunk * LANES, (chunk + 1) * LANES)
        away = (big - chunk) * LANES
        toward = log_ref[:rows, there]
        if abs(big - chunk) >= 2:
            lane = NB - 1 if away > 0 else 0
            toward = toward + tq_ref[head, some, lane : lane + 1]
            lane = NB - 1 - lane
            beside = jnp.broadcast_to(tk_ref[head, there, lane : lane + 1], (LANES, LANES))
        else:
            toward = toward + lane_gather(tq_ref[head, some, :NB], bucket(slant + away)[:rows])
            beside = lane_gather(tk_ref[head, there, :NB], bucket(slant - away))
        for kind in range(2):
            lanes = slice((kind + 1) * NB, (kind + 2) * NB)
            toward = toward + lane_gather(tq_ref[head, some, lanes], idx_ref[kind, chunk, some, :])
            beside = beside + lane_gather(tk_ref[head, there, lanes], idx_ref[kind, big, there, :])
        log_ref[:rows, there] = toward + beside.T[:rows]
    block = 32
    for start in range(0, rows, block):
        at = slice(start, start + block)
        j_at = lax.broadcasted_iota(jnp.int32, (block, wide), 1)
        masked = jnp.where(j_at < length, log_ref[at, :], NEG_FILL)
        peak = jnp.max(masked, axis=-1, keepdims=True)
        grown = jnp.exp((masked - peak) * scale)
        total = jnp.sum(grown, axis=-1, keepdims=True)
        attend_ref[head, big * LANES + start : big * LANES + start + block, :] = (
            grown * (1.0 / total)
        ).astype(LOW)
    ctx_ref[head, some, :] = dot_nn(attend_ref[head, some, :], v_ref[head]).astype(LOW)


def make_steps(step_ref, col_ref, slots):
    wide = step_ref.shape[1]
    block = 64
    if wide > slots:
        step_ref[:, slots:, :] = jnp.zeros_like(step_ref[:, slots:, :])

    @pl.loop(0, slots // block)
    def _(step):
        at = span(step * block, block)
        quotient = lax.broadcasted_iota(jnp.int32, (block, NB), 1) * BOX_STEP
        for kind in range(2):
            own = col_ref[kind, at, :]
            for rest in range(BOX_STEP):
                lanes = slice(rest * NB, (rest + 1) * NB)
                step_ref[kind, at, lanes] = (own <= quotient + rest).astype(FULL).astype(LOW)


def fold_at(kind, r, at):
    return (kind, at, slice(r % 3 * NB, (r % 3 + 1) * NB))


def bucket_sums(big, rows, mat, step_ref, col_ref, fold_ref, hist_ref):
    chunks = step_ref.shape[1] // LANES
    for kind in range(2):
        value = dot_nn(mat[...], step_ref[kind])
        for r in range(BOX_STEP):
            fold_ref[fold_at(kind, r, slice(r // 3 * LANES, r // 3 * LANES + rows))] = value[
                :, r * NB : (r + 1) * NB
            ]
    block = rows

    def some(local):
        at = slice(local, local + block)
        far = slice(big * LANES + local, big * LANES + local + block)
        lane = lax.broadcasted_iota(jnp.int32, (block, NB), 1)
        row = lax.broadcasted_iota(jnp.int32, (block, NB), 0) + local
        part = [mat[at, c * LANES : (c + 1) * LANES].astype(FULL) for c in range(chunks)]
        zero = jnp.zeros((block, LANES), FULL)
        before = part[big - 1] if big >= 1 else zero
        after = part[big + 1] if big + 1 < chunks else zero
        mid = part[big]
        delta = lane - row
        window = jnp.where(delta > NB // 2, before, jnp.where(delta < 1 - NB // 2, after, mid))
        spread = lane_gather(window, (row + NB // 2 - lane) & (NB - 1))
        under = jnp.where(delta <= NB // 2 + 1, before, 0.0) + jnp.where(
            delta <= 1 - NB // 2, mid, 0.0
        )
        over = jnp.where(delta >= NB // 2, mid, 0.0) + jnp.where(delta >= -(NB // 2), after, 0.0)
        for c in range(big - 1):
            under = under + part[c]
        for c in range(big + 2, chunks):
            over = over + part[c]
        under = jnp.sum(under, axis=-1, keepdims=True)
        over = jnp.sum(over, axis=-1, keepdims=True)
        spread = jnp.where(lane == 0, over, jnp.where(lane == NB - 1, under, spread))
        hist_ref[at, 0:NB] = spread.astype(LOW)
        for kind in range(2):
            own = col_ref[kind, far, :]
            groups = [
                fold_ref[fold_at(kind, r, slice(r // 3 * LANES + local, r // 3 * LANES + local + block))]
                for r in range(BOX_STEP)
            ]
            every = groups[-1][:, NB - 1 : NB]
            for bit in range(3):
                odd = (own & (1 << bit)) != 0
                groups = [
                    jnp.where(odd, groups[g + 1], groups[g]) for g in range(0, len(groups), 2)
                ]
            index = (own >> 3) + NB // 2 - lane
            found = lane_gather(groups[0], index & (NB - 1))
            found = jnp.where(index < 0, 0.0, found)
            found = jnp.where((index >= NB) | (lane == 0), every, found)
            following = pltpu.roll(found, NB - 1, 1)
            found = found - jnp.where(lane == NB - 1, 0.0, following)
            hist_ref[at, (kind + 1) * NB : (kind + 2) * NB] = found.astype(LOW)

    some(0)


def copies(pairs, sems):
    return [
        pltpu.make_async_copy(source, target, sems.at[at]) for at, (source, target) in enumerate(pairs)
    ]


def layer_kernel(
    length_ref, tok_ref, wq_ref, wk_ref, wv_ref, rel_ref, corner_ref,
    wo_in, cot_in, wi_in, wu_in, bo_ref, ga_ref, sa_ref, bi_ref, bu_ref, gf_ref, sf_ref,
    q_out, k_out, qrel_out, ctx_ref, out_ref, grad_ref, grad_low_ref, small_ref, mat_ref,
    gq_ref, gv_ref, gkrel_ref, step_out, col_out, owi_ref, owu_ref,
    hidden_ref, active_ref, mid_low_ref, inner_low_ref, v_ref, krel_ref, attend_ref, tq_ref, tk_ref, idx_ref, row_ref, log_ref,
    own, inner, outer, normed_ref, scale_ref, sums_ref, gc_ref, hist_ref, gv_sum, block_ref,
    wo_ref, cot_ref, wi_ref, wu_ref, q_ref, k_ref, qrel_ref, step_ref, col_ref,
    in_send, in_recv, out_send, out_recv, block_sem, load_sem, save_sem, *rest,
    bits,
):
    slots = tok_ref.shape[0]
    chunks = slots // HOP
    heads, wide = q_ref.shape[0], q_ref.shape[1]
    blocks = wide // LANES
    per = LANES // HOP
    scale = (7.0 * HEAD) ** (-0.5)
    line = Line("head", own, inner, outer, (in_send, in_recv, out_send, out_recv))
    barrier = pltpu.get_barrier_semaphore()
    line.greet(barrier)
    greet_batch(barrier, bits)
    loads = copies(((wo_in, wo_ref), (cot_in, cot_ref), (wi_in, wi_ref), (wu_in, wu_ref)), load_sem)
    saves = copies(
        ((q_ref, q_out), (k_ref, k_out), (qrel_ref, qrel_out), (col_ref, col_out), (step_ref, step_out)),
        save_sem,
    )
    for load in loads:
        load.start()
    share = owi_ref.shape[1] // RELAYS
    rounds = share // STRIP
    relays = []
    for at in range(2 * RELAYS):
        work, *got = rest[at * (bits + 1) : (at + 1) * (bits + 1)]
        first = 2 * RELAYS * (bits + 1) + 3 * at
        sems = rest[first : first + 3]
        start = at // 2 * share
        out = (owi_ref, owu_ref)[at % 2].at[:, start : start + share]
        relays.append(Rounds(batch_orders(bits)[at % 2], work, got, out, rounds, *sems))
    sums_ref[...] = jnp.zeros_like(sums_ref)
    gv_sum[...] = jnp.zeros_like(gv_sum)
    gkrel_ref[...] = jnp.zeros_like(gkrel_ref)
    attention_setup(tok_ref, wq_ref, wk_ref, wv_ref, rel_ref, corner_ref,
                    q_ref, k_ref, v_ref, krel_ref, qrel_ref, tq_ref, tk_ref, idx_ref, col_ref, row_ref)
    for save in saves[:4]:
        save.start()
    for load in loads:
        load.wait()
    pl.semaphore_wait(barrier, line.greeted() + bits)
    root = 0.5**0.5
    bell = (0.5 / jnp.pi) ** 0.5

    def forward_head(big, head):
        attention_block(big, head, length_ref[0], q_ref, k_ref, v_ref, tq_ref, tk_ref, idx_ref, log_ref,
                        attend_ref, ctx_ref)

    def put(c, value):
        for part in range(PAIR // HOP):
            own[c * (PAIR // HOP) + part] = value[part * HOP : (part + 1) * HOP]

    def got(u):
        first = line.total(u * (PAIR // HOP))
        return jnp.concatenate([outer[first + part] for part in range(PAIR // HOP)], axis=0)

    def project(c):
        at = span(c * PAIR, PAIR)
        context = jnp.concatenate([ctx_ref[head, at, :] for head in range(heads)], axis=1)
        put(c, dot_nn(context, wo_ref[...]))

    def after_attention(c, u):
        at = span(c * PAIR, PAIR)
        normed, scaling = centre(got(u) + bo_ref[...] + tok_ref[at, :].astype(FULL))
        normed_ref[at, :] = normed
        scale_ref[at, :] = scaling
        hidden_low = (normed * ga_ref[...] + sa_ref[...]).astype(LOW)
        hidden_ref[at, :] = hidden_low
        pre = dot_nn(hidden_low, wi_ref[...]) + bi_ref[...]
        grad_ref[at, :] = pre
        active = (pre * (1.0 + lax.erf(pre * root)) * 0.5).astype(LOW)
        active_ref[at, :] = active
        put(c, dot_nn(active, wu_ref[...]))

    def after_ffn(c, u):
        at = span(c * PAIR, PAIR)
        hidden = normed_ref[at, :] * ga_ref[...] + sa_ref[...]
        normed, scaling = centre(got(u) + bu_ref[...] + hidden)
        out_ref[at, :] = (normed * gf_ref[...] + sf_ref[...]).astype(LOW)
        upstream = cot_ref[at, :].astype(FULL)
        grad_mid = norm_inward(upstream * gf_ref[...], normed, scaling)
        sums_ref[4] += fold_rows(grad_mid)
        sums_ref[5] += fold_rows(upstream * normed)
        sums_ref[6] += fold_rows(upstream)
        pre = grad_ref[at, :]
        grad_ref[at, :] = grad_mid
        mid_low = grad_mid.astype(LOW)
        mid_low_ref[at, :] = mid_low
        grad_active = dot_nt(mid_low, wu_ref[...])
        slope = (1.0 + lax.erf(pre * root)) * 0.5 + pre * jnp.exp(-0.5 * pre * pre) * bell
        inner_low = (grad_active * slope).astype(LOW)
        sums_ref[3] += fold_rows(inner_low.astype(FULL))
        inner_low_ref[at, :] = inner_low
        put(c, dot_nt(inner_low, wi_ref[...]))

    def after_hidden(c, u):
        at = span(c * PAIR, PAIR)
        upstream = got(u) + grad_ref[at, :]
        normed = normed_ref[at, :]
        grad_attn = norm_inward(upstream * ga_ref[...], normed, scale_ref[at, :])
        sums_ref[0] += fold_rows(grad_attn)
        sums_ref[1] += fold_rows(upstream * normed)
        sums_ref[2] += fold_rows(upstream)
        grad_ref[at, :] = grad_attn
        grad_low_ref[at, :] = grad_attn.astype(LOW)

    def backward_block(big):
        rows = min(LANES, slots - big * LANES)
        some = slice(big * LANES, big * LANES + rows)
        value = dot_nt(grad_low_ref[some, :], wo_ref[...]).astype(LOW)
        for head in range(heads):
            gc_ref[head, :rows, :] = value[:, head * HEAD : (head + 1) * HEAD]

    def block_copy(big, head, rows):
        buffer = lax.rem(head, 2)
        return pltpu.make_async_copy(
            block_ref.at[buffer, :rows, :],
            mat_ref.at[head, pl.ds(big * LANES, rows), :],
            block_sem.at[buffer],
        )

    def backward_head(big, head):
        rows = min(LANES, slots - big * LANES)
        some = slice(big * LANES, big * LANES + rows)

        @pl.when(head >= 2)
        def _():
            block_copy(big, head - 2, rows).wait()

        if big > 0:

            @pl.when(head < 2)
            def _():
                block_copy(big - 1, head + 2, LANES).wait()

        gc = gc_ref[head, :rows, :]
        grad_attend = dot_nt(gc, v_ref[head])
        mean = jnp.sum(gc.astype(FULL) * ctx_ref[head, some, :].astype(FULL), axis=-1, keepdims=True)
        attend = attend_ref[head, some, :]
        mat = block_ref.at[lax.rem(head, 2), :rows, :]
        mat[...] = (attend.astype(FULL) * (grad_attend - mean)).astype(LOW)
        block_copy(big, head, rows).start()
        gv_sum[head] += dot_tn(attend, gc)
        bucket_sums(big, rows, mat, step_ref, col_ref, tq_ref, hist_ref)
        hist = hist_ref[:rows, :]
        gq = dot_nn(mat[...], k_ref[head]) + dot_nn(hist, krel_ref[head])
        gq_ref[head, some, :] = (gq * scale).astype(LOW)
        gkrel_ref[head] += dot_tn(hist, q_ref[head, some, :])

    def relay_begin(at, number):
        start = at // 2 * share + number * STRIP
        lanes = slice(start, start + STRIP)
        if at % 2 == 0:
            value = dot_tn(hidden_ref[...], inner_low_ref[:, lanes])
        else:
            value = dot_tn(mid_low_ref[...], active_ref[:, lanes])
        relays[at].begin(number, value)

    for head in range(heads):
        forward_head(0, head)
    count = 3 * chunks
    ratio = PAIR // HOP
    first_back = 2 * chunks + line.trip + per
    last_slot = first_back + (blocks - 1) * per + heads
    tasks = {}

    def add(when, task):
        tasks.setdefault(when, []).append(task)

    after = 2 * chunks + line.trip
    for number in range(rounds):
        for at in range(2 * RELAYS):
            base = after + 5 * number + at
            add(base, lambda at=at, number=number: relay_begin(at, number))
            for stage in range(bits):
                when = base + 2 + 2 * stage
                add(when, lambda at=at, stage=stage, number=number: relays[at].turn(stage, number))

    @pl.loop(0, max(count + line.trip, last_slot, max(tasks) + 1))
    def _(slot):
        @pl.when((slot < chunks) & (lax.rem(slot, ratio) == 0))
        def _():
            project(slot // ratio)

        line.step(slot, count)
        ahead = slot + per
        for big in range(1, blocks):

            @pl.when(ahead // per == big)
            def _(big=big):
                forward_head(big, lax.rem(ahead, per))

        done = slot - line.trip - (ratio - 1)
        pair = done // ratio
        ready = (done >= 0) & (lax.rem(done + ratio, ratio) == 0)
        pairs = chunks // ratio

        @pl.when(ready & (pair < pairs))
        def _():
            after_attention(pair, pair)

        @pl.when(ready & (pair >= pairs) & (pair < 2 * pairs))
        def _():
            after_ffn(pair - pairs, pair)

        @pl.when(ready & (pair >= 2 * pairs) & (pair < 3 * pairs))
        def _():
            after_hidden(pair - 2 * pairs, pair)

        @pl.when(slot == 2 * chunks)
        def _():
            make_steps(step_ref, col_ref, slots)
            saves[4].start()

        for when in sorted(tasks):

            @pl.when(slot == when)
            def _(when=when):
                for task in tasks[when]:
                    task()

        since = slot - first_back
        for big in range(blocks):

            @pl.when((since >= 0) & (since // per == big))
            def _(big=big):
                at_head = lax.rem(since, per)

                @pl.when(at_head == 0)
                def _():
                    backward_block(big)

                backward_head(big, at_head)

    for at in range(7):
        small_ref[at : at + 1, :] = jnp.sum(sums_ref[at], axis=0, keepdims=True)
    small_ref[7:8, :] = jnp.zeros_like(small_ref[7:8, :])
    for head in range(heads):
        gv_ref[head] = gv_sum[head, :slots, :].astype(LOW)
        gkrel_ref[head] = gkrel_ref[head] * scale
    for head in range(heads - 2, heads):
        block_copy(blocks - 1, head, slots - (blocks - 1) * LANES).wait()
    line.drain(count)
    for save in saves:
        save.wait()


def layer(
    tokens, length, corners, w_query, w_key, w_value, rel, w_output, cotangent, w_inner, w_outer, vectors, batch
):
    slots, width = tokens.shape
    units = w_inner.shape[1]
    mine = w_query.shape[1]
    heads = mine // HEAD
    wide = -(-slots // LANES) * LANES
    assert units == width and heads == LANES // HOP and slots % PAIR == 0
    vmem = pl.BlockSpec(memory_space=pltpu.VMEM)
    far = pl.BlockSpec(memory_space=pl.ANY)
    chunks = slots // HOP
    shape = jax.ShapeDtypeStruct
    dma = pltpu.SemaphoreType.DMA
    bits = batch.bit_length() - 1
    assert 1 << bits == batch
    part = width // batch
    relay = [pltpu.VMEM((2,) * (bits - s) + (part, STRIP), FULL) for s in range(bits + 1)]
    return pl.pallas_call(
        functools.partial(layer_kernel, bits=bits),
        out_shape=(
            shape((heads, wide, HEAD), LOW),
            shape((heads, wide, HEAD), LOW),
            shape((heads, 3 * NB, HEAD), LOW),
            shape((heads, slots, HEAD), LOW),
            shape((slots, width), LOW),
            shape((slots, width), FULL),
            shape((slots, width), LOW),
            shape((8, width), FULL),
            shape((heads, slots, wide), LOW),
            shape((heads, slots, HEAD), LOW),
            shape((heads, slots, HEAD), LOW),
            shape((heads, 3 * NB, HEAD), FULL),
            shape((2, wide, BOX_STEP * NB), LOW),
            shape((2, wide, LANES), jnp.int32),
            shape((part, units), FULL),
            shape((part, units), FULL),
        ),
        in_specs=[pl.BlockSpec(memory_space=pltpu.SMEM)] + [vmem] * 6 + [far] * 4 + [vmem] * 7,
        out_specs=(far,) * 3 + (vmem,) * 5 + (far,) + (vmem,) * 3 + (far,) * 2 + (vmem,) * 2,
        scratch_shapes=[
            pltpu.VMEM((slots, width), LOW),
            pltpu.VMEM((slots, units), LOW),
            pltpu.VMEM((slots, width), LOW),
            pltpu.VMEM((slots, units), LOW),
            pltpu.VMEM((heads, wide, HEAD), LOW),
            pltpu.VMEM((heads, 3 * NB, HEAD), LOW),
            pltpu.VMEM((heads, slots, wide), LOW),
            pltpu.VMEM((heads, slots, 3 * NB), FULL),
            pltpu.VMEM((heads, wide, 3 * NB), FULL),
            pltpu.VMEM((2, wide // LANES, wide, LANES), jnp.int32),
            pltpu.VMEM((2, wide), jnp.int32),
            pltpu.VMEM((LANES, wide), FULL),
            pltpu.VMEM((chunks, HOP, width), FULL),
            pltpu.VMEM((chunks, HOP, width), FULL),
            pltpu.VMEM((2 * chunks, HOP, width), FULL),
            pltpu.VMEM((slots, width), FULL),
            pltpu.VMEM((slots, 1), FULL),
            pltpu.VMEM((7, 8, width), FULL),
            pltpu.VMEM((heads, LANES, HEAD), LOW),
            pltpu.VMEM((LANES, 3 * NB), LOW),
            pltpu.VMEM((heads, wide, HEAD), FULL),
            pltpu.VMEM((2, LANES, wide), LOW),
            pltpu.VMEM((mine, width), LOW),
            pltpu.VMEM((slots, width), LOW),
            pltpu.VMEM((width, units), LOW),
            pltpu.VMEM((units, width), LOW),
            pltpu.VMEM((heads, wide, HEAD), LOW),
            pltpu.VMEM((heads, wide, HEAD), LOW),
            pltpu.VMEM((heads, 3 * NB, HEAD), LOW),
            pltpu.VMEM((2, wide, BOX_STEP * NB), LOW),
            pltpu.VMEM((2, wide, LANES), jnp.int32),
            dma((chunks,)),
            dma((chunks,)),
            dma((2 * chunks,)),
            dma((2 * chunks,)),
            dma((2,)),
            dma((4,)),
            dma((5,)),
        ]
        + relay * (2 * RELAYS)
        + [dma((bits,)), dma((bits,)), pltpu.SemaphoreType.REGULAR((bits,))] * (2 * RELAYS),
        compiler_params=pltpu.CompilerParams(
            vmem_limit_bytes=VMEM_LIMIT, collective_id=1, has_side_effects=True
        ),
        name="layer",
    )(length, tokens, w_query, w_key, w_value, rel, corners,
      w_output, cotangent, w_inner, w_outer, *[v.reshape(1, -1) for v in vectors])


class Halving:
    def __init__(self, order, source, got, out, send, recv):
        self.order, self.source, self.got, self.out = order, source, got, out
        self.send, self.recv = send, recv
        self.b = lax.axis_index("batch")

    def part(self, stage, flip):
        bit = self.order[stage]
        rest = sorted(self.order[stage:], reverse=True)
        mine = (self.b >> bit) & 1
        pick = 1 - mine if flip else mine
        return tuple(pick if k == bit else slice(None) for k in rest)

    def copy(self, stage):
        source = self.source if stage == 0 else self.got[stage - 1]
        return pltpu.make_async_remote_copy(
            src_ref=source.at[self.part(stage, True)],
            dst_ref=self.got[stage],
            send_sem=self.send.at[stage],
            recv_sem=self.recv.at[stage],
            device_id={"batch": self.b ^ (1 << self.order[stage])},
            device_id_type=MESH,
        )

    def start(self):
        self.copy(0).start()

    def turn(self, stage):
        self.copy(stage).wait_recv()
        kept = self.source if stage == 0 else self.got[stage - 1]
        value = kept[self.part(stage, False)] + self.got[stage][...]
        if stage == 0:
            self.copy(0).wait_send()
        if stage + 1 < len(self.order):
            self.got[stage][...] = value
            self.copy(stage + 1).start()
        else:
            self.out[...] = value

    def drain(self):
        for stage in range(1, len(self.order)):
            self.copy(stage).wait_send()


def gradient_kernel(
    tok_in, wq_in, wk_in, wv_in, rel_in_hbm,
    q_ref, k_ref, qrel_ref, ctx_in, grad_in, grad_low_in, small_ref, mat_ref,
    gq_in, gv_in, gkrel_ref, step_ref, col_ref,
    gtok_ref, owq_ref, owk_ref, owv_ref, owo_ref, orel_ref, osmall_ref,
    own, inner, outer, turned_ref, fold_ref, hist_ref, gk_ref, gk_low_ref, gqrel_sum,
    work_ref, rel_work, rel_sum, rel_own, rel_in, rel_out, rel_all, small_sum, small_got,
    wq_ref, wk_ref, wv_ref, gq_ref, gv_ref, tok_ref, rel_ref, ctx_ref, grad_ref, grad_low_ref, load_sem,
    *rest,
    bits, pieces,
):
    jobs_all = len(pieces) + 2
    got = [rest[at * bits : (at + 1) * bits] for at in range(jobs_all)]
    (in_send, in_recv, out_send, out_recv, rin_send, rin_recv, rout_send, rout_recv,
     piece_send, piece_recv, back_send, back_recv, small_send, small_recv) = rest[jobs_all * bits :]
    slots, width = tok_ref.shape
    chunks = slots // HOP
    heads, wide = q_ref.shape[0], q_ref.shape[1]
    blocks = wide // LANES
    per = LANES // HOP
    scale = (7.0 * HEAD) ** (-0.5)
    line = Line("head", own, inner, outer, (in_send, in_recv, out_send, out_recv))
    rel_line = Line("head", rel_own, rel_in, rel_out, (rin_send, rin_recv, rout_send, rout_recv), 1)
    b = lax.axis_index("batch")
    barrier = pltpu.get_barrier_semaphore()
    line.greet(barrier)
    greet_batch(barrier, bits)
    loads = copies(
        (
            (wq_in, wq_ref), (wk_in, wk_ref), (wv_in, wv_ref), (gq_in, gq_ref), (gv_in, gv_ref),
            (tok_in, tok_ref), (rel_in_hbm, rel_ref), (ctx_in, ctx_ref), (grad_in, grad_ref),
            (grad_low_in, grad_low_ref),
        ),
        load_sem,
    )
    for load in loads:
        load.start()
    orders = batch_orders(bits)
    outs = (owq_ref, owk_ref, owv_ref, owo_ref)
    jobs = []
    for at, which in enumerate(pieces):
        jobs.append(
            Halving(orders[at % 2], work_ref.at[at], got[at], outs[which], piece_send.at[at], piece_recv.at[at])
        )
    rel_jobs = []
    for side in range(2):
        at = len(pieces) + side
        rel_jobs.append(
            Halving(orders[side], rel_work.at[side], got[at], rel_sum.at[side], piece_send.at[at], piece_recv.at[at])
        )

    def heads_of(ref):
        return jnp.concatenate([ref[head] for head in range(heads)], axis=1)

    def make(at):
        which = pieces[at]
        if which == 0:
            value = dot_tn(tok_ref[...], heads_of(gq_ref)) + dot_tn(rel_ref[...], rel_low(1))
        elif which == 1:
            value = dot_tn(tok_ref[...], gk_ref[...]) + dot_tn(rel_ref[...], rel_low(0))
        elif which == 2:
            value = dot_tn(tok_ref[...], heads_of(gv_ref))
        else:
            value = dot_tn(grad_low_ref[...], heads_of(ctx_ref))
        target = work_ref.at[at]
        target[...] = value.reshape(target.shape)
        jobs[at].start()

    def rel_low(side):
        return heads_of(gqrel_sum if side else gkrel_ref).astype(LOW)

    def rel_start(side):
        if side:
            for head in range(heads):
                gqrel_sum[head] = gqrel_sum[head] * scale
        target = rel_work.at[side]
        target[...] = heads_of(gqrel_sum if side else gkrel_ref).reshape(target.shape)
        rel_jobs[side].start()

    def small_copy(k):
        return pltpu.make_async_remote_copy(
            src_ref=small_sum.at[k],
            dst_ref=small_got.at[k],
            send_sem=small_send.at[k],
            recv_sem=small_recv.at[k],
            device_id={"batch": b ^ (1 << k)},
            device_id_type=MESH,
        )

    def small_turn(k):
        small_copy(k).wait_recv()
        value = small_sum[k] + small_got[k]
        if k + 1 < bits:
            small_sum[k + 1] = value
            small_copy(k + 1).start()
        else:
            osmall_ref[...] = value

    def back_copy(half, turn):
        sequence = orders[half][::-1]
        region = tuple(
            slice(None) if k in sequence[:turn] else (b >> k) & 1 for k in range(bits - 1, -1, -1)
        )
        target = rel_all.at[(half,) + region]
        return pltpu.make_async_remote_copy(
            src_ref=target,
            dst_ref=target,
            send_sem=back_send.at[half, turn],
            recv_sem=back_recv.at[half, turn],
            device_id={"batch": b ^ (1 << sequence[turn])},
            device_id_type=MESH,
        )

    def back_turn(half, turn):
        back_copy(half, turn).wait_recv()
        if turn + 1 < bits:
            back_copy(half, turn + 1).start()

    def rel_meet():
        value = dot_nt(rel_sum[0].astype(LOW), wk_ref[...]) + dot_nt(rel_sum[1].astype(LOW), wq_ref[...])
        size = width // 2
        for half in range(2):
            rel_own[half] = value[:, half * size : (half + 1) * size]

    def rel_step(hop):
        rel_line.step(jnp.int32(hop), 2)
        half = hop - rel_line.trip
        if half >= 0:
            region = tuple((b >> k) & 1 for k in range(bits - 1, -1, -1))
            rel_all[(half,) + region] = rel_out[half]
            back_copy(half, 0).start()

    def column_head(big, head):
        rows = min(LANES, slots - big * LANES)
        some = slice(big * LANES, big * LANES + rows)
        lanes = slice(big * LANES, (big + 1) * LANES)
        for chunk in range(blocks):
            there = slice(chunk * LANES, min((chunk + 1) * LANES, slots))
            turned_ref[:, there] = mat_ref[head, there, lanes].T
        bucket_sums(big, rows, turned_ref.at[:rows, :], step_ref, col_ref, fold_ref, hist_ref)
        hist = hist_ref[:rows, :]
        gk = dot_nn(turned_ref[:rows, :], q_ref[head]) + dot_nn(hist, qrel_ref[head])
        gk_low_ref[head, :rows, :] = (gk * scale).astype(LOW)
        gqrel_sum[head] += dot_tn(hist, k_ref[head, some, :])

    def inputs_block(big):
        rows = min(LANES, slots - big * LANES)
        some = slice(big * LANES, big * LANES + rows)
        gk = jnp.concatenate([gk_low_ref[head, :rows, :] for head in range(heads)], axis=1)
        gk_ref[some, :] = gk
        gq = jnp.concatenate([gq_ref[head, some, :] for head in range(heads)], axis=1)
        gv = jnp.concatenate([gv_ref[head, some, :] for head in range(heads)], axis=1)
        value = dot_nt(gq, wq_ref[...]) + dot_nt(gk, wk_ref[...]) + dot_nt(gv, wv_ref[...])
        for part in range(rows // HOP):
            own[big * per + part] = value[part * HOP : (part + 1) * HOP]

    gqrel_sum[...] = jnp.zeros_like(gqrel_sum)
    if wide > slots:
        turned_ref[:, slots:] = jnp.zeros((LANES, wide - slots), LOW)
    small_sum[0] = small_ref[...]
    pl.semaphore_wait(barrier, line.greeted() + bits)
    small_copy(0).start()
    rel_start(0)

    @pl.loop(0, heads)
    def _(head):
        column_head(0, head)

    for load in loads:
        load.wait()
    inputs_block(0)

    tasks = {}

    def add(slot, task):
        tasks.setdefault(slot, []).append(task)

    ended = 2 * (blocks - 1)
    add(ended, lambda: rel_start(1))
    for at in range(2):
        add(at, lambda at=at: make(at))
        add(ended + at, lambda at=at: make(2 + at))
        for stage in range(bits):
            after = 4 * stage if stage < 2 else 2 + 2 * stage
            add(2 + at + after, lambda at=at, stage=stage: jobs[at].turn(stage))
            add(ended + 2 + at + after, lambda at=at, stage=stage: jobs[2 + at].turn(stage))
    for stage in range(bits):
        add(2 + 2 * stage, lambda stage=stage: rel_jobs[0].turn(stage))
        add(3 + 2 * stage, lambda stage=stage: small_turn(stage))
        add(ended + 2 + 2 * stage, lambda stage=stage: rel_jobs[1].turn(stage))
    met = ended + 2 * bits
    add(met, rel_meet)
    for hop in range(rel_line.trip + 2):
        add(met + 1 * hop, lambda hop=hop: rel_step(hop))
    for half in range(2):
        for turn in range(bits):
            add(met + 1 * (rel_line.trip + half) + 2 * (1 + turn), lambda half=half, turn=turn: back_turn(half, turn))
    total = chunks + line.trip

    @pl.loop(0, max(total, max(tasks) + 1))
    def _(slot):
        line.step(slot, chunks)
        for big in range(1, blocks):

            @pl.when(slot // 2 + 1 == big)
            def _(big=big):
                late = lax.rem(slot, 2)

                @pl.loop(0, heads // 2)
                def _(head):
                    column_head(big, late * (heads // 2) + head)

                @pl.when(late == 1)
                def _():
                    inputs_block(big)

        for when in sorted(tasks):

            @pl.when(slot == when)
            def _(when=when):
                for task in tasks[when]:
                    task()

        done = slot - line.trip

        @pl.when((done >= 0) & (done < chunks))
        def _():
            at = span(done * HOP, HOP)
            gtok_ref[at, :] = (outer[done] + grad_ref[at, :]).astype(LOW)

    whole = (slice(None),) * (bits + 1)
    for half in range(2):
        size = width // 2
        orel_ref[whole + (slice(half * size, (half + 1) * size),)] = rel_all[half]
    line.drain(chunks)
    rel_line.drain(2)
    for job in jobs + rel_jobs:
        job.drain()
    for k in range(bits):
        small_copy(k).wait_send()
        for half in range(2):
            back_copy(half, k).wait_send()


def gradients(tokens, w_query, w_key, w_value, rel, kept, batch):
    slots, width = tokens.shape
    q = kept[0]
    heads, wide = q.shape[:2]
    mine = heads * HEAD
    bits = batch.bit_length() - 1
    assert 1 << bits == batch
    vmem = pl.BlockSpec(memory_space=pltpu.VMEM)
    far = pl.BlockSpec(memory_space=pl.ANY)
    chunks = slots // HOP
    split = (2,) * bits
    part = width // batch
    rel_part = rel.shape[0] // batch
    assert mine == PIECE
    pieces = [2, 3, 0, 1]
    shape = jax.ShapeDtypeStruct
    got = []
    for _ in pieces:
        got += [pltpu.VMEM((2,) * (bits - 1 - s) + (part, PIECE), FULL) for s in range(bits)]
    for _ in range(2):
        got += [pltpu.VMEM((2,) * (bits - 1 - s) + (rel_part, mine), FULL) for s in range(bits)]
    dma = pltpu.SemaphoreType.DMA
    return pl.pallas_call(
        functools.partial(gradient_kernel, bits=bits, pieces=pieces),
        out_shape=(
            shape((slots, width), LOW),
            shape((part, mine), FULL),
            shape((part, mine), FULL),
            shape((part, mine), FULL),
            shape((part, mine), FULL),
            shape(split + (rel_part, width), FULL),
            shape((8, width), FULL),
        ),
        in_specs=[far] * 5 + [vmem] * 3 + [far] * 3 + [vmem] * 2 + [far] * 2 + [vmem] * 3,
        out_specs=(vmem,) * 7,
        scratch_shapes=[
            pltpu.VMEM((chunks, HOP, width), FULL),
            pltpu.VMEM((chunks, HOP, width), FULL),
            pltpu.VMEM((chunks, HOP, width), FULL),
            pltpu.VMEM((LANES, wide), LOW),
            pltpu.VMEM((2, 3 * LANES, 3 * NB), FULL),
            pltpu.VMEM((LANES, 3 * NB), LOW),
            pltpu.VMEM((slots, mine), LOW),
            pltpu.VMEM((heads, LANES, HEAD), LOW),
            pltpu.VMEM((heads, 3 * NB, HEAD), FULL),
            pltpu.VMEM((len(pieces),) + split + (part, PIECE), FULL),
            pltpu.VMEM((2,) + split + (rel_part, mine), FULL),
            pltpu.VMEM((2, rel_part, mine), FULL),
            pltpu.VMEM((2, rel_part, width // 2), FULL),
            pltpu.VMEM((2, rel_part, width // 2), FULL),
            pltpu.VMEM((2, rel_part, width // 2), FULL),
            pltpu.VMEM((2,) + split + (rel_part, width // 2), FULL),
            pltpu.VMEM((bits, 8, width), FULL),
            pltpu.VMEM((bits, 8, width), FULL),
            pltpu.VMEM((width, mine), LOW),
            pltpu.VMEM((width, mine), LOW),
            pltpu.VMEM((width, mine), LOW),
            pltpu.VMEM((heads, slots, HEAD), LOW),
            pltpu.VMEM((heads, slots, HEAD), LOW),
            pltpu.VMEM((slots, width), LOW),
            pltpu.VMEM(rel.shape, LOW),
            pltpu.VMEM((heads, slots, HEAD), LOW),
            pltpu.VMEM((slots, width), FULL),
            pltpu.VMEM((slots, width), LOW),
            dma((10,)),
        ]
        + got
        + [dma((chunks,))] * 4
        + [dma((2,))] * 4
        + [dma((len(pieces) + 2, bits))] * 2
        + [dma((2, bits))] * 2
        + [dma((bits,))] * 2,
        compiler_params=pltpu.CompilerParams(
            vmem_limit_bytes=VMEM_LIMIT, collective_id=2, has_side_effects=True
        ),
        name="gradients",
    )(tokens, w_query, w_key, w_value, rel, *kept)


def finish_kernel(out, gtok, gwq, gwk, gwv, gwo, gwi, gwu, grel, small, *targets):
    (o_out, o_gtok, o_gwq, o_gwk, o_gwv, o_gwo, o_gwi, o_gwu, o_grel) = targets[:9]
    o_out[...] = out[...]
    o_gtok[...] = gtok[...]
    o_gwq[...] = gwq[...]
    o_gwk[...] = gwk[...]
    o_gwv[...] = gwv[...]
    o_gwo[...] = gwo[...].T
    o_gwi[...] = gwi[...]
    o_gwu[...] = gwu[...].T
    o_grel[...] = grel[...]
    for at, target in enumerate(targets[9:]):
        target[...] = small[at]


def finish(out, gtok, gwq, gwk, gwv, gwo, gwi, gwu, grel, small):
    vmem = pl.BlockSpec(memory_space=pltpu.VMEM)
    shape = jax.ShapeDtypeStruct
    same = lambda a: shape(a.shape, a.dtype)
    turn = lambda a: shape(a.shape[::-1], a.dtype)
    return pl.pallas_call(
        finish_kernel,
        out_shape=(same(out), same(gtok), same(gwq), same(gwk), same(gwv), turn(gwo), same(gwi), turn(gwu), same(grel))
        + (shape(small.shape[1:], FULL),) * 7,
        in_specs=[vmem] * 10,
        out_specs=(vmem,) * 16,
        compiler_params=pltpu.CompilerParams(vmem_limit_bytes=VMEM_LIMIT),
        name="finish",
    )(out, gtok, gwq, gwk, gwv, gwo, gwi, gwu, grel, small)


def shards(
    tokens,
    page_lengths,
    corners,
    w_query,
    w_key,
    w_value,
    w_output,
    b_output,
    gain_attn,
    shift_attn,
    w_inner,
    b_inner,
    w_outer,
    b_outer,
    gain_ffn,
    shift_ffn,
    rel_tables,
    cotangent,
):
    rel = rel_tables.reshape(3 * NB, rel_tables.shape[2])
    vectors = (b_output, gain_attn, shift_attn, b_inner, b_outer, gain_ffn, shift_ffn)
    q, k, qrel, ctx, output, *kept, gwi, gwu = layer(
        tokens, page_lengths, corners, w_query, w_key, w_value, rel,
        w_output, cotangent, w_inner, w_outer, vectors, lax.axis_size("batch"),
    )
    done = gradients(
        tokens, w_query, w_key, w_value, rel, (q, k, qrel, ctx, *kept), lax.axis_size("batch")
    )
    gtok, gwq, gwk, gwv, gwo, grel, small = done
    grel = grel.reshape(rel_tables.shape)
    (output, gtok, gwq, gwk, gwv, gwo, gwi, gwu, grel, gbo, gga, gsa, gbi, gbu, ggf, gsf) = finish(
        output, gtok, gwq, gwk, gwv, gwo, gwi, gwu, grel, small
    )
    return (output, gtok, gwq, gwk, gwv, gwo, gbo, gga, gsa, gwi, gbi, gwu, gbu, ggf, gsf, grel)


def solution(mesh):
    in_specs = (
        P("batch", None),
        P("batch"),
        P(None, "batch"),
        P(None, "head"),
        P(None, "head"),
        P(None, "head"),
        P("head", None),
        P(),
        P(),
        P(),
        P(None, "head"),
        P("head"),
        P("head", None),
        P(),
        P(),
        P(),
        P(),
        P("batch", None),
    )
    out_specs = (
        P("batch", None),
        P("batch", None),
        P("batch", "head"),
        P("batch", "head"),
        P("batch", "head"),
        P("head", "batch"),
        P(),
        P(),
        P(),
        P("batch", "head"),
        P("head"),
        P("head", "batch"),
        P(),
        P(),
        P(),
        P(),
    )
    return jax.shard_map(shards, mesh=mesh, in_specs=in_specs, out_specs=out_specs, check_vma=False)
```
